32 devices in a mesh: dp: 2 (over x), depth: 4 (over y, core), wide: 4 (over z).
Axes of the slice: x: 2, y: 2, z: 4, core: 2. Of those that a mesh axis runs over, the one named last changes fastest.
Arguments:
- voxels: bfloat16 [16, 16, 64, 32, 192], P('dp', 'depth', None, 'wide'), may hold values from -6 to 6
- cotangent: bfloat16 [16, 16, 64, 32, 192], P('dp', 'depth', None, 'wide'), may hold values from -45 to 45
- project_in: float32 [192, 576], replicated, may hold values from -0.4375 to 0.4375
- project_out: float32 [192, 192], replicated, may hold values from -1.25 to 1.25
- expand: float32 [192, 768], replicated, may hold values from -0.4375 to 0.4375
- contract: float32 [768, 192], replicated, may hold values from -0.21875 to 0.21875
- bias_table: float32 [6, 343], replicated, may hold values from -4 to 4
- vectors: float32 [2304], replicated, may hold values from -0.8 to 1.3
- project_in_first: float32 [192, 576], replicated, may hold values from -1 to 1
- project_out_first: float32 [192, 192], replicated, may hold values from -1 to 1
- expand_first: float32 [192, 768], replicated, may hold values from -1 to 1
- contract_first: float32 [768, 192], replicated, may hold values from -1 to 1
- bias_table_first: float32 [6, 343], replicated, may hold values from -1 to 1
- vectors_first: float32 [2304], replicated, may hold values from -4 to 4
- project_in_second: float32 [192, 576], replicated, may hold values from 0.0022384885 to 0.008953954
- project_out_second: float32 [192, 192], replicated, may hold values from 0.0022384885 to 0.008953954
- expand_second: float32 [192, 768], replicated, may hold values from 0.0022384885 to 0.008953954
- contract_second: float32 [768, 192], replicated, may hold values from 0.0022384885 to 0.008953954
- bias_table_second: float32 [6, 343], replicated, may hold values from 0.0022384885 to 0.008953954
- vectors_second: float32 [2304], replicated, may hold values from 0.035815816 to 0.14326327
Outputs:
- layer_out: bfloat16 [16, 16, 64, 32, 192], P('dp', 'depth', None, 'wide')
- voxel_grad: bfloat16 [16, 16, 64, 32, 192], P('dp', 'depth', None, 'wide')
- project_in_grad: float32 [192, 576], replicated
- project_in_first_new: float32 [192, 576], replicated
- project_in_second_new: float32 [192, 576], replicated
- project_in_next: float32 [192, 576], replicated
- project_out_grad: float32 [192, 192], replicated
- project_out_first_new: float32 [192, 192], replicated
- project_out_second_new: float32 [192, 192], replicated
- project_out_next: float32 [192, 192], replicated
- expand_grad: float32 [192, 768], replicated
- expand_first_new: float32 [192, 768], replicated
- expand_second_new: float32 [192, 768], replicated
- expand_next: float32 [192, 768], replicated
- contract_grad: float32 [768, 192], replicated
- contract_first_new: float32 [768, 192], replicated
- contract_second_new: float32 [768, 192], replicated
- contract_next: float32 [768, 192], replicated
- bias_table_grad: float32 [6, 343], replicated
- bias_table_first_new: float32 [6, 343], replicated
- bias_table_second_new: float32 [6, 343], replicated
- bias_table_next: float32 [6, 343], replicated
- vectors_grad: float32 [2304], replicated
- vectors_first_new: float32 [2304], replicated
- vectors_second_new: float32 [2304], replicated
- vectors_next: float32 [2304], replicated
- project_in_copy: bfloat16 [192, 576], replicated
- project_out_copy: bfloat16 [192, 192], replicated
- expand_copy: bfloat16 [192, 768], replicated
- contract_copy: bfloat16 [768, 192], replicated
- grad_norm: float32 [], replicated
The draws below stay inside these ranges and needn't reach their ends.
All inputs are finite; a program needn't handle non-finite values.
Results may differ from the reference program's by a relative error of at most 0.012.
The reference program's roundings to bfloat16 on the way count: a program that leaves them out, or rounds other values in their place, can miss the bound.
Values may be sent and summed in bfloat16 or wider, within the bound.
A program may use at most 512 MiB of HBM per device.

```python
import math
import jax
import jax.numpy as jnp
import numpy as np
from jax import lax

C = 192
HEADS = 6
HD = 32
MLP = 768
WIN = 4
SHIFT = 2
STEP = 10
H = 64
CROPS = 16
DZ = 16
W = 32
REL = 343
VEC = 2304
NPARAM = 446730


def draw_cotangent(key, part):
    key = jax.random.fold_in(key, 7)
    growth = 3.0
    base = jnp.clip(jax.random.normal(key, (CROPS, DZ, H, W, C), jnp.float32), -4.0, 4.0)
    crop_place = jnp.arange(CROPS, dtype=jnp.float32) / (CROPS - 1)
    plane_place = jnp.arange(DZ, dtype=jnp.float32) / (DZ - 1)
    column_place = jnp.arange(W, dtype=jnp.float32) / (W - 1)
    exponent = crop_place[:, None, None, None, None] + plane_place[None, :, None, None, None] + column_place[None, None, None, :, None] - 1.5
    return (base * jnp.exp(jnp.log(growth) * exponent)).astype(jnp.bfloat16)


def draw_vectors(key, part):
    key = jax.random.fold_in(key, 11)
    gain_key, bias_key = jax.random.split(key)
    places = jnp.arange(8 * C + MLP)
    is_gain = (places < C) | (places >= 5 * C) & (places < 6 * C)
    gains = jax.random.uniform(gain_key, (8 * C + MLP,), jnp.float32, 0.7, 1.3)
    biases = jnp.clip(0.2 * jax.random.normal(bias_key, (8 * C + MLP,), jnp.float32), -0.8, 0.8)
    return jnp.where(is_gain, gains, biases)


def block_scale(stream_key, shape, cuts, least, largest):
    loudness = 1.0
    for dim, parts in cuts:
        draws = jax.random.uniform(jax.random.fold_in(jax.random.fold_in(stream_key, 6), dim), (parts,), jnp.float32, least / len(cuts), largest / len(cuts))
        loudness = loudness * jnp.repeat(jnp.exp(draws), shape[dim] // parts).reshape((-1,) + (1,) * (len(shape) - 1 - dim))
    return loudness


def scatter_about(rng, shape, scale, most, pieces=(), kind=jnp.bfloat16):
    values = jax.random.normal(rng, shape, jnp.float32) * scale
    if len(pieces) > 0:
        values = block_scale(rng, shape, pieces, -0.22, 0.18) * values
    return jnp.clip(values, min=-most, max=most).astype(kind)


def setup_inputs(seed: int = 0) -> dict:
    streams_of = jax.random.split(jax.random.key(seed), 21)
    voxels = scatter_about(streams_of[0], (CROPS, DZ, H, W, C), 1.0, 6.0, ((0, 2), (1, 4), (3, 4)))
    cotangent = draw_cotangent(jax.random.fold_in(streams_of[20], 71), 0)
    project_in = scatter_about(streams_of[2], (C, 3 * C), C ** -0.5, 0.4375, (), jnp.float32)
    project_out = scatter_about(streams_of[3], (C, C), (C // 8) ** -0.5, 1.25, (), jnp.float32)
    expand = scatter_about(streams_of[4], (C, MLP), C ** -0.5, 0.4375, (), jnp.float32)
    contract = scatter_about(streams_of[5], (MLP, C), MLP ** -0.5, 0.21875, (), jnp.float32)
    bias_table = scatter_about(streams_of[6], (HEADS, REL), 0.7, 4.0, (), jnp.float32)
    vectors = draw_vectors(jax.random.fold_in(streams_of[20], 71), 0)
    project_in_first = scatter_about(streams_of[8], (C, 3 * C), (110 / NPARAM ** 0.5), 1.0, (), jnp.float32)
    project_out_first = scatter_about(streams_of[9], (C, C), (110 / NPARAM ** 0.5), 1.0, (), jnp.float32)
    expand_first = scatter_about(streams_of[10], (C, MLP), (110 / NPARAM ** 0.5), 1.0, (), jnp.float32)
    contract_first = scatter_about(streams_of[11], (MLP, C), (110 / NPARAM ** 0.5), 1.0, (), jnp.float32)
    bias_table_first = scatter_about(streams_of[12], (HEADS, REL), (110 / NPARAM ** 0.5), 1.0, (), jnp.float32)
    vectors_first = scatter_about(streams_of[13], (VEC,), (440 / NPARAM ** 0.5), 4.0, (), jnp.float32)
    project_in_second = jnp.clip(jnp.exp(jax.random.uniform(streams_of[14], (C, 3 * C), jnp.float32, math.log(0.0022384885), math.log(0.008953954))), 0.0022384885, 0.008953954)
    project_out_second = jnp.clip(jnp.exp(jax.random.uniform(streams_of[15], (C, C), jnp.float32, math.log(0.0022384885), math.log(0.008953954))), 0.0022384885, 0.008953954)
    expand_second = jnp.clip(jnp.exp(jax.random.uniform(streams_of[16], (C, MLP), jnp.float32, math.log(0.0022384885), math.log(0.008953954))), 0.0022384885, 0.008953954)
    contract_second = jnp.clip(jnp.exp(jax.random.uniform(streams_of[17], (MLP, C), jnp.float32, math.log(0.0022384885), math.log(0.008953954))), 0.0022384885, 0.008953954)
    bias_table_second = jnp.clip(jnp.exp(jax.random.uniform(streams_of[18], (HEADS, REL), jnp.float32, math.log(0.0022384885), math.log(0.008953954))), 0.0022384885, 0.008953954)
    vectors_second = jnp.clip(jnp.exp(jax.random.uniform(streams_of[19], (VEC,), jnp.float32, math.log(0.035815816), math.log(0.14326327))), 0.035815816, 0.14326327)
    return {"voxels": voxels, "cotangent": cotangent, "project_in": project_in, "project_out": project_out, "expand": expand, "contract": contract, "bias_table": bias_table, "vectors": vectors, "project_in_first": project_in_first, "project_out_first": project_out_first, "expand_first": expand_first, "contract_first": contract_first, "bias_table_first": bias_table_first, "vectors_first": vectors_first, "project_in_second": project_in_second, "project_out_second": project_out_second, "expand_second": expand_second, "contract_second": contract_second, "bias_table_second": bias_table_second, "vectors_second": vectors_second}


@jax.custom_vjp
def low(v):
    return lax.optimization_barrier(v.astype(jnp.bfloat16)).astype(jnp.float32)

@jax.custom_vjp
def low_back(v):
    return v

def low_keep(v):
    return (low(v), None)

def low_pass(kept, grad):
    return (grad,)

def back_keep(v):
    return (v, None)

def back_low(kept, grad):
    return (low(grad),)
low.defvjp(low_keep, low_pass)
low_back.defvjp(back_keep, back_low)
norm_eps = 1e-05
mask_fill = -100.0
clip_bound = 1000.0
rate_matrix = 0.1
rate_vector = 0.6
weight_decay = 0.01
beta_first = 0.9
beta_second = 0.999
adam_eps = 1e-08

def relative_index():
    extent = 2 * WIN - 1
    corner = np.arange(WIN)
    places = np.stack(np.meshgrid(corner, corner, corner, indexing='ij'), -1).reshape(-1, 3)
    offsets = places[:, None, :] - places[None, :, :] + WIN - 1
    return (offsets[..., 0] * extent + offsets[..., 1]) * extent + offsets[..., 2]

def region_labels(count, start, length):
    places = start + jnp.arange(count, dtype=jnp.int32)
    return (places >= length - WIN).astype(jnp.int32) + (places >= length - SHIFT).astype(jnp.int32)

def window_split(tensor):
    batches, planes, height, breadth, feature = tensor.shape
    tensor = tensor.reshape(batches, planes // WIN, WIN, height // WIN, WIN, breadth // WIN, WIN, feature)
    tensor = tensor.transpose(0, 1, 3, 5, 2, 4, 6, 7)
    return tensor.reshape(-1, WIN ** 3, feature)

def window_join(tensor, batches, planes, height, breadth):
    feature = tensor.shape[-1]
    tensor = tensor.reshape(batches, planes // WIN, height // WIN, breadth // WIN, WIN, WIN, WIN, feature)
    tensor = tensor.transpose(0, 1, 4, 2, 5, 3, 6, 7)
    return tensor.reshape(batches, planes, height, breadth, feature)

def layer_norm(tensor, gain, offset):
    centred = tensor - lax.optimization_barrier(jnp.mean(tensor, -1, keepdims=True))
    inverse = lax.rsqrt(lax.optimization_barrier(jnp.mean(centred * centred, -1, keepdims=True)) + norm_eps)
    return centred * inverse * gain + offset

def adam_update(weight, first, second, gradient, rate, decay):
    first_new = beta_first * first + (1.0 - beta_first) * gradient
    second_new = beta_second * second + (1.0 - beta_second) * gradient * gradient
    first_hat = first_new / (1.0 - beta_first ** STEP)
    second_hat = second_new / (1.0 - beta_second ** STEP)
    weight_new = weight - rate * (first_hat / (jnp.sqrt(second_hat) + adam_eps) + decay * weight)
    return (first_new, second_new, weight_new)

def crop_forward(crop, rounded, pair_bias, vector_set, masks):
    exact = lax.Precision.HIGHEST
    members = [vector_set[member * C:(member + 1) * C] for member in range(8)]
    gain_one, shift_one, query_bias, value_bias, out_bias, gain_two, shift_two, contract_bias = members
    expand_bias = vector_set[8 * C:]
    shifted = jnp.roll(crop, (-SHIFT, -SHIFT, -SHIFT), (0, 1, 2))
    tokens = window_split(shifted[None])
    windows = tokens.shape[0]
    normed_one = low(layer_norm(tokens, gain_one, shift_one))
    in_bias = jnp.concatenate([query_bias, jnp.zeros((C,), jnp.float32), value_bias])
    triple = low(low_back(jnp.einsum('wtc,cf->wtf', normed_one, rounded[0], precision=exact) + in_bias))
    query = triple[..., :C].reshape(windows, WIN ** 3, HEADS, HD)
    keys = triple[..., C:2 * C].reshape(windows, WIN ** 3, HEADS, HD)
    values = triple[..., 2 * C:].reshape(windows, WIN ** 3, HEADS, HD)
    scores = jnp.einsum('wihd,wjhd->whij', query, keys, precision=exact) * HD ** (-0.5)
    scores = low_back(scores + pair_bias[None] + masks[:, None])
    probs = jax.nn.softmax(scores, axis=-1)
    mixed = jnp.einsum('whij,wjhd->wihd', low(probs), values, precision=exact).reshape(windows, WIN ** 3, C)
    mixed = low(low_back(mixed))
    middle = tokens + low_back(jnp.einsum('wtc,cf->wtf', mixed, rounded[1], precision=exact) + out_bias)
    normed_two = low(layer_norm(middle, gain_two, shift_two))
    hidden = low_back(jnp.einsum('wtc,cf->wtf', normed_two, rounded[2], precision=exact) + expand_bias)
    active = low(jax.nn.gelu(hidden, approximate=False))
    result = middle + low_back(jnp.einsum('wtf,fc->wtc', active, rounded[3], precision=exact) + contract_bias)
    grid = window_join(result, 1, DZ, H, W)[0]
    return jnp.roll(grid, (SHIFT, SHIFT, SHIFT), (0, 1, 2))

def reference(voxels, cotangent, project_in, project_out, expand, contract, bias_table, vectors, project_in_first, project_out_first, expand_first, contract_first, bias_table_first, vectors_first, project_in_second, project_out_second, expand_second, contract_second, bias_table_second, vectors_second):
    labels = region_labels(DZ, 0, DZ)[:, None, None] * 9 + region_labels(H, 0, H)[None, :, None] * 3 + region_labels(W, 0, W)[None, None, :]
    labels = window_split(jnp.broadcast_to(labels[None, :, :, :, None], (1, DZ, H, W, 1)))[..., 0]
    masks = jnp.where(labels[:, :, None] == labels[:, None, :], 0.0, mask_fill).astype(jnp.float32)
    order = jnp.asarray(relative_index(), jnp.int32)

    def forward(inputs, weight_in, weight_out, weight_up, weight_down, table, vector_set):
        rounded = (low(weight_in), low(weight_out), low(weight_up), low(weight_down))
        pair_bias = table[:, order]

        def one_crop(crop):
            return crop_forward(crop, rounded, pair_bias, vector_set, masks)
        return lax.map(jax.checkpoint(one_crop), inputs)
    params = (project_in, project_out, expand, contract, bias_table, vectors)
    firsts = (project_in_first, project_out_first, expand_first, contract_first, bias_table_first, vectors_first)
    seconds = (project_in_second, project_out_second, expand_second, contract_second, bias_table_second, vectors_second)
    outcome, pull = jax.vjp(forward, voxels.astype(jnp.float32), *params)
    grads = pull(cotangent.astype(jnp.float32))
    raws = grads[1:]
    squares = jnp.float32(0.0)
    for member in raws:
        squares = squares + jnp.sum(member * member)
    norm_value = jnp.sqrt(squares)
    factor = jnp.minimum(1.0, clip_bound / (norm_value + 1e-06))
    rates = [rate_matrix] * 4 + [rate_vector] * 2
    decays = [weight_decay] * 4 + [0.0, 0.0]
    updated = []
    copies = []
    for member in range(6):
        clipped = raws[member] * factor
        first_new, second_new, weight_new = adam_update(params[member], firsts[member], seconds[member], clipped, rates[member], decays[member])
        updated = updated + [clipped, first_new, second_new, weight_new]
        if member < 4:
            copies = copies + [weight_new.astype(jnp.bfloat16)]
    return tuple([outcome.astype(jnp.bfloat16), grads[0].astype(jnp.bfloat16)] + updated + copies + [norm_value])
```

```python
from functools import partial

import jax
import jax.numpy as jnp
import numpy as np
from jax import lax
from jax.experimental import pallas as pl
from jax.experimental.pallas import tpu as pltpu
from jax.sharding import PartitionSpec as P

HEADS = 6
WIN = 4
SHIFT = 2
STEP = 10
TOK = WIN**3
GROUP = 4
LANES = GROUP * TOK

norm_eps = 1e-05
mask_fill = -100.0
clip_bound = 1000.0
rate_matrix = 0.1
rate_vector = 0.6
weight_decay = 0.01
beta_first = 0.9
beta_second = 0.999
adam_eps = 1e-08
LOG2E = 1.4426950408889634
INV_SQRT2 = 0.7071067811865476
INV_SQRT2PI = 0.3989422804014327


def relative_index():
    extent = 2 * WIN - 1
    corner = np.arange(WIN)
    places = np.stack(np.meshgrid(corner, corner, corner, indexing="ij"), -1).reshape(-1, 3)
    offsets = places[:, None, :] - places[None, :, :] + WIN - 1
    return (offsets[..., 0] * extent + offsets[..., 1]) * extent + offsets[..., 2]


def region_labels(count, start, length):
    places = start + jnp.arange(count, dtype=jnp.int32)
    return (places >= length - WIN).astype(jnp.int32) + (places >= length - SHIFT).astype(jnp.int32)


def window_split(tensor):
    batches, planes, height, breadth, feature = tensor.shape
    tensor = tensor.reshape(
        batches, planes // WIN, WIN, height // WIN, WIN, breadth // WIN, WIN, feature
    )
    tensor = tensor.transpose(0, 1, 3, 5, 2, 4, 6, 7)
    return tensor.reshape(-1, WIN**3, feature)


def adam_update(weight, first, second, gradient, rate, decay):
    first_new = beta_first * first + (1.0 - beta_first) * gradient
    second_new = beta_second * second + (1.0 - beta_second) * gradient * gradient
    first_hat = first_new / (1.0 - beta_first**STEP)
    second_hat = second_new / (1.0 - beta_second**STEP)
    weight_new = weight - rate * (first_hat / (jnp.sqrt(second_hat) + adam_eps) + decay * weight)
    return (first_new, second_new, weight_new)


def whole_update(totals, weights, firsts, seconds, rates, decays):
    squares = jnp.float32(0.0)
    for member in totals:
        squares = squares + jnp.sum(member * member)
    norm_value = jnp.sqrt(squares)
    factor = jnp.minimum(1.0, clip_bound / (norm_value + 1e-06))
    outputs = []
    for member in range(6):
        clipped = totals[member] * factor
        outputs.append(
            (clipped,)
            + adam_update(
                weights[member],
                firsts[member],
                seconds[member],
                clipped,
                rates[member],
                decays[member],
            )
        )
    return (outputs, norm_value)


fl = jnp.float32
bf = jnp.bfloat16


def dot(a, b):
    return jnp.dot(a, b, preferred_element_type=fl)


def dot_nt(a, b):
    return lax.dot_general(a, b, (((1,), (1,)), ((), ())), preferred_element_type=fl)


def wide(v, lanes):
    return jnp.concatenate([v] * (lanes // v.shape[1]), axis=1)


def unit_norm(v):
    width = v.shape[0]
    mean = jnp.sum(v, 0, keepdims=True) * (1.0 / width)
    centred = v - mean
    inverse = lax.rsqrt(jnp.sum(centred * centred, 0, keepdims=True) * (1.0 / width) + norm_eps)
    return centred * inverse, inverse


def unit_back(grad, unit, inverse, gain):
    width = grad.shape[0]
    scaled = grad * gain
    inner = jnp.sum(scaled, 0, keepdims=True) * (1.0 / width)
    along = jnp.sum(scaled * unit, 0, keepdims=True) * (1.0 / width)
    return inverse * (scaled - inner - unit * along)


def fold(v):
    total = v[:, :128]
    for lane in range(128, v.shape[1], 128):
        total = total + v[:, lane : lane + 128]
    return total


def pair_blocks(low, c0, rows, lane0):
    count = rows // 32
    zero = jnp.zeros((32, 128), bf)
    out = []
    for a in range(count):
        out.append(
            jnp.concatenate(
                [
                    low[c0 + 32 * a : c0 + 32 * a + 32, lane0 : lane0 + 128] if a == b else zero
                    for b in range(count)
                ],
                axis=1,
            )
        )
    return jnp.concatenate(out, axis=0)


def cross(token_major, low, lane0, first_half):
    pieces = []
    for c0, rows in ((0, 128), (128, 64)):
        full = dot(
            token_major[lane0 : lane0 + 128, c0 : c0 + rows], pair_blocks(low, c0, rows, lane0)
        )
        for b in range(rows // 32):
            block = full[:, 128 * b : 128 * b + 128]
            pieces.append(jnp.where(first_half, block[:TOK], block[TOK:]))
    return pieces


def two_windows(compact, first_half):
    zero = jnp.zeros_like(compact)
    return jnp.concatenate(
        [jnp.where(first_half, compact, zero), jnp.where(first_half, zero, compact)], axis=0
    )


def placement():
    take = np.zeros((LANES, LANES + TOK), np.float32)
    give = np.zeros((LANES + TOK, LANES), np.float32)
    pick = np.zeros((TOK, LANES), np.float32)
    fill = np.zeros((LANES, TOK), np.float32)
    for hw in range(2):
        for ww in range(2):
            for d in range(WIN):
                for hh in range(WIN):
                    for wl in range(WIN):
                        t = ((hw * 2 + ww) * WIN + d) * 16 + hh * 4 + wl
                        h, w = 4 * hw + hh, 4 * ww + wl
                        if w < 2 * WIN - SHIFT:
                            row = d * 64 + h * 8 + w + SHIFT
                        else:
                            row = LANES + d * 16 + h * 2 + w - (2 * WIN - SHIFT)
                        take[t, row] = 1.0
                        give[row, t] = 1.0
    for d in range(WIN):
        for h in range(2 * WIN):
            for w in range(SHIFT):
                pick[d * 16 + h * 2 + w, d * 64 + h * 8 + w] = 1.0
                fill[d * 64 + h * 8 + w, d * 16 + h * 2 + w] = 1.0
    return [jnp.asarray(m, bf) for m in (take, give, pick, fill)]


def block_kernel(
    vox,
    cot,
    table_ref,
    vec_ref,
    w_in_t,
    w_in,
    w_out_t,
    w_out,
    w_exp_t,
    w_exp,
    w_con,
    w_con_t,
    take,
    give,
    pick,
    fill,
    out_res,
    out_tok,
    d_in,
    d_out,
    d_exp,
    d_con,
    d_vec,
    d_tab,
    own,
    halo_d,
    halo_w,
    send_w,
    back_send,
    back_recv,
    grid_out,
    own_sem,
    d_send,
    d_recv,
    w_send,
    w_recv,
    b_send,
    b_recv,
    o_sem,
    r_send,
    r_recv,
):
    crops = vox.shape[0]
    rows = vox.shape[2]
    width = vox.shape[3]
    units = rows // TOK
    n = LANES
    depth, peers_d = lax.axis_index("depth"), lax.axis_size("depth")
    column, peers_w = lax.axis_index("wide"), lax.axis_size("wide")
    d_prev = {"depth": lax.rem(depth + peers_d - 1, peers_d)}
    d_next = {"depth": lax.rem(depth + 1, peers_d)}
    w_prev = {"wide": lax.rem(column + peers_w - 1, peers_w)}
    w_next = {"wide": lax.rem(column + 1, peers_w)}
    mesh_id = pl.DeviceIdType.MESH
    sources = (vox, cot)
    results = (out_res, out_tok)

    def own_copy(c, a):
        slot = lax.rem(c, 2)
        return pltpu.make_async_copy(
            sources[a].at[c, pl.ds(SHIFT, 2)], own.at[slot, a], own_sem.at[slot, a]
        )

    def depth_copy(c, a):
        return pltpu.make_async_remote_copy(
            src_ref=sources[a].at[c, pl.ds(0, SHIFT)],
            dst_ref=halo_d.at[c, a],
            send_sem=d_send.at[c, a],
            recv_sem=d_recv.at[c, a],
            device_id=d_prev,
            device_id_type=mesh_id,
        )

    def wide_copy(c):
        return pltpu.make_async_remote_copy(
            src_ref=send_w.at[c],
            dst_ref=halo_w.at[c],
            send_sem=w_send.at[c],
            recv_sem=w_recv.at[c],
            device_id=w_prev,
            device_id_type=mesh_id,
        )

    def back_copy(c):
        return pltpu.make_async_remote_copy(
            src_ref=back_send.at[c],
            dst_ref=back_recv.at[c],
            send_sem=b_send.at[c],
            recv_sem=b_recv.at[c],
            device_id=w_next,
            device_id_type=mesh_id,
        )

    def keep_copy(c, a):
        slot = lax.rem(c, 2)
        return pltpu.make_async_copy(
            grid_out.at[slot, a, pl.ds(0, 2)], results[a].at[c, pl.ds(SHIFT, 2)], o_sem.at[slot, a]
        )

    def return_copy(c, a):
        slot = lax.rem(c, 2)
        return pltpu.make_async_remote_copy(
            src_ref=grid_out.at[slot, a, pl.ds(2, 2)],
            dst_ref=results[a].at[c, pl.ds(0, SHIFT)],
            send_sem=r_send.at[slot, a],
            recv_sem=r_recv.at[c, a],
            device_id=d_next,
            device_id_type=mesh_id,
        )

    barrier = pltpu.get_barrier_semaphore()
    for peer in (d_prev, d_next, w_prev, w_next):
        pl.semaphore_signal(barrier, inc=1, device_id=peer, device_id_type=mesh_id)
    pl.semaphore_wait(barrier, 4)

    for a in range(2):
        own_copy(0, a).start()

    def send_depth(c, carry):
        for a in range(2):
            depth_copy(c, a).start()
        return carry

    lax.fori_loop(0, crops, send_depth, 0)
    for ref in (d_in, d_out, d_exp, d_con, d_vec, d_tab):
        ref[...] = jnp.zeros_like(ref)

    def starts(u):
        first = pl.multiple_of(u * TOK + 16, 16)
        second = pl.multiple_of(lax.rem(u * TOK + TOK, rows), 16)
        return first, second

    def natural(c, a, u):
        first, second = starts(u)
        slot = lax.rem(c, 2)
        parts = []
        for d in range(2):
            parts.append(own[slot, a, d, pl.ds(first, 48), :])
            parts.append(own[slot, a, d, pl.ds(second, 16), :])
        for d in range(2):
            parts.append(halo_d[c, a, d, pl.ds(first, 48), :])
            parts.append(halo_d[c, a, d, pl.ds(second, 16), :])
        return jnp.concatenate(parts, axis=0)

    def pack(c):
        for a in range(2):
            own_copy(c, a).wait()
            depth_copy(c, a).wait_recv()

        def one(u, carry):
            for a in range(2):
                send_w[c, a, pl.ds(pl.multiple_of(u * TOK, TOK), TOK), :] = dot(
                    pick[...], natural(c, a, u)
                ).astype(bf)
            return carry

        lax.fori_loop(0, units, one, 0)
        wide_copy(c).start()

    def merge(c):
        slot = lax.rem(c, 2)
        back_copy(c).wait_recv()

        def one(u, carry):
            first, second = starts(u)
            for a in range(2):
                extra = dot(fill[...], back_recv[c, a, pl.ds(pl.multiple_of(u * TOK, TOK), TOK), :])
                for d in range(WIN):
                    for start, size, at in ((first, 48, 64 * d), (second, 16, 64 * d + 48)):
                        place = pl.ds(start, size)
                        grid_out[slot, a, d, place, :] = (
                            grid_out[slot, a, d, place, :].astype(fl) + extra[at : at + size]
                        ).astype(bf)
            return carry

        lax.fori_loop(0, units, one, 0)
        for a in range(2):
            keep_copy(c, a).start()
            return_copy(c, a).start()

    eye_c = (
        lax.broadcasted_iota(jnp.int32, (width, width), 0)
        == lax.broadcasted_iota(jnp.int32, (width, width), 1)
    ).astype(bf)
    eye_t = (
        lax.broadcasted_iota(jnp.int32, (n, n), 0) == lax.broadcasted_iota(jnp.int32, (n, n), 1)
    ).astype(bf)
    first_half = lax.broadcasted_iota(jnp.int32, (TOK, 128), 1) < TOK
    ones = jnp.ones((16, n), bf)
    scale = 32 ** (-0.5)

    def vec(index, size=width):
        return wide(vec_ref[index : index + size, :], n)

    def unit(c, u):
        here = pl.ds(pl.multiple_of(u * TOK, TOK), TOK)

        def tokens(a):
            low = dot(
                take[...], jnp.concatenate([natural(c, a, u), halo_w[c, a, here, :]], axis=0)
            ).astype(bf)
            return dot_nt(eye_c, low)

        def put(a, low):
            first, second = starts(u)
            slot = lax.rem(c, 2)
            placed = dot_nt(give[...], low).astype(bf)
            for d in range(WIN):
                grid_out[slot, a, d, pl.ds(first, 48), :] = placed[64 * d : 64 * d + 48]
                grid_out[slot, a, d, pl.ds(second, 16), :] = placed[64 * d + 48 : 64 * d + 64]
            back_send[c, a, here, :] = placed[n:]

        x = tokens(0)
        up = tokens(1)
        up_low = up.astype(bf)
        unit_one, inverse_one = unit_norm(x)
        entry_one = (unit_one * vec(0) + vec(width)).astype(bf)
        triple = dot(w_in_t[...], entry_one)
        query = (triple[:width] + vec(2 * width)).astype(bf)
        keys = triple[width : 2 * width].astype(bf)
        values = (triple[2 * width :] + vec(3 * width)).astype(bf)
        turned = dot_nt(eye_t, jnp.concatenate([keys, values], axis=0)).astype(bf)
        keys_t = turned[:, :width]
        values_t = turned[:, width:]
        probs = []
        probs_wide = []
        mixed = []
        edge = (u == units - 1).astype(jnp.int32)
        for half in range(2):
            lane0 = 128 * half
            pieces = cross(keys_t, query, lane0, first_half)
            which = edge if half == 1 else 0
            cols = []
            for head in range(HEADS):
                s = (
                    pieces[head] * (scale * LOG2E)
                    + table_ref[which, :, 128 * head : 128 * head + 128]
                )
                e = jnp.exp2(s - jnp.max(s, 0, keepdims=True))
                p = e * (1.0 / jnp.sum(e, 0, keepdims=True))
                p_wide = two_windows(p.astype(bf), first_half)
                probs.append(p)
                probs_wide.append(p_wide)
                cols.append(dot(values[32 * head : 32 * head + 32, lane0 : lane0 + 128], p_wide))
            mixed.append(jnp.concatenate(cols, axis=0))
        mixed = jnp.concatenate(mixed, axis=1).astype(bf)
        middle = x + dot(w_out_t[...], mixed) + vec(4 * width)
        unit_two, inverse_two = unit_norm(middle)
        entry_two = (unit_two * vec(5 * width) + vec(6 * width)).astype(bf)
        hidden = dot(w_exp_t[...], entry_two) + vec(8 * width, 4 * width)
        phi = 0.5 + 0.5 * lax.erf(hidden * INV_SQRT2)
        slope = phi + hidden * (INV_SQRT2PI * jnp.exp2(hidden * hidden * (-0.5 * LOG2E)))
        active = (hidden * phi).astype(bf)
        result = middle + dot(w_con_t[...], active) + vec(7 * width)
        put(0, result.astype(bf))
        hidden_low = (dot(w_con[...], up_low) * slope).astype(bf)
        grad_two = dot(w_exp[...], hidden_low)
        middle_grad = up + unit_back(grad_two, unit_two, inverse_two, vec(5 * width))
        branch_low = middle_grad.astype(bf)
        mixed_low = dot(w_out[...], branch_low).astype(bf)
        d_cols = [[], [], []]
        for half in range(2):
            lane0 = 128 * half
            pieces = cross(values_t, mixed_low, lane0, first_half)
            dq, dk, dv = [], [], []
            for head in range(HEADS):
                p = probs[half * HEADS + head]
                pg = pieces[head]
                sg = (p * (pg - jnp.sum(pg * p, 0, keepdims=True))).astype(bf)
                d_tab[:, 128 * head : 128 * head + 128] += sg.astype(fl)
                s_wide = two_windows(sg, first_half)
                at = slice(32 * head, 32 * head + 32)
                dq.append(dot(keys[at, lane0 : lane0 + 128], s_wide))
                dk.append(dot_nt(query[at, lane0 : lane0 + 128], s_wide))
                dv.append(
                    dot_nt(mixed_low[at, lane0 : lane0 + 128], probs_wide[half * HEADS + head])
                )
            for member, part in enumerate((dq, dk, dv)):
                d_cols[member].append(jnp.concatenate(part, axis=0))
        dq, dk, dv = [jnp.concatenate(part, axis=1) for part in d_cols]
        triple_low = jnp.concatenate([dq * scale, dk * scale, dv], axis=0).astype(bf)
        grad_one = dot(w_in[...], triple_low)
        token_grad = middle_grad + unit_back(grad_one, unit_one, inverse_one, vec(0))
        put(1, token_grad.astype(bf))
        d_in[...] += dot_nt(triple_low, jnp.concatenate([entry_one, ones], axis=0))
        d_out[...] += dot_nt(branch_low, jnp.concatenate([mixed, ones], axis=0))
        d_exp[...] += dot_nt(hidden_low, jnp.concatenate([entry_two, ones], axis=0))
        d_con[...] += dot_nt(active, up_low)
        d_vec[0:width, :] += fold(grad_one * unit_one)
        d_vec[width : 2 * width, :] += fold(grad_one)
        d_vec[2 * width : 3 * width, :] += fold(grad_two * unit_two)
        d_vec[3 * width : 4 * width, :] += fold(grad_two)
        d_vec[4 * width : 5 * width, :] += fold(up)

    pack(0)

    def crop(c, carry):
        wide_copy(c).wait_recv()

        @pl.when(c + 1 < crops)
        def _():
            for a in range(2):
                own_copy(c + 1, a).start()

        @pl.when(c >= 2)
        def _():
            for a in range(2):
                keep_copy(c - 2, a).wait()
                return_copy(c - 2, a).wait_send()

        def one(u, inner):
            unit(c, u)

            @pl.when((u == 1) & (c + 1 < crops))
            def _():
                pack(c + 1)

            @pl.when((u == units - 2) & (c > 0))
            def _():
                merge(c - 1)

            return inner

        lax.fori_loop(0, units, one, 0)
        back_copy(c).start()
        return carry

    lax.fori_loop(0, crops, crop, 0)
    merge(crops - 1)

    def finish(c, carry):
        for a in range(2):
            depth_copy(c, a).wait_send()
            return_copy(c, a).wait_recv()
        wide_copy(c).wait_send()
        back_copy(c).wait_send()
        return carry

    lax.fori_loop(0, crops, finish, 0)

    def close(c, carry):
        for a in range(2):
            keep_copy(c, a).wait()
            return_copy(c, a).wait_send()
        return carry

    lax.fori_loop(crops - 2, crops, close, 0)


def block_call(voxels, cotangent, table, vec_wide, mats):
    crops, planes, rows, width = voxels.shape
    hid = 4 * width
    whole = pl.BlockSpec(memory_space=pltpu.VMEM)
    far = pl.BlockSpec(memory_space=pl.ANY)
    consts = [table, vec_wide] + mats + placement()
    sem = pltpu.SemaphoreType.DMA
    return pl.pallas_call(
        block_kernel,
        in_specs=[far, far] + [whole] * len(consts),
        out_specs=[far, far] + [whole] * 6,
        out_shape=[
            jax.ShapeDtypeStruct(voxels.shape, bf),
            jax.ShapeDtypeStruct(voxels.shape, bf),
            jax.ShapeDtypeStruct((3 * width, width + 16), fl),
            jax.ShapeDtypeStruct((width, width + 16), fl),
            jax.ShapeDtypeStruct((hid, width + 16), fl),
            jax.ShapeDtypeStruct((hid, width), fl),
            jax.ShapeDtypeStruct((5 * width, 128), fl),
            jax.ShapeDtypeStruct((TOK, HEADS * 128), fl),
        ],
        scratch_shapes=[
            pltpu.VMEM((2, 2, 2, rows, width), bf),
            pltpu.VMEM((crops, 2, 2, rows, width), bf),
            pltpu.VMEM((crops, 2, rows, width), bf),
            pltpu.VMEM((crops, 2, rows, width), bf),
            pltpu.VMEM((crops, 2, rows, width), bf),
            pltpu.VMEM((crops, 2, rows, width), bf),
            pltpu.VMEM((2, 2, 4, rows, width), bf),
            sem((2, 2)),
            sem((crops, 2)),
            sem((crops, 2)),
            sem((crops,)),
            sem((crops,)),
            sem((crops,)),
            sem((crops,)),
            sem((2, 2)),
            sem((2, 2)),
            sem((crops, 2)),
        ],
        compiler_params=pltpu.CompilerParams(
            vmem_limit_bytes=60 * 2**20, collective_id=0, has_side_effects=True
        ),
        name="block",
    )(voxels, cotangent, *consts)


def make_tables(bias_table, planes, height, breadth):
    extent = (2 * WIN - 1) ** 3
    selector = (
        jnp.asarray(relative_index().T.reshape(-1), jnp.int32)[:, None]
        == jnp.arange(extent, dtype=jnp.int32)[None, :]
    ).astype(fl)
    pair_bias = jnp.einsum("hr,pr->hp", bias_table, selector, precision=lax.Precision.HIGHEST)
    pair_bias = pair_bias.reshape(HEADS, TOK, TOK)
    plane_labels = region_labels(
        planes, lax.axis_index("depth") * planes, planes * lax.axis_size("depth")
    )
    column_labels = region_labels(
        breadth, lax.axis_index("wide") * breadth, breadth * lax.axis_size("wide")
    )
    tables = []
    for place in (0, height - WIN):
        height_labels = region_labels(height, 0, height)[place : place + WIN]
        labels = (
            plane_labels[:, None, None] * 9
            + height_labels[None, :, None] * 3
            + column_labels[None, None, :]
        )
        labels = window_split(labels[None, :, :, :, None])[..., 0]
        masks = jnp.where(labels[:, :, None] == labels[:, None, :], 0.0, mask_fill).astype(fl)
        both = pair_bias[:, None] + masks[None]
        tables.append(both.transpose(2, 0, 1, 3).reshape(TOK, HEADS * 128))
    return jnp.stack(tables) * LOG2E, selector


def local(
    voxels,
    cotangent,
    project_in,
    project_out,
    expand,
    contract,
    bias_table,
    vectors,
    project_in_first,
    project_out_first,
    expand_first,
    contract_first,
    bias_table_first,
    vectors_first,
    project_in_second,
    project_out_second,
    expand_second,
    contract_second,
    bias_table_second,
    vectors_second,
):
    batches, planes, height, breadth, width = voxels.shape
    table, selector = make_tables(bias_table, planes, height, breadth)
    vec_wide = jnp.broadcast_to(vectors[:, None], (vectors.shape[0], 128))
    in_low = project_in.astype(bf)
    out_low = project_out.astype(bf)
    expand_low = expand.astype(bf)
    contract_low = contract.astype(bf)
    mats = [
        in_low.T, in_low, out_low.T, out_low,
        expand_low.T, expand_low, contract_low, contract_low.T,
    ]
    flat = (batches, planes, height * breadth, width)
    result, token_grad, d_in, d_out, d_exp, d_con, d_vec, d_tab = block_call(
        voxels.reshape(flat), cotangent.reshape(flat), table, vec_wide, mats
    )
    sums = jnp.sum(d_vec, -1).reshape(5, width)
    vector_grad = jnp.concatenate(
        [
            sums[0],
            sums[1],
            d_in[:width, width],
            d_in[2 * width :, width],
            d_out[:, width],
            sums[2],
            sums[3],
            sums[4],
            d_exp[:, width],
        ]
    )
    table_grad = d_tab.reshape(TOK, HEADS, 2, TOK).sum(2).transpose(1, 0, 2).reshape(HEADS, -1)
    table_grad = jnp.einsum("hp,pr->hr", table_grad, selector, precision=lax.Precision.HIGHEST)
    weights = [project_in, project_out, expand, contract, bias_table, vectors]
    firsts = [
        project_in_first,
        project_out_first,
        expand_first,
        contract_first,
        bias_table_first,
        vectors_first,
    ]
    seconds = [
        project_in_second,
        project_out_second,
        expand_second,
        contract_second,
        bias_table_second,
        vectors_second,
    ]
    rates = [rate_matrix] * 4 + [rate_vector] * 2
    decays = [weight_decay] * 4 + [0.0, 0.0]
    totals = list(
        lax.psum(
            (
                d_in[:, :width].T,
                d_out[:, :width].T,
                d_exp[:, :width].T,
                d_con,
                table_grad,
                vector_grad,
            ),
            ("dp", "depth", "wide"),
        )
    )
    outputs, norm_value = whole_update(totals, weights, firsts, seconds, rates, decays)
    flat_out = [result.reshape(voxels.shape), token_grad.reshape(voxels.shape)]
    for member in range(6):
        flat_out = flat_out + list(outputs[member])
    for member in range(4):
        flat_out = flat_out + [outputs[member][3].astype(bf)]
    flat_out = flat_out + [norm_value]
    return tuple(flat_out)


def solution(mesh):
    split = P("dp", "depth", None, "wide", None)
    return jax.shard_map(
        local,
        mesh=mesh,
        in_specs=(split,) * 2 + (P(),) * 18,
        out_specs=(split,) * 2 + (P(),) * 29,
        check_vma=False,
    )
```

```python
from functools import partial

import jax
import jax.numpy as jnp
import numpy as np
from jax import lax
from jax.experimental import pallas as pl
from jax.experimental.pallas import tpu as pltpu
from jax.sharding import PartitionSpec as P

HEADS = 6
WIN = 4
SHIFT = 2
STEP = 10
TOK = WIN**3
GROUP = 4
LANES = GROUP * TOK

norm_eps = 1e-05
mask_fill = -100.0
clip_bound = 1000.0
rate_matrix = 0.1
rate_vector = 0.6
weight_decay = 0.01
beta_first = 0.9
beta_second = 0.999
adam_eps = 1e-08
LOG2E = 1.4426950408889634
INV_SQRT2 = 0.7071067811865476
INV_SQRT2PI = 0.3989422804014327


def relative_index():
    extent = 2 * WIN - 1
    corner = np.arange(WIN)
    places = np.stack(np.meshgrid(corner, corner, corner, indexing="ij"), -1).reshape(-1, 3)
    offsets = places[:, None, :] - places[None, :, :] + WIN - 1
    return (offsets[..., 0] * extent + offsets[..., 1]) * extent + offsets[..., 2]


def adam_update(weight, first, second, gradient, rate, decay):
    first_new = beta_first * first + (1.0 - beta_first) * gradient
    second_new = beta_second * second + (1.0 - beta_second) * gradient * gradient
    first_hat = first_new / (1.0 - beta_first**STEP)
    second_hat = second_new / (1.0 - beta_second**STEP)
    weight_new = weight - rate * (first_hat / (jnp.sqrt(second_hat) + adam_eps) + decay * weight)
    return (first_new, second_new, weight_new)


fl = jnp.float32
bf = jnp.bfloat16


def dot(a, b):
    return jnp.dot(a, b, preferred_element_type=fl)


def dot_nt(a, b):
    return lax.dot_general(a, b, (((1,), (1,)), ((), ())), preferred_element_type=fl)


def wide(v, lanes):
    return jnp.concatenate([v] * (lanes // v.shape[1]), axis=1)


def unit_norm(v):
    width = v.shape[0]
    mean = jnp.sum(v, 0, keepdims=True) * (1.0 / width)
    centred = v - mean
    inverse = lax.rsqrt(jnp.sum(centred * centred, 0, keepdims=True) * (1.0 / width) + norm_eps)
    return centred * inverse, inverse


def unit_back(grad, unit, inverse, gain):
    width = grad.shape[0]
    scaled = grad * gain
    inner = jnp.sum(scaled, 0, keepdims=True) * (1.0 / width)
    along = jnp.sum(scaled * unit, 0, keepdims=True) * (1.0 / width)
    return inverse * (scaled - inner - unit * along)


def fold(v):
    total = v[:, :128]
    for lane in range(128, v.shape[1], 128):
        total = total + v[:, lane : lane + 128]
    return total


def pair_blocks(low, c0, rows, lane0):
    count = rows // 32
    zero = jnp.zeros((32, 128), bf)
    out = []
    for a in range(count):
        out.append(
            jnp.concatenate(
                [
                    low[c0 + 32 * a : c0 + 32 * a + 32, lane0 : lane0 + 128] if a == b else zero
                    for b in range(count)
                ],
                axis=1,
            )
        )
    return jnp.concatenate(out, axis=0)


def cross(token_major, low, lane0, first_half):
    pieces = []
    for c0, rows in ((0, 128), (128, 64)):
        full = dot(
            token_major[lane0 : lane0 + 128, c0 : c0 + rows], pair_blocks(low, c0, rows, lane0)
        )
        for b in range(rows // 32):
            block = full[:, 128 * b : 128 * b + 128]
            pieces.append(jnp.where(first_half, block[:TOK], block[TOK:]))
    return pieces


def two_windows(compact, first_half):
    zero = jnp.zeros_like(compact)
    return jnp.concatenate(
        [jnp.where(first_half, compact, zero), jnp.where(first_half, zero, compact)], axis=0
    )


def placement():
    take = np.zeros((LANES, LANES + TOK), np.float32)
    give = np.zeros((LANES + TOK, LANES), np.float32)
    pick = np.zeros((TOK, LANES), np.float32)
    fill = np.zeros((LANES, TOK), np.float32)
    for hw in range(2):
        for ww in range(2):
            for d in range(WIN):
                for hh in range(WIN):
                    for wl in range(WIN):
                        t = ((hw * 2 + ww) * WIN + d) * 16 + hh * 4 + wl
                        h, w = 4 * hw + hh, 4 * ww + wl
                        if w < 2 * WIN - SHIFT:
                            row = d * 64 + h * 8 + w + SHIFT
                        else:
                            row = LANES + d * 16 + h * 2 + w - (2 * WIN - SHIFT)
                        take[t, row] = 1.0
                        give[row, t] = 1.0
    for d in range(WIN):
        for h in range(2 * WIN):
            for w in range(SHIFT):
                pick[d * 16 + h * 2 + w, d * 64 + h * 8 + w] = 1.0
                fill[d * 64 + h * 8 + w, d * 16 + h * 2 + w] = 1.0
    return [jnp.asarray(m, bf) for m in (take, give, pick, fill)]


def block_kernel(
    vox,
    cot,
    f_in,
    f_out,
    f_exp,
    f_con,
    bias_ref,
    vectors_ref,
    related,
    take,
    give,
    pick,
    fill,
    out_res,
    out_tok,
    out_total,
    table_ref,
    vec_ref,
    w_in_t,
    w_in,
    w_out_t,
    w_out,
    w_exp_t,
    w_exp,
    w_con,
    w_con_t,
    acc_in,
    acc_exp,
    acc_con,
    d_vec,
    d_tab,
    d_row,
    bucket,
    landed,
    partial_sum,
    landed_two,
    total,
    own,
    halo_d,
    halo_w,
    send_w,
    back_send,
    back_recv,
    grid_out,
    own_sem,
    d_send,
    d_recv,
    w_send,
    w_recv,
    b_send,
    b_recv,
    o_sem,
    r_send,
    r_recv,
    s1_send,
    s1_recv,
    s2_send,
    s2_recv,
    s3_send,
    s3_recv,
    s4_send,
    s4_recv,
):
    crops = vox.shape[0]
    rows = vox.shape[2]
    width = vox.shape[3]
    units = rows // TOK
    n = LANES
    depth, peers_d = lax.axis_index("depth"), lax.axis_size("depth")
    column, peers_w = lax.axis_index("wide"), lax.axis_size("wide")
    d_prev = {"depth": lax.rem(depth + peers_d - 1, peers_d)}
    d_next = {"depth": lax.rem(depth + 1, peers_d)}
    w_prev = {"wide": lax.rem(column + peers_w - 1, peers_w)}
    w_next = {"wide": lax.rem(column + 1, peers_w)}
    mesh_id = pl.DeviceIdType.MESH
    sources = (vox, cot)
    results = (out_res, out_tok)

    def own_copy(c, a):
        slot = lax.rem(c, 2)
        return pltpu.make_async_copy(
            sources[a].at[c, pl.ds(SHIFT, 2)], own.at[slot, a], own_sem.at[slot, a]
        )

    def depth_copy(c, a):
        return pltpu.make_async_remote_copy(
            src_ref=sources[a].at[c, pl.ds(0, SHIFT)],
            dst_ref=halo_d.at[c, a],
            send_sem=d_send.at[c, a],
            recv_sem=d_recv.at[c, a],
            device_id=d_prev,
            device_id_type=mesh_id,
        )

    def wide_copy(c):
        return pltpu.make_async_remote_copy(
            src_ref=send_w.at[c],
            dst_ref=halo_w.at[c],
            send_sem=w_send.at[c],
            recv_sem=w_recv.at[c],
            device_id=w_prev,
            device_id_type=mesh_id,
        )

    def back_copy(c):
        return pltpu.make_async_remote_copy(
            src_ref=back_send.at[c],
            dst_ref=back_recv.at[c],
            send_sem=b_send.at[c],
            recv_sem=b_recv.at[c],
            device_id=w_next,
            device_id_type=mesh_id,
        )

    def keep_copy(c, a):
        slot = lax.rem(c, 2)
        return pltpu.make_async_copy(
            grid_out.at[slot, a, pl.ds(0, 2)], results[a].at[c, pl.ds(SHIFT, 2)], o_sem.at[slot, a]
        )

    def return_copy(c, a):
        slot = lax.rem(c, 2)
        return pltpu.make_async_remote_copy(
            src_ref=grid_out.at[slot, a, pl.ds(2, 2)],
            dst_ref=results[a].at[c, pl.ds(0, SHIFT)],
            send_sem=r_send.at[slot, a],
            recv_sem=r_recv.at[c, a],
            device_id=d_next,
            device_id_type=mesh_id,
        )

    crew = lax.axis_size("dp") * peers_d
    place = lax.axis_index("dp") * peers_d + depth

    def mate(step):
        other = lax.rem(place + step, crew)
        return other, {"dp": other // peers_d, "depth": lax.rem(other, peers_d)}

    def across(step):
        other = lax.rem(column + step, peers_w)
        return other, {"wide": other}

    barrier = pltpu.get_barrier_semaphore()
    for step in range(1, crew):
        pl.semaphore_signal(barrier, inc=1, device_id=mate(step)[1], device_id_type=mesh_id)
    for step in range(1, peers_w):
        pl.semaphore_signal(barrier, inc=1, device_id=across(step)[1], device_id_type=mesh_id)
    pl.semaphore_wait(barrier, crew + peers_w - 2)

    for a in range(2):
        own_copy(0, a).start()

    def send_depth(c, carry):
        for a in range(2):
            depth_copy(c, a).start()
        return carry

    lax.fori_loop(0, crops, send_depth, 0)
    for ref in (acc_in, acc_exp, acc_con, d_vec, d_tab):
        ref[...] = jnp.zeros_like(ref)
    for source, straight, turned in (
        (f_in, w_in, w_in_t),
        (f_out, w_out, w_out_t),
        (f_exp, w_exp, w_exp_t),
        (f_con, w_con_t, w_con),
    ):
        straight[...] = source[...].astype(bf)
        turned[...] = source[...].T.astype(bf)
    for tile in range(vectors_ref.shape[0]):
        vec_ref[128 * tile : 128 * tile + 128, :] = jnp.broadcast_to(
            vectors_ref[tile : tile + 1, :], (128, 128)
        ).T

    def chooser(places):
        return (
            lax.broadcasted_iota(jnp.int32, (384, 128), 0)
            == jnp.broadcast_to(places, (384, 128))
        ).astype(bf)

    def eight(block):
        return pl.ds(pl.multiple_of(8 * block, 8), 8)

    def thirds(v):
        high = v.astype(bf)
        rest = v - high.astype(fl)
        middle = rest.astype(bf)
        return jnp.concatenate([high, middle, (rest - middle.astype(fl)).astype(bf)], axis=0)

    def ends(v):
        return v[:8] + v[8:16] + v[16:24]

    def code(at, window, edge):
        last_d = (depth == peers_d - 1).astype(jnp.int32)
        last_w = (column == peers_w - 1).astype(jnp.int32)
        d, h, w = at // 16, lax.rem(at // 4, 4), lax.rem(at, 4)
        return (
            last_d * (d >= SHIFT).astype(jnp.int32) * 4
            + edge * (h >= SHIFT).astype(jnp.int32) * 2
            + last_w * window * (w >= SHIFT).astype(jnp.int32)
        )

    bias_parts = thirds(bias_ref[...])

    def table_rows(block, carry):
        near = related[eight(block), :]
        found = [ends(dot(bias_parts, chooser(near[k : k + 1]))) for k in range(8)]
        lane = lax.broadcasted_iota(jnp.int32, (8, 128), 1)
        j = lax.broadcasted_iota(jnp.int32, (8, 128), 0) + 8 * block
        window, i = lane // TOK, lax.rem(lane, TOK)
        for edge in range(2):
            differ = code(i, window, edge) != code(j, window, edge)
            mask = jnp.where(differ, mask_fill, 0.0)
            for head in range(HEADS):
                values = jnp.concatenate([row[head : head + 1, :] for row in found], axis=0)
                table_ref[edge, eight(block), 128 * head : 128 * head + 128] = (
                    values + mask
                ) * LOG2E
        return carry

    lax.fori_loop(0, TOK // 8, table_rows, 0)

    def starts(u):
        first = pl.multiple_of(u * TOK + 16, 16)
        second = pl.multiple_of(lax.rem(u * TOK + TOK, rows), 16)
        return first, second

    def natural(c, a, u):
        first, second = starts(u)
        slot = lax.rem(c, 2)
        parts = []
        for d in range(2):
            parts.append(own[slot, a, d, pl.ds(first, 48), :])
            parts.append(own[slot, a, d, pl.ds(second, 16), :])
        for d in range(2):
            parts.append(halo_d[c, a, d, pl.ds(first, 48), :])
            parts.append(halo_d[c, a, d, pl.ds(second, 16), :])
        return jnp.concatenate(parts, axis=0)

    def pack(c):
        for a in range(2):
            own_copy(c, a).wait()
            depth_copy(c, a).wait_recv()

        def one(u, carry):
            for a in range(2):
                send_w[c, a, pl.ds(pl.multiple_of(u * TOK, TOK), TOK), :] = dot(
                    pick[...], natural(c, a, u)
                ).astype(bf)
            return carry

        lax.fori_loop(0, units, one, 0)
        wide_copy(c).start()

    def merge(c):
        slot = lax.rem(c, 2)
        back_copy(c).wait_recv()

        def one(u, carry):
            first, second = starts(u)
            for a in range(2):
                extra = dot(fill[...], back_recv[c, a, pl.ds(pl.multiple_of(u * TOK, TOK), TOK), :])
                for d in range(WIN):
                    for start, size, at in ((first, 48, 64 * d), (second, 16, 64 * d + 48)):
                        place = pl.ds(start, size)
                        grid_out[slot, a, d, place, :] = (
                            grid_out[slot, a, d, place, :].astype(fl) + extra[at : at + size]
                        ).astype(bf)
            return carry

        lax.fori_loop(0, units, one, 0)
        for a in range(2):
            keep_copy(c, a).start()
            return_copy(c, a).start()

    eye_c = (
        lax.broadcasted_iota(jnp.int32, (width, width), 0)
        == lax.broadcasted_iota(jnp.int32, (width, width), 1)
    ).astype(bf)
    eye_t = (
        lax.broadcasted_iota(jnp.int32, (n, n), 0) == lax.broadcasted_iota(jnp.int32, (n, n), 1)
    ).astype(bf)
    first_half = lax.broadcasted_iota(jnp.int32, (TOK, 128), 1) < TOK
    ones = jnp.ones((16, n), bf)
    scale = 32 ** (-0.5)

    def vec(index, size=width):
        return wide(vec_ref[index : index + size, :], n)

    def unit(c, u):
        here = pl.ds(pl.multiple_of(u * TOK, TOK), TOK)

        def tokens(a):
            low = dot(
                take[...], jnp.concatenate([natural(c, a, u), halo_w[c, a, here, :]], axis=0)
            ).astype(bf)
            return dot_nt(eye_c, low)

        def put(a, low):
            first, second = starts(u)
            slot = lax.rem(c, 2)
            placed = dot_nt(give[...], low).astype(bf)
            for d in range(WIN):
                grid_out[slot, a, d, pl.ds(first, 48), :] = placed[64 * d : 64 * d + 48]
                grid_out[slot, a, d, pl.ds(second, 16), :] = placed[64 * d + 48 : 64 * d + 64]
            back_send[c, a, here, :] = placed[n:]

        x = tokens(0)
        up = tokens(1)
        up_low = up.astype(bf)
        unit_one, inverse_one = unit_norm(x)
        entry_one = (unit_one * vec(0) + vec(width)).astype(bf)
        triple = dot(w_in_t[...], entry_one)
        query = (triple[:width] + vec(2 * width)).astype(bf)
        keys = triple[width : 2 * width].astype(bf)
        values = (triple[2 * width :] + vec(3 * width)).astype(bf)
        turned = dot_nt(eye_t, jnp.concatenate([keys, values], axis=0)).astype(bf)
        keys_t = turned[:, :width]
        values_t = turned[:, width:]
        probs = []
        probs_wide = []
        mixed = []
        edge = (u == units - 1).astype(jnp.int32)
        for half in range(2):
            lane0 = 128 * half
            pieces = cross(keys_t, query, lane0, first_half)
            which = edge if half == 1 else 0
            cols = []
            for head in range(HEADS):
                s = (
                    pieces[head] * (scale * LOG2E)
                    + table_ref[which, :, 128 * head : 128 * head + 128]
                )
                e = jnp.exp2(s - jnp.max(s, 0, keepdims=True))
                p = e * (1.0 / jnp.sum(e, 0, keepdims=True))
                p_wide = two_windows(p.astype(bf), first_half)
                probs.append(p)
                probs_wide.append(p_wide)
                cols.append(dot(values[32 * head : 32 * head + 32, lane0 : lane0 + 128], p_wide))
            mixed.append(jnp.concatenate(cols, axis=0))
        mixed = jnp.concatenate(mixed, axis=1).astype(bf)
        middle = x + dot(w_out_t[...], mixed) + vec(4 * width)
        unit_two, inverse_two = unit_norm(middle)
        entry_two = (unit_two * vec(5 * width) + vec(6 * width)).astype(bf)
        hidden = dot(w_exp_t[...], entry_two) + vec(8 * width, 4 * width)
        phi = 0.5 + 0.5 * lax.erf(hidden * INV_SQRT2)
        slope = phi + hidden * (INV_SQRT2PI * jnp.exp2(hidden * hidden * (-0.5 * LOG2E)))
        active = (hidden * phi).astype(bf)
        result = middle + dot(w_con_t[...], active) + vec(7 * width)
        put(0, result.astype(bf))
        hidden_low = (dot(w_con[...], up_low) * slope).astype(bf)
        grad_two = dot(w_exp[...], hidden_low)
        middle_grad = up + unit_back(grad_two, unit_two, inverse_two, vec(5 * width))
        branch_low = middle_grad.astype(bf)
        mixed_low = dot(w_out[...], branch_low).astype(bf)
        d_cols = [[], [], []]
        for half in range(2):
            lane0 = 128 * half
            pieces = cross(values_t, mixed_low, lane0, first_half)
            dq, dk, dv = [], [], []
            for head in range(HEADS):
                p = probs[half * HEADS + head]
                pg = pieces[head]
                sg = (p * (pg - jnp.sum(pg * p, 0, keepdims=True))).astype(bf)
                d_tab[:, 128 * head : 128 * head + 128] += sg.astype(fl)
                s_wide = two_windows(sg, first_half)
                at = slice(32 * head, 32 * head + 32)
                dq.append(dot(keys[at, lane0 : lane0 + 128], s_wide))
                dk.append(dot_nt(query[at, lane0 : lane0 + 128], s_wide))
                dv.append(
                    dot_nt(mixed_low[at, lane0 : lane0 + 128], probs_wide[half * HEADS + head])
                )
            for member, part in enumerate((dq, dk, dv)):
                d_cols[member].append(jnp.concatenate(part, axis=0))
        dq, dk, dv = [jnp.concatenate(part, axis=1) for part in d_cols]
        triple_low = jnp.concatenate([dq * scale, dk * scale, dv], axis=0).astype(bf)
        grad_one = dot(w_in[...], triple_low)
        token_grad = middle_grad + unit_back(grad_one, unit_one, inverse_one, vec(0))
        put(1, token_grad.astype(bf))
        acc_in[: 3 * width, :] += dot_nt(triple_low, jnp.concatenate([entry_one, ones], axis=0))
        acc_in[3 * width :, :] += dot_nt(branch_low, jnp.concatenate([mixed, ones], axis=0))
        acc_exp[...] += dot_nt(hidden_low, jnp.concatenate([entry_two, ones], axis=0))
        acc_con[...] += dot_nt(active, up_low)
        d_vec[0:width, :] += fold(grad_one * unit_one)
        d_vec[width : 2 * width, :] += fold(grad_one)
        d_vec[2 * width : 3 * width, :] += fold(grad_two * unit_two)
        d_vec[3 * width : 4 * width, :] += fold(grad_two)
        d_vec[4 * width : 5 * width, :] += fold(up)

    pack(0)

    def crop(c, carry):
        wide_copy(c).wait_recv()

        @pl.when(c + 1 < crops)
        def _():
            for a in range(2):
                own_copy(c + 1, a).start()

        @pl.when(c >= 2)
        def _():
            for a in range(2):
                keep_copy(c - 2, a).wait()
                return_copy(c - 2, a).wait_send()

        def one(u, inner):
            unit(c, u)

            @pl.when((u == 1) & (c + 1 < crops))
            def _():
                pack(c + 1)

            @pl.when((u == units - 2) & (c > 0))
            def _():
                merge(c - 1)

            return inner

        lax.fori_loop(0, units, one, 0)
        back_copy(c).start()
        return carry

    lax.fori_loop(0, crops, crop, 0)

    extra = 18 * width
    for tile in range(12):
        acc, at = ((acc_in, 128 * tile), (acc_exp, 128 * (tile - 6)))[tile // 6]
        turned = acc[at : at + 128, :].T
        bucket[width * tile : width * tile + width, :] = turned[:width].astype(bf)
        d_row[tile : tile + 1, :] = turned[width : width + 1]
    for tile in range(6):
        bucket[width * (12 + tile) : width * (13 + tile), :] = (
            acc_con[128 * tile : 128 * tile + 128, :].T.astype(bf)
        )
    for tile in range(8):
        size = min(128, 5 * width - 128 * tile)
        d_row[12 + tile : 13 + tile, :size] = jnp.sum(
            d_vec[128 * tile : 128 * tile + size, :].T, 0, keepdims=True
        )
    d_row[19:20, 64:] = jnp.zeros((1, 64), fl)

    def table_sums(block, carry):
        near = related[eight(block), :]
        held = d_tab[eight(block), :]
        for k in range(8):
            rows_k = jnp.concatenate(
                [held[k : k + 1, 128 * head : 128 * head + 128] for head in range(HEADS)]
                + [jnp.zeros((2, 128), fl)],
                axis=0,
            )
            carry = carry + dot_nt(thirds(rows_k), chooser(near[k : k + 1]))
        return carry

    sums = ends(lax.fori_loop(0, TOK // 8, table_sums, jnp.zeros((24, 384), fl)))
    for tile in range(3):
        d_row[24 + 8 * tile : 32 + 8 * tile, :] = sums[:, 128 * tile : 128 * tile + 128]
    d_row[20:24, :] = jnp.zeros((4, 128), fl)
    bucket[extra : extra + 48, :] = d_row[...].astype(bf)
    length = bucket.shape[0]
    if length > extra + 48:
        bucket[extra + 48 :, :] = jnp.zeros((length - extra - 48, 128), bf)

    share = length // crew
    piece = share // peers_w

    def span(start, size):
        return pl.ds(pl.multiple_of(start, 16), size)

    def first_copy(step):
        other, peer = mate(step)
        return pltpu.make_async_remote_copy(
            src_ref=bucket.at[span(other * share, share)],
            dst_ref=landed.at[step - 1],
            send_sem=s1_send.at[step - 1],
            recv_sem=s1_recv.at[step - 1],
            device_id=peer,
            device_id_type=mesh_id,
        )

    def second_copy(step):
        other, peer = across(step)
        return pltpu.make_async_remote_copy(
            src_ref=partial_sum.at[span(other * piece, piece)],
            dst_ref=landed_two.at[step - 1],
            send_sem=s2_send.at[step - 1],
            recv_sem=s2_recv.at[step - 1],
            device_id=peer,
            device_id_type=mesh_id,
        )

    def third_copy(step):
        rows_mine = total.at[span(place * share + column * piece, piece)]
        return pltpu.make_async_remote_copy(
            src_ref=rows_mine,
            dst_ref=rows_mine,
            send_sem=s3_send.at[step - 1],
            recv_sem=s3_recv.at[step - 1],
            device_id=across(step)[1],
            device_id_type=mesh_id,
        )

    def fourth_copy(step):
        rows_mine = total.at[span(place * share, share)]
        return pltpu.make_async_remote_copy(
            src_ref=rows_mine,
            dst_ref=rows_mine,
            send_sem=s4_send.at[step - 1],
            recv_sem=s4_recv.at[step - 1],
            device_id=mate(step)[1],
            device_id_type=mesh_id,
        )

    def third_arrival(step):
        other = lax.rem(column + peers_w - step, peers_w)
        rows_there = total.at[span(place * share + other * piece, piece)]
        return pltpu.make_async_remote_copy(
            src_ref=rows_there,
            dst_ref=rows_there,
            send_sem=s3_send.at[step - 1],
            recv_sem=s3_recv.at[step - 1],
            device_id=across(step)[1],
            device_id_type=mesh_id,
        )

    def fourth_arrival(step):
        other = lax.rem(place + crew - step, crew)
        rows_there = total.at[span(other * share, share)]
        return pltpu.make_async_remote_copy(
            src_ref=rows_there,
            dst_ref=rows_there,
            send_sem=s4_send.at[step - 1],
            recv_sem=s4_recv.at[step - 1],
            device_id=mate(step)[1],
            device_id_type=mesh_id,
        )

    for step in range(1, crew):
        first_copy(step).start()
    merge(crops - 1)
    for step in range(1, crew):
        first_copy(step).wait_recv()
    summed = bucket[span(place * share, share), :].astype(fl)
    for step in range(1, crew):
        summed = summed + landed[step - 1].astype(fl)
    partial_sum[...] = summed.astype(bf)
    for step in range(1, peers_w):
        second_copy(step).start()
    for step in range(1, peers_w):
        second_copy(step).wait_recv()
    summed = partial_sum[span(column * piece, piece), :].astype(fl)
    for step in range(1, peers_w):
        summed = summed + landed_two[step - 1].astype(fl)
    total[span(place * share + column * piece, piece), :] = summed.astype(bf)
    for step in range(1, peers_w):
        third_copy(step).start()
    for step in range(1, peers_w):
        third_arrival(step).wait_recv()
    for step in range(1, crew):
        fourth_copy(step).start()
    for step in range(1, crew):
        fourth_arrival(step).wait_recv()
    out_total[...] = total[...]
    for step in range(1, crew):
        first_copy(step).wait_send()
        fourth_copy(step).wait_send()
    for step in range(1, peers_w):
        second_copy(step).wait_send()
        third_copy(step).wait_send()

    def finish(c, carry):
        for a in range(2):
            depth_copy(c, a).wait_send()
            return_copy(c, a).wait_recv()
        wide_copy(c).wait_send()
        back_copy(c).wait_send()
        return carry

    lax.fori_loop(0, crops, finish, 0)

    def close(c, carry):
        for a in range(2):
            keep_copy(c, a).wait()
            return_copy(c, a).wait_send()
        return carry

    lax.fori_loop(crops - 2, crops, close, 0)


def block_call(voxels, cotangent, matrices, bias_table, vectors):
    crops, planes, rows, width = voxels.shape
    hid = 4 * width
    whole = pl.BlockSpec(memory_space=pltpu.VMEM)
    far = pl.BlockSpec(memory_space=pl.ANY)
    related = relative_index().T
    related = jnp.asarray(np.concatenate([related, related], axis=1), jnp.int32)
    consts = list(matrices) + [bias_table, vectors, related] + placement()
    sem = pltpu.SemaphoreType.DMA
    crew = lax.axis_size("dp") * lax.axis_size("depth")
    peers_w = lax.axis_size("wide")
    unit_rows = 16 * crew * peers_w
    length = -(-(18 * width + 48) // unit_rows) * unit_rows
    share = length // crew
    piece = share // peers_w
    return pl.pallas_call(
        block_kernel,
        in_specs=[far, far] + [whole] * len(consts),
        out_specs=[far, far, whole],
        out_shape=[
            jax.ShapeDtypeStruct(voxels.shape, bf),
            jax.ShapeDtypeStruct(voxels.shape, bf),
            jax.ShapeDtypeStruct((length, 128), bf),
        ],
        scratch_shapes=[
            pltpu.VMEM((2, TOK, HEADS * 128), fl),
            pltpu.VMEM((12 * width, 128), fl),
            pltpu.VMEM((3 * width, width), bf),
            pltpu.VMEM((width, 3 * width), bf),
            pltpu.VMEM((width, width), bf),
            pltpu.VMEM((width, width), bf),
            pltpu.VMEM((hid, width), bf),
            pltpu.VMEM((width, hid), bf),
            pltpu.VMEM((hid, width), bf),
            pltpu.VMEM((width, hid), bf),
            pltpu.VMEM((4 * width, width + 16), fl),
            pltpu.VMEM((hid, width + 16), fl),
            pltpu.VMEM((hid, width), fl),
            pltpu.VMEM((5 * width, 128), fl),
            pltpu.VMEM((TOK, HEADS * 128), fl),
            pltpu.VMEM((48, 128), fl),
            pltpu.VMEM((length, 128), bf),
            pltpu.VMEM((crew - 1, share, 128), bf),
            pltpu.VMEM((share, 128), bf),
            pltpu.VMEM((peers_w - 1, piece, 128), bf),
            pltpu.VMEM((length, 128), bf),
            pltpu.VMEM((2, 2, 2, rows, width), bf),
            pltpu.VMEM((crops, 2, 2, rows, width), bf),
            pltpu.VMEM((crops, 2, rows, width), bf),
            pltpu.VMEM((crops, 2, rows, width), bf),
            pltpu.VMEM((crops, 2, rows, width), bf),
            pltpu.VMEM((crops, 2, rows, width), bf),
            pltpu.VMEM((2, 2, 4, rows, width), bf),
            sem((2, 2)),
            sem((crops, 2)),
            sem((crops, 2)),
            sem((crops,)),
            sem((crops,)),
            sem((crops,)),
            sem((crops,)),
            sem((2, 2)),
            sem((2, 2)),
            sem((crops, 2)),
            sem((crew - 1,)),
            sem((crew - 1,)),
            sem((peers_w - 1,)),
            sem((peers_w - 1,)),
            sem((peers_w - 1,)),
            sem((peers_w - 1,)),
            sem((crew - 1,)),
            sem((crew - 1,)),
        ],
        compiler_params=pltpu.CompilerParams(
            vmem_limit_bytes=60 * 2**20, collective_id=0, has_side_effects=True
        ),
        name="block",
    )(voxels, cotangent, *consts)


def update_kernel(*refs):
    far_in, total, params, far_out, outs, norm_ref, held, in_sem, out_sem = (
        refs[0:2], refs[2], refs[3:21], refs[21:23], refs[23:51], refs[51], refs[52],
        refs[53], refs[54],
    )
    crops = far_in[0].shape[0]

    def fetch(a, c):
        return pltpu.make_async_copy(far_in[a].at[c], held.at[a, c], in_sem.at[a, c])

    def store(a, c):
        return pltpu.make_async_copy(held.at[a, c], far_out[a].at[c], out_sem.at[a, c])

    for a in range(2):
        for c in range(crops):
            fetch(a, c).start()
    for a in range(2):
        for c in range(crops):
            fetch(a, c).wait()
            store(a, c).start()
    width = 192

    def slab(tile):
        return total[width * tile : width * tile + width, :].astype(fl)

    small = total[18 * width : 18 * width + 48, :].astype(fl)
    low_half = slab(4)
    grads = [
        jnp.concatenate([slab(k) for k in range(4)] + [low_half[:, :64]], axis=1),
        jnp.concatenate([low_half[:, 64:], slab(5)], axis=1),
        jnp.concatenate([slab(k) for k in range(6, 12)], axis=1),
        jnp.concatenate([slab(k) for k in range(12, 18)], axis=1),
    ]
    flat_bias = jnp.concatenate([small[k : k + 1] for k in range(12)], axis=1)
    flat_sum = jnp.concatenate([small[k : k + 1] for k in range(12, 20)], axis=1)

    def cut(flat, index):
        return flat[:, width * index : width * index + width]

    table = jnp.concatenate([small[24:32], small[32:40], small[40:48]], axis=1)
    grads.append(table[:HEADS, : params[4].shape[1]])
    grads.append(
        jnp.concatenate(
            [
                cut(flat_sum, 0), cut(flat_sum, 1), cut(flat_bias, 0), cut(flat_bias, 2),
                cut(flat_bias, 3), cut(flat_sum, 2), cut(flat_sum, 3), cut(flat_sum, 4),
                flat_bias[:, 4 * width : 8 * width],
            ],
            axis=1,
        )
    )
    squares = jnp.zeros((1, 1), fl)
    for grad in grads:
        squares = squares + jnp.sum(
            jnp.sum(grad * grad, 0, keepdims=True), 1, keepdims=True
        )
    norm_value = jnp.sqrt(squares)
    norm_ref[...] = norm_value
    factor = jnp.minimum(1.0, clip_bound / (norm_value + 1e-06))
    for member in range(6):
        matrix = member < 4
        clipped = grads[member] * factor
        first, second, fresh = adam_update(
            params[member][...],
            params[6 + member][...],
            params[12 + member][...],
            clipped,
            rate_matrix if matrix else rate_vector,
            weight_decay if matrix else 0.0,
        )
        for place, value in enumerate((clipped, first, second, fresh)):
            outs[4 * member + place][...] = value
        if matrix:
            outs[24 + member][...] = fresh.astype(bf)
    for a in range(2):
        for c in range(crops):
            store(a, c).wait()


def update_call(result, token_grad, total, params):
    whole = pl.BlockSpec(memory_space=pltpu.VMEM)
    far = pl.BlockSpec(memory_space=pl.ANY)
    shapes = []
    for member in range(6):
        shapes = shapes + [jax.ShapeDtypeStruct(params[member].shape, fl)] * 4
    for member in range(4):
        shapes.append(jax.ShapeDtypeStruct(params[member].shape, bf))
    shapes.append(jax.ShapeDtypeStruct((1, 1), fl))
    big = jax.ShapeDtypeStruct(result.shape, bf)
    return pl.pallas_call(
        update_kernel,
        in_specs=[far, far, whole] + [whole] * 18,
        out_specs=[far, far] + [whole] * 29,
        out_shape=[big, big] + shapes,
        scratch_shapes=[
            pltpu.VMEM((2,) + result.shape, bf),
            pltpu.SemaphoreType.DMA((2, result.shape[0])),
            pltpu.SemaphoreType.DMA((2, result.shape[0])),
        ],
        compiler_params=pltpu.CompilerParams(vmem_limit_bytes=56 * 2**20),
        name="update",
    )(result, token_grad, total, *params)


def local(
    voxels,
    cotangent,
    project_in,
    project_out,
    expand,
    contract,
    bias_table,
    vectors,
    project_in_first,
    project_out_first,
    expand_first,
    contract_first,
    bias_table_first,
    vectors_first,
    project_in_second,
    project_out_second,
    expand_second,
    contract_second,
    bias_table_second,
    vectors_second,
):
    batches, planes, height, breadth, width = voxels.shape
    flat = (batches, planes, height * breadth, width)
    result, token_grad, total = block_call(
        voxels.reshape(flat),
        cotangent.reshape(flat),
        (project_in, project_out, expand, contract.T),
        jnp.pad(bias_table, ((0, 2), (0, 384 - bias_table.shape[1]))),
        vectors.reshape(-1, 128),
    )
    params = [
        project_in,
        project_out,
        expand,
        contract.T,
        bias_table,
        vectors.reshape(1, -1),
        project_in_first,
        project_out_first,
        expand_first,
        contract_first.T,
        bias_table_first,
        vectors_first.reshape(1, -1),
        project_in_second,
        project_out_second,
        expand_second,
        contract_second.T,
        bias_table_second,
        vectors_second.reshape(1, -1),
    ]
    done = update_call(result, token_grad, total, params)
    outs = list(done[2:30])
    for place in range(20, 24):
        outs[place] = outs[place].reshape(-1)
    for place in (12, 13, 14, 15, 27):
        outs[place] = outs[place].T
    return (
        (done[0].reshape(voxels.shape), done[1].reshape(voxels.shape))
        + tuple(outs)
        + (done[30].reshape(()),)
    )


def solution(mesh):
    split = P("dp", "depth", None, "wide", None)
    return jax.shard_map(
        local,
        mesh=mesh,
        in_specs=(split,) * 2 + (P(),) * 18,
        out_specs=(split,) * 2 + (P(),) * 29,
        check_vma=False,
    )
```

```python
from functools import partial

import jax
import jax.numpy as jnp
import numpy as np
from jax import lax
from jax.experimental import pallas as pl
from jax.experimental.pallas import tpu as pltpu
from jax.sharding import PartitionSpec as P

HEADS = 6
WIN = 4
SHIFT = 2
STEP = 10
TOK = WIN**3
GROUP = 4
LANES = GROUP * TOK

norm_eps = 1e-05
mask_fill = -100.0
clip_bound = 1000.0
rate_matrix = 0.1
rate_vector = 0.6
weight_decay = 0.01
beta_first = 0.9
beta_second = 0.999
adam_eps = 1e-08
LOG2E = 1.4426950408889634
INV_SQRT2 = 0.7071067811865476
INV_SQRT2PI = 0.3989422804014327


def relative_index():
    extent = 2 * WIN - 1
    corner = np.arange(WIN)
    places = np.stack(np.meshgrid(corner, corner, corner, indexing="ij"), -1).reshape(-1, 3)
    offsets = places[:, None, :] - places[None, :, :] + WIN - 1
    return (offsets[..., 0] * extent + offsets[..., 1]) * extent + offsets[..., 2]


def adam_update(weight, first, second, gradient, rate, decay):
    first_new = beta_first * first + (1.0 - beta_first) * gradient
    second_new = beta_second * second + (1.0 - beta_second) * gradient * gradient
    first_hat = first_new / (1.0 - beta_first**STEP)
    second_hat = second_new / (1.0 - beta_second**STEP)
    weight_new = weight - rate * (first_hat / (jnp.sqrt(second_hat) + adam_eps) + decay * weight)
    return (first_new, second_new, weight_new)


fl = jnp.float32
bf = jnp.bfloat16


def dot(a, b):
    return jnp.dot(a, b, preferred_element_type=fl)


def dot_nt(a, b):
    return lax.dot_general(a, b, (((1,), (1,)), ((), ())), preferred_element_type=fl)


def wide(v, lanes):
    return jnp.concatenate([v] * (lanes // v.shape[1]), axis=1)


def unit_norm(v):
    width = v.shape[0]
    mean = jnp.sum(v, 0, keepdims=True) * (1.0 / width)
    centred = v - mean
    inverse = lax.rsqrt(jnp.sum(centred * centred, 0, keepdims=True) * (1.0 / width) + norm_eps)
    return centred * inverse, inverse


def unit_back(grad, unit, inverse, gain):
    width = grad.shape[0]
    scaled = grad * gain
    inner = jnp.sum(scaled, 0, keepdims=True) * (1.0 / width)
    along = jnp.sum(scaled * unit, 0, keepdims=True) * (1.0 / width)
    return inverse * (scaled - inner - unit * along)


def fold(v):
    total = v[:, :128]
    for lane in range(128, v.shape[1], 128):
        total = total + v[:, lane : lane + 128]
    return total


def two_windows(compact, first_half):
    zero = jnp.zeros_like(compact)
    return jnp.concatenate(
        [jnp.where(first_half, compact, zero), jnp.where(first_half, zero, compact)], axis=0
    )


def two_heads(ref, head_pair, lanes):
    at = 64 * head_pair
    zero = jnp.zeros((32, 128), bf)
    return jnp.concatenate(
        [
            jnp.concatenate([ref[at : at + 32, lanes], zero], axis=1),
            jnp.concatenate([zero, ref[at + 32 : at + 64, lanes]], axis=1),
        ],
        axis=0,
    )


def cross(token_major, low, first, head_pair, first_half):
    right = two_heads(low, head_pair, slice(first, first + 128))
    if head_pair == 1:
        right = jnp.concatenate([jnp.zeros((64, 256), bf), right], axis=0)
        left = token_major[first : first + 128, 0:128]
    else:
        at = 64 * head_pair
        left = token_major[first : first + 128, at : at + 64]
    full = dot(left, right)
    out = []
    for head in range(2):
        block = full[:, 128 * head : 128 * head + 128]
        out.append(jnp.where(first_half, block[:TOK], block[TOK:]))
    return out


def weave(one, other):
    whole_one = sum(weight for weight, _ in one) + 1e-9
    whole_other = sum(weight for weight, _ in other) + 1e-9
    merged, done_one, done_other = [], 0.0, 0.0
    one, other = list(one), list(other)
    while one or other:
        if not other or (
            one
            and (done_one + one[0][0] / 2) / whole_one
            <= (done_other + other[0][0] / 2) / whole_other
        ):
            merged.append(one.pop(0))
            done_one += merged[-1][0]
        else:
            merged.append(other.pop(0))
            done_other += merged[-1][0]
    return merged


def placement():
    take = np.zeros((LANES + TOK, LANES), np.float32)
    pick = np.zeros((TOK, LANES), np.float32)
    for hw in range(2):
        for ww in range(2):
            for d in range(WIN):
                for hh in range(WIN):
                    for wl in range(WIN):
                        t = ((hw * 2 + ww) * WIN + d) * 16 + hh * 4 + wl
                        h, w = 4 * hw + hh, 4 * ww + wl
                        if w < 2 * WIN - SHIFT:
                            row = d * 64 + h * 8 + w + SHIFT
                        else:
                            row = LANES + d * 16 + h * 2 + w - (2 * WIN - SHIFT)
                        take[row, t] = 1.0
    for d in range(WIN):
        for h in range(2 * WIN):
            for w in range(SHIFT):
                pick[d * 16 + h * 2 + w, d * 64 + h * 8 + w] = 1.0
    return [jnp.asarray(m, bf) for m in (take, take.T, pick, pick.T)]


WIDTH = 192
HID = 4 * WIDTH
SPAN = 2 * LANES
PAIRS = SPAN // 128
SUBS = SPAN // LANES
SLOTS = 3
BOTH = {
    "up": ((WIDTH, SPAN), fl),
    "up_low": ((WIDTH, SPAN), bf),
    "unit_one": ((WIDTH, SPAN), fl),
    "inverse_one": ((8, SPAN), fl),
    "entry_one": ((WIDTH + 16, SPAN), bf),
    "query": ((WIDTH, SPAN), bf),
    "keys": ((WIDTH, SPAN), bf),
    "values": ((WIDTH, SPAN), bf),
    "values_t": ((SPAN, WIDTH), bf),
    "probs": ((PAIRS, HEADS, TOK, 128), fl),
    "probs_wide": ((PAIRS, HEADS, 128, 128), bf),
    "mixed": ((WIDTH + 16, SPAN), bf),
    "unit_two": ((WIDTH, SPAN), fl),
    "inverse_two": ((8, SPAN), fl),
    "entry_two": ((WIDTH + 16, SPAN), bf),
    "slope": ((HID, SPAN), fl),
    "active": ((HID, SPAN), bf),
    "edge_res": ((SUBS, WIDTH, TOK), bf),
}
ONCE = {
    "x": ((WIDTH, SPAN), fl),
    "keys_t": ((SPAN, WIDTH), bf),
    "middle": ((WIDTH, SPAN), fl),
    "result": ((WIDTH, SPAN), bf),
    "hidden_low": ((HID, SPAN), bf),
    "grad_two": ((WIDTH, SPAN), fl),
    "middle_grad": ((WIDTH, SPAN), fl),
    "branch_low": ((WIDTH, SPAN), bf),
    "mixed_low": ((WIDTH, SPAN), bf),
    "triple_low": ((3 * WIDTH, SPAN), bf),
    "grad_one": ((WIDTH, SPAN), fl),
    "token_grad": ((WIDTH, SPAN), bf),
}
WEIGHTS = {
    "table": ((2, TOK, HEADS * 128), fl),
    "vec": ((5 * WIDTH, 128), fl),
    "w_in_t": ((3 * WIDTH, WIDTH + 16), bf),
    "w_in": ((WIDTH, 3 * WIDTH), bf),
    "w_out_t": ((WIDTH, WIDTH + 16), bf),
    "w_out": ((WIDTH, WIDTH), bf),
    "w_exp_t": ((HID, WIDTH + 16), bf),
    "w_exp": ((WIDTH, HID), bf),
    "w_con": ((HID, WIDTH), bf),
    "w_con_t": ((WIDTH, HID), bf),
    "acc_in": ((4 * WIDTH, WIDTH + 16), fl),
    "acc_exp": ((HID, WIDTH + 16), fl),
    "acc_con": ((HID, WIDTH), fl),
    "d_vec": ((5 * WIDTH, 128), fl),
    "d_tab": ((TOK, HEADS * 128), fl),
    "d_row": ((48, 128), fl),
}
GAIN_ONE, SHIFT_ONE, GAIN_TWO, SHIFT_TWO, CON_BIAS = (WIDTH * k for k in range(5))
scale = 32 ** (-0.5)


def forward_tasks(r, first_half, tokens_of, edge, put):
    tasks = []
    slots = [(k, hp) for k in range(PAIRS) for hp in range(3)]
    held = {}

    def vec(at, lanes=SPAN):
        return wide(r["vec"][at : at + WIDTH, :], lanes)

    def fetch():
        rows = []
        for s in range(SUBS):
            rows = rows + tokens_of(s)
        moved = dot(jnp.concatenate(rows, axis=0), r["take"][...])
        for s in range(SUBS):
            lanes = slice(LANES * s, LANES * s + LANES)
            at = 2 * WIDTH * s
            up = moved[at + WIDTH : at + 2 * WIDTH]
            r["x"][:, lanes] = moved[at : at + WIDTH]
            r["up"][:, lanes] = up
            r["up_low"][:, lanes] = up.astype(bf)

    def norm_one():
        unit_vals, inverse = unit_norm(r["x"][...])
        r["unit_one"][...] = unit_vals
        r["inverse_one"][...] = jnp.broadcast_to(inverse, (8, SPAN))
        r["entry_one"][:WIDTH] = (unit_vals * vec(GAIN_ONE) + vec(SHIFT_ONE)).astype(bf)

    def project():
        triple = dot(r["w_in_t"][...], r["entry_one"][...]).astype(bf)
        r["query"][...] = triple[:WIDTH]
        r["keys"][...] = triple[WIDTH : 2 * WIDTH]
        r["values"][...] = triple[2 * WIDTH :]

    def turn():
        r["keys_t"][...] = r["keys"][...].T
        r["values_t"][...] = r["values"][...].T

    def scores(t):
        k, hp = slots[t]
        held["s", t] = cross(r["keys_t"], r["query"], 128 * k, hp, first_half)

    def soft(t):
        k, hp = slots[t]
        pieces = held.pop(("s", t))
        wides = []
        for head in (2 * hp, 2 * hp + 1):
            which = edge if k == PAIRS - 1 else 0
            s = (
                pieces[head - 2 * hp] * (scale * LOG2E)
                + r["table"][which, :, 128 * head : 128 * head + 128]
            )
            e = jnp.exp2(s - jnp.max(s, 0, keepdims=True))
            p = e * (1.0 / jnp.sum(e, 0, keepdims=True))
            r["probs"][k, head] = p
            p_wide = two_windows(p.astype(bf), first_half)
            r["probs_wide"][k, head] = p_wide
            wides.append(p_wide)
        held["p", t] = wides

    def mix(t):
        k, hp = slots[t]
        lanes = slice(128 * k, 128 * k + 128)
        r["mixed"][64 * hp : 64 * hp + 64, lanes] = dot(
            two_heads(r["values"], hp, lanes), jnp.concatenate(held.pop(("p", t)), axis=0)
        ).astype(bf)

    def attend(t):
        def run():
            if t == 0:
                scores(0)
            if t + 1 < len(slots):
                scores(t + 1)
            if t < len(slots):
                soft(t)
            if t >= 1:
                mix(t - 1)

        return run

    def join():
        r["middle"][...] = r["x"][...] + dot(r["w_out_t"][...], r["mixed"][...])

    def norm_two():
        unit_vals, inverse = unit_norm(r["middle"][...])
        r["unit_two"][...] = unit_vals
        r["inverse_two"][...] = jnp.broadcast_to(inverse, (8, SPAN))
        r["entry_two"][:WIDTH] = (unit_vals * vec(GAIN_TWO) + vec(SHIFT_TWO)).astype(bf)

    def gelu(s, part):
        def run():
            lanes = slice(LANES * s, LANES * s + LANES)
            rows = slice(HID // 2 * part, HID // 2 * part + HID // 2)
            hidden = dot(r["w_exp_t"][rows], r["entry_two"][:, lanes])
            twice = 1.0 + lax.erf(hidden * INV_SQRT2)
            r["active"][rows, lanes] = (hidden * twice).astype(bf)
            r["slope"][rows, lanes] = twice + hidden * (
                (2.0 * INV_SQRT2PI) * jnp.exp2(hidden * hidden * (-0.5 * LOG2E))
            )

        return run

    def contracted(s):
        def run():
            lanes = slice(LANES * s, LANES * s + LANES)
            r["result"][:, lanes] = (
                r["middle"][:, lanes]
                + dot(r["w_con_t"][...], r["active"][:, lanes])
                + vec(CON_BIAS, LANES)
            ).astype(bf)

        return run

    tasks = tasks + [(340, fetch), (120, norm_one), (180, project), (80, turn)]
    tasks = tasks + [(80, attend(t)) for t in range(len(slots) + 1)]
    tasks = tasks + [(100, join), (150, norm_two)]
    tasks = tasks + [(270, gelu(s, part)) for s in range(SUBS) for part in range(2)]
    tasks = tasks + [(130, contracted(s)) for s in range(SUBS)]
    tasks = tasks + [(70, put(s)) for s in range(SUBS)]
    return tasks


def backward_tasks(r, first_half, put):
    slots = [(k, hp) for k in range(PAIRS) for hp in range(3)]
    held = {}

    def vec(at):
        return wide(r["vec"][at : at + WIDTH, :], SPAN)

    def hidden_back(s, part):
        def run():
            lanes = slice(LANES * s, LANES * s + LANES)
            rows = slice(HID // 2 * part, HID // 2 * part + HID // 2)
            r["hidden_low"][rows, lanes] = (
                dot(r["w_con"][rows], r["up_low"][:, lanes]) * r["slope"][rows, lanes]
            ).astype(bf)

        return run

    def expand_back(s):
        def run():
            lanes = slice(LANES * s, LANES * s + LANES)
            r["grad_two"][:, lanes] = dot(r["w_exp"][...], r["hidden_low"][:, lanes])

        return run

    def norm_two_back():
        grad = r["up"][...] + unit_back(
            r["grad_two"][...], r["unit_two"][...], r["inverse_two"][0:1, :], vec(GAIN_TWO)
        )
        r["middle_grad"][...] = grad
        r["branch_low"][...] = grad.astype(bf)

    def out_back():
        r["mixed_low"][...] = dot(r["w_out"][...], r["branch_low"][...]).astype(bf)

    def expand_sum(part):
        def run():
            rows = slice(HID // 2 * part, HID // 2 * part + HID // 2)
            r["acc_exp"][rows, :] += dot_nt(r["hidden_low"][rows, :], r["entry_two"][...])

        return run

    def contract_sum(part):
        def run():
            rows = slice(HID // 2 * part, HID // 2 * part + HID // 2)
            r["acc_con"][rows, :] += dot_nt(r["active"][rows, :], r["up_low"][...])

        return run

    def prob_back(t):
        k, hp = slots[t]
        held["g", t] = cross(r["values_t"], r["mixed_low"], 128 * k, hp, first_half)

    def score_back(t):
        k, hp = slots[t]
        pieces = held.pop(("g", t))
        wides = []
        for head in (2 * hp, 2 * hp + 1):
            p, g = r["probs"][k, head], pieces[head - 2 * hp]
            s = p * (g - jnp.sum(g * p, 0, keepdims=True))
            r["d_tab"][:, 128 * head : 128 * head + 128] += s
            wides.append(two_windows(s.astype(bf), first_half))
        held["s", t] = wides

    def triple_back(t):
        k, hp = slots[t]
        wides = held.pop(("s", t))
        lanes = slice(128 * k, 128 * k + 128)
        at = 64 * hp
        r["triple_low"][at : at + 64, lanes] = (
            dot(two_heads(r["keys"], hp, lanes), jnp.concatenate(wides, axis=0)) * scale
        ).astype(bf)
        r["triple_low"][WIDTH + at : WIDTH + at + 64, lanes] = (
            dot_nt(two_heads(r["query"], hp, lanes), jnp.concatenate(wides, axis=1)) * scale
        ).astype(bf)
        probs = jnp.concatenate([r["probs_wide"][k, 2 * hp], r["probs_wide"][k, 2 * hp + 1]], axis=1)
        r["triple_low"][2 * WIDTH + at : 2 * WIDTH + at + 64, lanes] = dot_nt(
            two_heads(r["mixed_low"], hp, lanes), probs
        ).astype(bf)

    def attend(t):
        def run():
            if t == 0:
                prob_back(0)
            if t + 1 < len(slots):
                prob_back(t + 1)
            if t < len(slots):
                score_back(t)
            if t >= 1:
                triple_back(t - 1)

        return run

    def entry_back(s):
        def run():
            lanes = slice(LANES * s, LANES * s + LANES)
            r["grad_one"][:, lanes] = dot(r["w_in"][...], r["triple_low"][:, lanes])

        return run

    def in_sum():
        r["acc_in"][: 3 * WIDTH, :] += dot_nt(r["triple_low"][...], r["entry_one"][...])

    def out_sum():
        r["acc_in"][3 * WIDTH :, :] += dot_nt(r["branch_low"][...], r["mixed"][...])

    def norm_one_back():
        r["token_grad"][...] = (
            r["middle_grad"][...]
            + unit_back(
                r["grad_one"][...], r["unit_one"][...], r["inverse_one"][0:1, :], vec(GAIN_ONE)
            )
        ).astype(bf)

    def vector_sum():
        one, two = r["grad_one"][...], r["grad_two"][...]
        for place, term in enumerate(
            (one * r["unit_one"][...], one, two * r["unit_two"][...], two, r["up"][...])
        ):
            r["d_vec"][WIDTH * place : WIDTH * place + WIDTH, :] += fold(term)

    tasks = [(80, hidden_back(s, part)) for s in range(SUBS) for part in range(2)]
    tasks = tasks + [(130, expand_back(s)) for s in range(SUBS)]
    tasks = tasks + [(200, norm_two_back), (100, out_back)]
    sums = [(130, expand_sum(part)) for part in range(2)]
    sums = sums + [(130, contract_sum(part)) for part in range(2)]
    tasks = tasks + weave([(130, attend(t)) for t in range(len(slots) + 1)], sums)
    tasks = tasks + [(110, entry_back(s)) for s in range(SUBS)]
    tasks = tasks + [(200, in_sum), (200, norm_one_back), (70, out_sum), (200, vector_sum)]
    tasks = tasks + [(70, put(s)) for s in range(SUBS)]
    return tasks


def block_kernel(*refs):
    names = (
        ["vox", "cot", "f_in", "f_out", "f_exp", "f_con", "bias", "vectors", "related"]
        + ["take", "give", "pick", "fill", "out_res", "out_tok", "out_total"]
        + list(WEIGHTS)
        + list(ONCE)
        + [name + "_0" for name in BOTH]
        + [name + "_1" for name in BOTH]
        + ["bucket", "landed", "partial_sum", "landed_two", "total"]
        + ["own", "halo_d", "halo_w", "send_w", "back_send", "back_recv", "grid_res", "grid_tok"]
        + ["own_sem", "d_send", "d_recv", "w_send", "w_recv", "b_send", "b_recv"]
        + ["o_sem", "r_send", "r_recv"]
        + ["s1_send", "s1_recv", "s2_send", "s2_recv", "s3_send", "s3_recv", "s4_send", "s4_recv"]
    )
    r = dict(zip(names, refs))
    states = []
    for parity in range(2):
        state = dict(r)
        for name in BOTH:
            state[name] = r[f"{name}_{parity}"]
        states.append(state)
    crops, _, rows, width = r["vox"].shape
    per_crop = rows // (2 * TOK)
    subs = rows // TOK
    steps = crops * per_crop
    half_rows = rows // 2
    depth, peers_d = lax.axis_index("depth"), lax.axis_size("depth")
    column, peers_w = lax.axis_index("wide"), lax.axis_size("wide")
    d_prev = {"depth": lax.rem(depth + peers_d - 1, peers_d)}
    d_next = {"depth": lax.rem(depth + 1, peers_d)}
    w_prev = {"wide": lax.rem(column + peers_w - 1, peers_w)}
    w_next = {"wide": lax.rem(column + 1, peers_w)}
    mesh_id = pl.DeviceIdType.MESH
    sources = (r["vox"], r["cot"])
    results = (r["out_res"], r["out_tok"])
    grids = (r["grid_res"], r["grid_tok"])
    own, halo_d, halo_w = r["own"], r["halo_d"], r["halo_w"]

    def own_copy(c, a):
        slot = lax.rem(c, SLOTS)
        return pltpu.make_async_copy(
            sources[a].at[c, pl.ds(SHIFT, 2)], own.at[slot, a], r["own_sem"].at[slot, a]
        )

    def depth_copy(c, a):
        return pltpu.make_async_remote_copy(
            src_ref=sources[a].at[c, pl.ds(0, SHIFT)],
            dst_ref=halo_d.at[c, a],
            send_sem=r["d_send"].at[c, a],
            recv_sem=r["d_recv"].at[c, a],
            device_id=d_prev,
            device_id_type=mesh_id,
        )

    def wide_copy(c, half):
        return pltpu.make_async_remote_copy(
            src_ref=r["send_w"].at[lax.rem(c, SLOTS), half],
            dst_ref=halo_w.at[c, half],
            send_sem=r["w_send"].at[c, half],
            recv_sem=r["w_recv"].at[c, half],
            device_id=w_prev,
            device_id_type=mesh_id,
        )

    def back_copy(c, half):
        return pltpu.make_async_remote_copy(
            src_ref=r["back_send"].at[lax.rem(c, SLOTS), half],
            dst_ref=r["back_recv"].at[c, half],
            send_sem=r["b_send"].at[c, half],
            recv_sem=r["b_recv"].at[c, half],
            device_id=w_next,
            device_id_type=mesh_id,
        )

    def keep_copy(c, a):
        slot = lax.rem(c, SLOTS)
        return pltpu.make_async_copy(
            grids[a].at[slot, pl.ds(0, 2)],
            results[a].at[c, pl.ds(SHIFT, 2)],
            r["o_sem"].at[slot, a],
        )

    def return_copy(c, a):
        slot = lax.rem(c, SLOTS)
        return pltpu.make_async_remote_copy(
            src_ref=grids[a].at[slot, pl.ds(2, 2)],
            dst_ref=results[a].at[c, pl.ds(0, SHIFT)],
            send_sem=r["r_send"].at[slot, a],
            recv_sem=r["r_recv"].at[c, a],
            device_id=d_next,
            device_id_type=mesh_id,
        )

    crew = lax.axis_size("dp") * peers_d
    place = lax.axis_index("dp") * peers_d + depth

    def mate(step):
        other = lax.rem(place + step, crew)
        return other, {"dp": other // peers_d, "depth": lax.rem(other, peers_d)}

    def across(step):
        other = lax.rem(column + step, peers_w)
        return other, {"wide": other}

    barrier = pltpu.get_barrier_semaphore()
    for step in range(1, crew):
        pl.semaphore_signal(barrier, inc=1, device_id=mate(step)[1], device_id_type=mesh_id)
    for step in range(1, peers_w):
        pl.semaphore_signal(barrier, inc=1, device_id=across(step)[1], device_id_type=mesh_id)
    pl.semaphore_wait(barrier, crew + peers_w - 2)

    for c in range(2):
        for a in range(2):
            own_copy(c, a).start()

    def send_depth(c, carry):
        for a in range(2):
            depth_copy(c, a).start()
        return carry

    lax.fori_loop(0, crops, send_depth, 0)

    for name in ("acc_in", "acc_exp", "acc_con", "d_vec", "d_tab"):
        r[name][...] = jnp.zeros_like(r[name])
    for parity in range(2):
        for name in ("entry_one", "entry_two", "mixed"):
            states[parity][name][WIDTH:, :] = jnp.ones((16, SPAN), bf)
    r["back_recv"][crops] = jnp.zeros(r["back_recv"].shape[1:], bf)
    for name in ("w_in_t", "w_out_t", "w_exp_t"):
        shape = r[name].shape
        r[name][:, WIDTH:] = jnp.zeros((shape[0], 16), bf)
    r["w_in"][...] = r["f_in"][...].astype(bf)
    r["w_in_t"][:, :WIDTH] = r["f_in"][...].T.astype(bf)
    r["w_out"][...] = r["f_out"][...].astype(bf)
    r["w_out_t"][:, :WIDTH] = r["f_out"][...].T.astype(bf)
    r["w_exp"][...] = (r["f_exp"][...].astype(bf).astype(fl) * 0.5).astype(bf)
    r["w_exp_t"][:, :WIDTH] = r["f_exp"][...].T.astype(bf)
    r["w_con_t"][...] = (r["f_con"][...].astype(bf).astype(fl) * 0.5).astype(bf)
    r["w_con"][...] = r["f_con"][...].T.astype(bf)
    lane16 = lax.broadcasted_iota(jnp.int32, (64, 16), 1)
    for tile in range(r["vectors"].shape[0]):
        spread = jnp.broadcast_to(r["vectors"][tile : tile + 1, :], (128, 128)).T
        for part in range(2):
            chunk = spread[64 * part : 64 * part + 64]
            member, at = divmod(128 * tile + 64 * part, WIDTH)
            narrow = chunk[:, :16]
            high = narrow.astype(bf).astype(fl)
            middle = (narrow - high).astype(bf).astype(fl)
            column_parts = jnp.where(
                lane16 == 0,
                high,
                jnp.where(
                    lane16 == 1, middle, jnp.where(lane16 == 2, narrow - high - middle, 0.0)
                ),
            ).astype(bf)
            if member in (0, 1, 5, 6, 7):
                base = {0: GAIN_ONE, 1: SHIFT_ONE, 5: GAIN_TWO, 6: SHIFT_TWO, 7: CON_BIAS}[member]
                r["vec"][base + at : base + at + 64, :] = chunk
            elif member == 2:
                r["w_in_t"][at : at + 64, WIDTH:] = column_parts
            elif member == 3:
                r["w_in_t"][2 * WIDTH + at : 2 * WIDTH + at + 64, WIDTH:] = column_parts
            elif member == 4:
                r["w_out_t"][at : at + 64, WIDTH:] = column_parts
            else:
                base = WIDTH * (member - 8)
                r["w_exp_t"][base + at : base + at + 64, WIDTH:] = column_parts

    related = r["related"]

    def chooser(places):
        return (
            lax.broadcasted_iota(jnp.int32, (384, 128), 0)
            == jnp.broadcast_to(places, (384, 128))
        ).astype(bf)

    def eight(block):
        return pl.ds(pl.multiple_of(8 * block, 8), 8)

    def thirds(v):
        high = v.astype(bf)
        rest = v - high.astype(fl)
        middle = rest.astype(bf)
        return jnp.concatenate([high, middle, (rest - middle.astype(fl)).astype(bf)], axis=0)

    def ends(v):
        return v[:8] + v[8:16] + v[16:24]

    def code(at, window, edge):
        last_d = (depth == peers_d - 1).astype(jnp.int32)
        last_w = (column == peers_w - 1).astype(jnp.int32)
        d, h, w = at // 16, lax.rem(at // 4, 4), lax.rem(at, 4)
        return (
            last_d * (d >= SHIFT).astype(jnp.int32) * 4
            + edge * (h >= SHIFT).astype(jnp.int32) * 2
            + last_w * window * (w >= SHIFT).astype(jnp.int32)
        )

    bias_parts = thirds(r["bias"][...])

    def table_rows(block, carry):
        near = related[eight(block), :]
        found = [ends(dot(bias_parts, chooser(near[k : k + 1]))) for k in range(8)]
        lane = lax.broadcasted_iota(jnp.int32, (8, 128), 1)
        j = lax.broadcasted_iota(jnp.int32, (8, 128), 0) + 8 * block
        window, i = lane // TOK, lax.rem(lane, TOK)
        for edge in range(2):
            differ = code(i, window, edge) != code(j, window, edge)
            mask = jnp.where(differ, mask_fill, 0.0)
            for head in range(HEADS):
                values = jnp.concatenate([row[head : head + 1, :] for row in found], axis=0)
                r["table"][edge, eight(block), 128 * head : 128 * head + 128] = (
                    values + mask
                ) * LOG2E
        return carry

    lax.fori_loop(0, TOK // 8, table_rows, 0)
    first_half = lax.broadcasted_iota(jnp.int32, (TOK, 128), 1) < TOK

    def starts(b):
        first = pl.multiple_of(b * TOK + 16, 16)
        second = pl.multiple_of(lax.rem(b * TOK + TOK, rows), 16)
        return first, second

    def natural(c, a, b):
        first, second = starts(b)
        slot = lax.rem(c, SLOTS)
        parts = []
        for d in range(2):
            parts.append(own[slot, a, d, pl.ds(first, 48), :])
            parts.append(own[slot, a, d, pl.ds(second, 16), :])
        for d in range(2):
            parts.append(halo_d[c, a, d, pl.ds(first, 48), :])
            parts.append(halo_d[c, a, d, pl.ds(second, 16), :])
        return jnp.concatenate(parts, axis=0)

    def edge_rows(b):
        half = b // (subs // 2)
        return half, pl.ds(pl.multiple_of(lax.rem(b, subs // 2) * TOK, TOK), TOK)

    def pack(c, b):
        half, there = edge_rows(b)
        source = jnp.minimum(c, crops - 1)
        r["send_w"][lax.rem(c, SLOTS), half, there, :] = jnp.concatenate(
            [dot(r["pick"][...], natural(source, a, b)) for a in range(2)], axis=1
        ).astype(bf)

    def merge(c, b):
        first, second = starts(b)
        half, there = edge_rows(b)
        slot = lax.rem(c + SLOTS, SLOTS)
        arrived = r["back_recv"][lax.rem(c + crops + 1, crops + 1), half, there, :]
        for a in range(2):
            extra = dot(r["fill"][...], arrived[:, WIDTH * a : WIDTH * a + WIDTH]).astype(bf)
            for d in range(WIN):
                for start, size, at in ((first, 48, 64 * d), (second, 16, 64 * d + 48)):
                    place_rows = pl.ds(start, size)
                    grids[a][slot, d, place_rows, :] = (
                        grids[a][slot, d, place_rows, :] + extra[at : at + size]
                    )

    def put_grid(a, c, b, low):
        first, second = starts(b)
        slot = lax.rem(c, SLOTS)
        placed = low.T
        for d in range(WIN):
            grids[a][slot, d, pl.ds(first, 48), :] = placed[64 * d : 64 * d + 48]
            grids[a][slot, d, pl.ds(second, 16), :] = placed[64 * d + 48 : 64 * d + 64]

    def forward_of(g, state):
        c, u = g // per_crop, lax.rem(g, per_crop)

        def tokens_of(s):
            b = 2 * u + s
            half, there = edge_rows(b)
            edges = halo_w[c, half, there, :].T
            return [
                jnp.concatenate(
                    [natural(c, a, b).T, edges[WIDTH * a : WIDTH * a + WIDTH]], axis=1
                )
                for a in range(2)
            ]

        def put(s):
            def run():
                moved = dot(
                    state["result"][:, LANES * s : LANES * s + LANES], state["give"][...]
                ).astype(bf)
                state["edge_res"][s] = moved[:, LANES:]
                put_grid(0, c, 2 * u + s, moved[:, :LANES])

            return run

        def ready(s):
            return lambda: pack(c + 1, 2 * u + s)

        edge = (u == per_crop - 1).astype(jnp.int32)
        tasks = forward_tasks(state, first_half, tokens_of, edge, put)
        return weave(tasks, [(80, ready(s)) for s in range(SUBS)])

    def backward_of(g, state):
        c, u = g // per_crop, lax.rem(g, per_crop)

        def put(s):
            def run():
                b = 2 * u + s
                moved = dot(
                    state["token_grad"][:, LANES * s : LANES * s + LANES], state["give"][...]
                ).astype(bf)
                put_grid(1, c, b, moved[:, :LANES])
                half, there = edge_rows(b)
                r["back_send"][lax.rem(c, SLOTS), half, there, :] = jnp.concatenate(
                    [state["edge_res"][s], moved[:, LANES:]], axis=0
                ).T

            return run

        def mended(s):
            return lambda: merge(c - 1, 2 * u + s)

        tasks = backward_tasks(state, first_half, put)
        return weave(tasks, [(120, mended(s)) for s in range(SUBS)])

    def before(f, b):
        if f is not None:
            c, u = f // per_crop, lax.rem(f, per_crop)

            @pl.when(u == 0)
            def _():
                wide_copy(c, 0).wait_recv()

                @pl.when(c + 2 < crops)
                def _():
                    for a in range(2):
                        own_copy(c + 2, a).start()

                @pl.when(c + 1 < crops)
                def _():
                    for a in range(2):
                        own_copy(c + 1, a).wait()
                        depth_copy(c + 1, a).wait_recv()

                @pl.when(c >= SLOTS - 1)
                def _():
                    for half in range(2):
                        wide_copy(c + 1 - SLOTS, half).wait_send()

                @pl.when(c >= SLOTS)
                def _():
                    for a in range(2):
                        keep_copy(c - SLOTS, a).wait()
                        return_copy(c - SLOTS, a).wait_send()

            @pl.when(u == per_crop // 2)
            def _():
                wide_copy(c, 1).wait_recv()

        if b is not None:
            c_b, u_b = b // per_crop, lax.rem(b, per_crop)

            @pl.when((u_b == 0) & (c_b >= SLOTS))
            def _():
                for half in range(2):
                    back_copy(c_b - SLOTS, half).wait_send()

            @pl.when((u_b == 0) & (c_b >= 1))
            def _():
                back_copy(c_b - 1, 0).wait_recv()

            @pl.when((u_b == per_crop // 2) & (c_b >= 1))
            def _():
                back_copy(c_b - 1, 1).wait_recv()

    def after(f, b):
        if f is not None:
            c, u = f // per_crop, lax.rem(f, per_crop)

            @pl.when((u == per_crop // 2 - 1) & (c + 1 < crops))
            def _():
                wide_copy(c + 1, 0).start()

            @pl.when((u == per_crop - 1) & (c + 1 < crops))
            def _():
                wide_copy(c + 1, 1).start()

        if b is not None:
            c_b, u_b = b // per_crop, lax.rem(b, per_crop)

            @pl.when(u_b == per_crop // 2 - 1)
            def _():
                back_copy(c_b, 0).start()

            @pl.when(u_b == per_crop - 1)
            def _():
                back_copy(c_b, 1).start()

                @pl.when(c_b >= 1)
                def _():
                    for a in range(2):
                        keep_copy(c_b - 1, a).start()
                        return_copy(c_b - 1, a).start()

    def half_step(f, b, forward_state, backward_state):
        before(f, b)
        ahead = [] if f is None else forward_of(f, forward_state)
        behind = [] if b is None else backward_of(b, backward_state)
        for _, task in weave(behind, ahead):
            task()
        after(f, b)

    for a in range(2):
        own_copy(0, a).wait()
        depth_copy(0, a).wait_recv()
    for half in range(2):

        def first_pack(b, carry):
            pack(0, b)
            return carry

        lax.fori_loop(half * (subs // 2), (half + 1) * (subs // 2), first_pack, 0)
        wide_copy(0, half).start()
    half_step(jnp.int32(0), None, states[0], None)

    def two_steps(i, carry):
        half_step(2 * i + 1, 2 * i, states[1], states[0])
        half_step(2 * i + 2, 2 * i + 1, states[0], states[1])
        return carry

    lax.fori_loop(0, steps // 2 - 1, two_steps, 0)
    half_step(jnp.int32(steps - 1), jnp.int32(steps - 2), states[1], states[0])
    half_step(None, jnp.int32(steps - 1), None, states[1])

    bucket, landed, total, d_row = r["bucket"], r["landed"], r["total"], r["d_row"]
    partial_sum, landed_two = r["partial_sum"], r["landed_two"]
    extra = 18 * width
    for tile in range(12):
        acc, at = ((r["acc_in"], 128 * tile), (r["acc_exp"], 128 * (tile - 6)))[tile // 6]
        turned = acc[at : at + 128, :].T * (1.0, 0.5)[tile // 6]
        bucket[width * tile : width * tile + width, :] = turned[:width].astype(bf)
        d_row[tile : tile + 1, :] = turned[width : width + 1]
    for tile in range(6):
        bucket[width * (12 + tile) : width * (13 + tile), :] = (
            r["acc_con"][128 * tile : 128 * tile + 128, :].T * 0.5
        ).astype(bf)
    for tile in range(8):
        size = min(128, 5 * width - 128 * tile)
        d_row[12 + tile : 13 + tile, :size] = jnp.sum(
            r["d_vec"][128 * tile : 128 * tile + size, :].T, 0, keepdims=True
        )
    d_row[19:20, 64:] = jnp.zeros((1, 64), fl)

    def table_sums(block, carry):
        near = related[eight(block), :]
        held = r["d_tab"][eight(block), :]
        for k in range(8):
            rows_k = jnp.concatenate(
                [held[k : k + 1, 128 * head : 128 * head + 128] for head in range(HEADS)]
                + [jnp.zeros((2, 128), fl)],
                axis=0,
            )
            carry = carry + dot_nt(thirds(rows_k), chooser(near[k : k + 1]))
        return carry

    sums = ends(lax.fori_loop(0, TOK // 8, table_sums, jnp.zeros((24, 384), fl)))
    for tile in range(3):
        d_row[24 + 8 * tile : 32 + 8 * tile, :] = sums[:, 128 * tile : 128 * tile + 128]
    d_row[20:24, :] = jnp.zeros((4, 128), fl)
    bucket[extra : extra + 48, :] = d_row[...].astype(bf)
    length = bucket.shape[0]
    if length > extra + 48:
        bucket[extra + 48 :, :] = jnp.zeros((length - extra - 48, 128), bf)

    share = length // crew
    piece = share // peers_w

    def span(start, size):
        return pl.ds(pl.multiple_of(start, 16), size)

    def first_copy(step):
        other, peer = mate(step)
        return pltpu.make_async_remote_copy(
            src_ref=bucket.at[span(other * share, share)],
            dst_ref=landed.at[step - 1],
            send_sem=r["s1_send"].at[step - 1],
            recv_sem=r["s1_recv"].at[step - 1],
            device_id=peer,
            device_id_type=mesh_id,
        )

    def second_copy(step):
        other, peer = across(step)
        return pltpu.make_async_remote_copy(
            src_ref=partial_sum.at[span(other * piece, piece)],
            dst_ref=landed_two.at[step - 1],
            send_sem=r["s2_send"].at[step - 1],
            recv_sem=r["s2_recv"].at[step - 1],
            device_id=peer,
            device_id_type=mesh_id,
        )

    def third_copy(step):
        rows_mine = total.at[span(place * share + column * piece, piece)]
        return pltpu.make_async_remote_copy(
            src_ref=rows_mine,
            dst_ref=rows_mine,
            send_sem=r["s3_send"].at[step - 1],
            recv_sem=r["s3_recv"].at[step - 1],
            device_id=across(step)[1],
            device_id_type=mesh_id,
        )

    def fourth_copy(step):
        rows_mine = total.at[span(place * share, share)]
        return pltpu.make_async_remote_copy(
            src_ref=rows_mine,
            dst_ref=rows_mine,
            send_sem=r["s4_send"].at[step - 1],
            recv_sem=r["s4_recv"].at[step - 1],
            device_id=mate(step)[1],
            device_id_type=mesh_id,
        )

    def third_arrival(step):
        other = lax.rem(column + peers_w - step, peers_w)
        rows_there = total.at[span(place * share + other * piece, piece)]
        return pltpu.make_async_remote_copy(
            src_ref=rows_there,
            dst_ref=rows_there,
            send_sem=r["s3_send"].at[step - 1],
            recv_sem=r["s3_recv"].at[step - 1],
            device_id=across(step)[1],
            device_id_type=mesh_id,
        )

    def fourth_arrival(step):
        other = lax.rem(place + crew - step, crew)
        rows_there = total.at[span(other * share, share)]
        return pltpu.make_async_remote_copy(
            src_ref=rows_there,
            dst_ref=rows_there,
            send_sem=r["s4_send"].at[step - 1],
            recv_sem=r["s4_recv"].at[step - 1],
            device_id=mate(step)[1],
            device_id_type=mesh_id,
        )

    for step in range(1, crew):
        first_copy(step).start()
    for half in range(2):
        back_copy(crops - 1, half).wait_recv()

        def last_merge(b, carry):
            merge(jnp.int32(crops - 1), b)
            return carry

        lax.fori_loop(half * (subs // 2), (half + 1) * (subs // 2), last_merge, 0)
    for a in range(2):
        keep_copy(crops - 1, a).start()
        return_copy(crops - 1, a).start()
    for step in range(1, crew):
        first_copy(step).wait_recv()
    summed = bucket[span(place * share, share), :].astype(fl)
    for step in range(1, crew):
        summed = summed + landed[step - 1].astype(fl)
    partial_sum[...] = summed.astype(bf)
    for step in range(1, peers_w):
        second_copy(step).start()
    for step in range(1, peers_w):
        second_copy(step).wait_recv()
    summed = partial_sum[span(column * piece, piece), :].astype(fl)
    for step in range(1, peers_w):
        summed = summed + landed_two[step - 1].astype(fl)
    total[span(place * share + column * piece, piece), :] = summed.astype(bf)
    for step in range(1, peers_w):
        third_copy(step).start()
    for step in range(1, peers_w):
        third_arrival(step).wait_recv()
    for step in range(1, crew):
        fourth_copy(step).start()
    for step in range(1, crew):
        fourth_arrival(step).wait_recv()
    r["out_total"][...] = total[...]
    for step in range(1, crew):
        first_copy(step).wait_send()
        fourth_copy(step).wait_send()
    for step in range(1, peers_w):
        second_copy(step).wait_send()
        third_copy(step).wait_send()

    def finish(c, carry):
        for a in range(2):
            depth_copy(c, a).wait_send()
            return_copy(c, a).wait_recv()
        return carry

    lax.fori_loop(0, crops, finish, 0)

    def close(c, carry):
        for a in range(2):
            keep_copy(c, a).wait()
            return_copy(c, a).wait_send()
        for half in range(2):
            back_copy(c, half).wait_send()
        return carry

    lax.fori_loop(crops - SLOTS, crops, close, 0)

    def close_wide(c, carry):
        for half in range(2):
            wide_copy(c, half).wait_send()
        return carry

    lax.fori_loop(crops + 1 - SLOTS, crops, close_wide, 0)


def block_call(voxels, cotangent, matrices, bias_table, vectors):
    crops, planes, rows, width = voxels.shape
    whole = pl.BlockSpec(memory_space=pltpu.VMEM)
    far = pl.BlockSpec(memory_space=pl.ANY)
    related = relative_index().T
    related = jnp.asarray(np.concatenate([related, related], axis=1), jnp.int32)
    consts = list(matrices) + [bias_table, vectors, related] + placement()
    sem = pltpu.SemaphoreType.DMA
    crew = lax.axis_size("dp") * lax.axis_size("depth")
    peers_w = lax.axis_size("wide")
    unit_rows = 16 * crew * peers_w
    length = -(-(18 * width + 48) // unit_rows) * unit_rows
    share = length // crew
    piece = share // peers_w
    return pl.pallas_call(
        block_kernel,
        in_specs=[far, far] + [whole] * len(consts),
        out_specs=[far, far, whole],
        out_shape=[
            jax.ShapeDtypeStruct(voxels.shape, bf),
            jax.ShapeDtypeStruct(voxels.shape, bf),
            jax.ShapeDtypeStruct((length, 128), bf),
        ],
        scratch_shapes=[
            pltpu.VMEM(*spec)
            for spec in list(WEIGHTS.values()) + list(ONCE.values()) + list(BOTH.values()) * 2
        ]
        + [
            pltpu.VMEM((length, 128), bf),
            pltpu.VMEM((crew - 1, share, 128), bf),
            pltpu.VMEM((share, 128), bf),
            pltpu.VMEM((peers_w - 1, piece, 128), bf),
            pltpu.VMEM((length, 128), bf),
            pltpu.VMEM((SLOTS, 2, 2, rows, width), bf),
            pltpu.VMEM((crops, 2, 2, rows, width), bf),
            pltpu.VMEM((crops, 2, rows // 2, 2 * width), bf),
            pltpu.VMEM((SLOTS, 2, rows // 2, 2 * width), bf),
            pltpu.VMEM((SLOTS, 2, rows // 2, 2 * width), bf),
            pltpu.VMEM((crops + 1, 2, rows // 2, 2 * width), bf),
            pltpu.VMEM((SLOTS, 4, rows, width), bf),
            pltpu.VMEM((SLOTS, 4, rows, width), bf),
            sem((SLOTS, 2)),
            sem((crops, 2)),
            sem((crops, 2)),
            sem((crops, 2)),
            sem((crops, 2)),
            sem((crops, 2)),
            sem((crops, 2)),
            sem((SLOTS, 2)),
            sem((SLOTS, 2)),
            sem((crops, 2)),
            sem((crew - 1,)),
            sem((crew - 1,)),
            sem((peers_w - 1,)),
            sem((peers_w - 1,)),
            sem((peers_w - 1,)),
            sem((peers_w - 1,)),
            sem((crew - 1,)),
            sem((crew - 1,)),
        ],
        compiler_params=pltpu.CompilerParams(
            vmem_limit_bytes=60 * 2**20, collective_id=0, has_side_effects=True
        ),
        name="block",
    )(voxels, cotangent, *consts)


def update_kernel(*refs):
    far_in, total, params, far_out, outs, norm_ref, held, in_sem, out_sem = (
        refs[0:2], refs[2], refs[3:21], refs[21:23], refs[23:51], refs[51], refs[52],
        refs[53], refs[54],
    )
    crops = far_in[0].shape[0]

    def fetch(a, c):
        return pltpu.make_async_copy(far_in[a].at[c], held.at[a, c], in_sem.at[a, c])

    def store(a, c):
        return pltpu.make_async_copy(held.at[a, c], far_out[a].at[c], out_sem.at[a, c])

    for a in range(2):
        for c in range(crops):
            fetch(a, c).start()
    for a in range(2):
        for c in range(crops):
            fetch(a, c).wait()
            store(a, c).start()
    width = 192

    def slab(tile):
        return total[width * tile : width * tile + width, :].astype(fl)

    small = total[18 * width : 18 * width + 48, :].astype(fl)
    low_half = slab(4)
    grads = [
        jnp.concatenate([slab(k) for k in range(4)] + [low_half[:, :64]], axis=1),
        jnp.concatenate([low_half[:, 64:], slab(5)], axis=1),
        jnp.concatenate([slab(k) for k in range(6, 12)], axis=1),
        jnp.concatenate([slab(k) for k in range(12, 18)], axis=1),
    ]
    flat_bias = jnp.concatenate([small[k : k + 1] for k in range(12)], axis=1)
    flat_sum = jnp.concatenate([small[k : k + 1] for k in range(12, 20)], axis=1)

    def cut(flat, index):
        return flat[:, width * index : width * index + width]

    table = jnp.concatenate([small[24:32], small[32:40], small[40:48]], axis=1)
    grads.append(table[:HEADS, : params[4].shape[1]])
    grads.append(
        jnp.concatenate(
            [
                cut(flat_sum, 0), cut(flat_sum, 1), cut(flat_bias, 0), cut(flat_bias, 2),
                cut(flat_bias, 3), cut(flat_sum, 2), cut(flat_sum, 3), cut(flat_sum, 4),
                flat_bias[:, 4 * width : 8 * width],
            ],
            axis=1,
        )
    )
    squares = jnp.zeros((1, 1), fl)
    for grad in grads:
        squares = squares + jnp.sum(
            jnp.sum(grad * grad, 0, keepdims=True), 1, keepdims=True
        )
    norm_value = jnp.sqrt(squares)
    norm_ref[...] = norm_value
    factor = jnp.minimum(1.0, clip_bound / (norm_value + 1e-06))
    for member in range(6):
        matrix = member < 4
        clipped = grads[member] * factor
        first, second, fresh = adam_update(
            params[member][...],
            params[6 + member][...],
            params[12 + member][...],
            clipped,
            rate_matrix if matrix else rate_vector,
            weight_decay if matrix else 0.0,
        )
        for place, value in enumerate((clipped, first, second, fresh)):
            outs[4 * member + place][...] = value
        if matrix:
            outs[24 + member][...] = fresh.astype(bf)
    for a in range(2):
        for c in range(crops):
            store(a, c).wait()


def update_call(result, token_grad, total, params):
    whole = pl.BlockSpec(memory_space=pltpu.VMEM)
    far = pl.BlockSpec(memory_space=pl.ANY)
    shapes = []
    for member in range(6):
        shapes = shapes + [jax.ShapeDtypeStruct(params[member].shape, fl)] * 4
    for member in range(4):
        shapes.append(jax.ShapeDtypeStruct(params[member].shape, bf))
    shapes.append(jax.ShapeDtypeStruct((1, 1), fl))
    big = jax.ShapeDtypeStruct(result.shape, bf)
    return pl.pallas_call(
        update_kernel,
        in_specs=[far, far, whole] + [whole] * 18,
        out_specs=[far, far] + [whole] * 29,
        out_shape=[big, big] + shapes,
        scratch_shapes=[
            pltpu.VMEM((2,) + result.shape, bf),
            pltpu.SemaphoreType.DMA((2, result.shape[0])),
            pltpu.SemaphoreType.DMA((2, result.shape[0])),
        ],
        compiler_params=pltpu.CompilerParams(vmem_limit_bytes=56 * 2**20),
        name="update",
    )(result, token_grad, total, *params)


def local(
    voxels,
    cotangent,
    project_in,
    project_out,
    expand,
    contract,
    bias_table,
    vectors,
    project_in_first,
    project_out_first,
    expand_first,
    contract_first,
    bias_table_first,
    vectors_first,
    project_in_second,
    project_out_second,
    expand_second,
    contract_second,
    bias_table_second,
    vectors_second,
):
    batches, planes, height, breadth, width = voxels.shape
    flat = (batches, planes, height * breadth, width)
    result, token_grad, total = block_call(
        voxels.reshape(flat),
        cotangent.reshape(flat),
        (project_in, project_out, expand, contract.T),
        jnp.pad(bias_table, ((0, 2), (0, 384 - bias_table.shape[1]))),
        vectors.reshape(-1, 128),
    )
    params = [
        project_in,
        project_out,
        expand,
        contract.T,
        bias_table,
        vectors.reshape(1, -1),
        project_in_first,
        project_out_first,
        expand_first,
        contract_first.T,
        bias_table_first,
        vectors_first.reshape(1, -1),
        project_in_second,
        project_out_second,
        expand_second,
        contract_second.T,
        bias_table_second,
        vectors_second.reshape(1, -1),
    ]
    done = update_call(result, token_grad, total, params)
    outs = list(done[2:30])
    for place in range(20, 24):
        outs[place] = outs[place].reshape(-1)
    for place in (12, 13, 14, 15, 27):
        outs[place] = outs[place].T
    return (
        (done[0].reshape(voxels.shape), done[1].reshape(voxels.shape))
        + tuple(outs)
        + (done[30].reshape(()),)
    )


def solution(mesh):
    split = P("dp", "depth", None, "wide", None)
    return jax.shard_map(
        local,
        mesh=mesh,
        in_specs=(split,) * 2 + (P(),) * 18,
        out_specs=(split,) * 2 + (P(),) * 29,
        check_vma=False,
    )
```

```python
from types import SimpleNamespace

import jax
import jax.numpy as jnp
import numpy as np
from jax import lax
from jax.experimental import pallas as pl
from jax.experimental.pallas import tpu as pltpu
from jax.sharding import PartitionSpec as P

HEADS = 6
WIN = 4
SHIFT = 2
STEP = 10
TOK = WIN**3
GROUP = 4
LANES = GROUP * TOK

norm_eps = 1e-05
mask_fill = -100.0
clip_bound = 1000.0
rate_matrix = 0.1
rate_vector = 0.6
weight_decay = 0.01
beta_first = 0.9
beta_second = 0.999
adam_eps = 1e-08
LOG2E = 1.4426950408889634
INV_SQRT2 = 0.7071067811865476
INV_SQRT2PI = 0.3989422804014327


def relative_index():
    extent = 2 * WIN - 1
    corner = np.arange(WIN)
    places = np.stack(np.meshgrid(corner, corner, corner, indexing="ij"), -1).reshape(-1, 3)
    offsets = places[:, None, :] - places[None, :, :] + WIN - 1
    return (offsets[..., 0] * extent + offsets[..., 1]) * extent + offsets[..., 2]


def adam_update(weight, first, second, gradient, rate, decay):
    first_new = beta_first * first + (1.0 - beta_first) * gradient
    second_new = beta_second * second + (1.0 - beta_second) * gradient * gradient
    first_hat = first_new / (1.0 - beta_first**STEP)
    second_hat = second_new / (1.0 - beta_second**STEP)
    weight_new = weight - rate * (first_hat / (jnp.sqrt(second_hat) + adam_eps) + decay * weight)
    return (first_new, second_new, weight_new)


fl = jnp.float32
bf = jnp.bfloat16


def dot(a, b):
    return jnp.dot(a, b, preferred_element_type=fl)


def dot_nt(a, b):
    return lax.dot_general(a, b, (((1,), (1,)), ((), ())), preferred_element_type=fl)


def wide(v, lanes):
    return jnp.concatenate([v] * (lanes // v.shape[1]), axis=1)


def unit_norm(v):
    width = v.shape[0]
    mean = jnp.sum(v, 0, keepdims=True) * (1.0 / width)
    centred = v - mean
    inverse = lax.rsqrt(jnp.sum(centred * centred, 0, keepdims=True) * (1.0 / width) + norm_eps)
    return centred * inverse, inverse


def unit_back(grad, unit, inverse, gain):
    width = grad.shape[0]
    scaled = grad * gain
    inner = jnp.sum(scaled, 0, keepdims=True) * (1.0 / width)
    along = jnp.sum(scaled * unit, 0, keepdims=True) * (1.0 / width)
    return inverse * (scaled - inner - unit * along)


def fold(v):
    total = v[:, :128]
    for lane in range(128, v.shape[1], 128):
        total = total + v[:, lane : lane + 128]
    return total


def two_windows(compact, first_half):
    zero = jnp.zeros_like(compact)
    return jnp.concatenate(
        [jnp.where(first_half, compact, zero), jnp.where(first_half, zero, compact)], axis=0
    )


def two_heads(ref, head_pair, lanes):
    at = 64 * head_pair
    zero = jnp.zeros((32, 128), bf)
    return jnp.concatenate(
        [
            jnp.concatenate([ref[at : at + 32, lanes], zero], axis=1),
            jnp.concatenate([zero, ref[at + 32 : at + 64, lanes]], axis=1),
        ],
        axis=0,
    )


def cross(token_major, low, first, head_pair, first_half):
    right = two_heads(low, head_pair, slice(first, first + 128))
    if head_pair == 1:
        right = jnp.concatenate([jnp.zeros((64, 256), bf), right], axis=0)
        left = token_major[first : first + 128, 0:128]
    else:
        at = 64 * head_pair
        left = token_major[first : first + 128, at : at + 64]
    full = dot(left, right)
    out = []
    for head in range(2):
        block = full[:, 128 * head : 128 * head + 128]
        out.append(jnp.where(first_half, block[:TOK], block[TOK:]))
    return out


def weave(one, other):
    whole_one = sum(weight for weight, _ in one) + 1e-9
    whole_other = sum(weight for weight, _ in other) + 1e-9
    merged, done_one, done_other = [], 0.0, 0.0
    one, other = list(one), list(other)
    while one or other:
        if not other or (
            one
            and (done_one + one[0][0] / 2) / whole_one
            <= (done_other + other[0][0] / 2) / whole_other
        ):
            merged.append(one.pop(0))
            done_one += merged[-1][0]
        else:
            merged.append(other.pop(0))
            done_other += merged[-1][0]
    return merged


def placement():
    take = np.zeros((LANES + TOK, LANES), np.float32)
    pick = np.zeros((TOK, LANES), np.float32)
    for hw in range(2):
        for ww in range(2):
            for d in range(WIN):
                for hh in range(WIN):
                    for wl in range(WIN):
                        t = ((hw * 2 + ww) * WIN + d) * 16 + hh * 4 + wl
                        h, w = 4 * hw + hh, 4 * ww + wl
                        if w < 2 * WIN - SHIFT:
                            row = d * 64 + h * 8 + w + SHIFT
                        else:
                            row = LANES + d * 16 + h * 2 + w - (2 * WIN - SHIFT)
                        take[row, t] = 1.0
    for d in range(WIN):
        for h in range(2 * WIN):
            for w in range(SHIFT):
                pick[d * 16 + h * 2 + w, d * 64 + h * 8 + w] = 1.0
    pick = pick[:32, :128]
    return [jnp.asarray(m, bf) for m in (take, take.T, pick, pick.T)]


WIDTH = 192
HID = 4 * WIDTH
SPAN = 2 * LANES
PAIRS = SPAN // 128
SUBS = SPAN // LANES
SLOTS = 3
DEPTH_SLOTS = 5
RETURN_SLOTS = 3
MERGE_LAG = 5
UNPACK_LAG = 9
BOTH = dict(
    up=((WIDTH, SPAN), fl),
    up_low=((WIDTH, SPAN), bf),
    unit_one=((WIDTH, SPAN), fl),
    inverse_one=((8, SPAN), fl),
    entry_one=((WIDTH + 16, SPAN), bf),
    query=((WIDTH, SPAN), bf),
    keys=((WIDTH, SPAN), bf),
    values=((WIDTH, SPAN), bf),
    values_t=((SPAN, WIDTH), bf),
    probs=((PAIRS, HEADS, TOK, 128), fl),
    probs_low=((PAIRS, HEADS, TOK, 128), bf),
    mixed=((WIDTH + 16, SPAN), bf),
    unit_two=((WIDTH, SPAN), fl),
    inverse_two=((8, SPAN), fl),
    entry_two=((WIDTH + 16, SPAN), bf),
    slope=((HID, SPAN), fl),
    active=((HID, SPAN), bf),
    edge_res=((SUBS, WIDTH, 3 * TOK), bf),
)
ONCE = dict(
    x=((WIDTH, SPAN), fl),
    keys_t=((SPAN, WIDTH), bf),
    result=((WIDTH, SPAN), bf),
    hidden_low=((HID, SPAN), bf),
    grad_two=((WIDTH, SPAN), fl),
    middle_grad=((WIDTH, SPAN), fl),
    branch_low=((WIDTH, SPAN), bf),
    mixed_low=((WIDTH, SPAN), bf),
    triple_low=((3 * WIDTH, SPAN), bf),
    grad_one=((WIDTH, SPAN), fl),
    token_grad=((WIDTH, SPAN), bf),
)
WEIGHTS = dict(
    table=((2, TOK, HEADS * 128), fl),
    vec=((5 * WIDTH, 128), fl),
    w_in_t=((3 * WIDTH, WIDTH + 16), bf),
    w_in=((WIDTH, 3 * WIDTH), bf),
    w_out_t=((WIDTH, WIDTH + 16), bf),
    w_out=((WIDTH, WIDTH), bf),
    w_exp_t=((HID, WIDTH + 16), bf),
    w_exp=((WIDTH, HID), bf),
    w_con=((HID, WIDTH), bf),
    w_con_t=((WIDTH, HID), bf),
    acc_in=((4 * WIDTH, WIDTH + 16), fl),
    acc_exp=((HID, WIDTH + 16), fl),
    acc_con=((HID, WIDTH), fl),
    d_vec=((5 * WIDTH, 128), fl),
    d_tab=((TOK, HEADS * 128), fl),
    d_row=((48, 128), fl),
    bias_pad=((8, 384), fl),
)
GAIN_ONE, SHIFT_ONE, GAIN_TWO, SHIFT_TWO, CON_BIAS = (WIDTH * k for k in range(5))
ENDS = dict(
    vox=0, cot=0, f_in=0, f_out=0, f_exp=0, f_con=0, bias=0, vectors=0, related=0,
    take=0, give=0, pick=0, fill=0, out_res=0, out_tok=0, out_total=0,
)
SIGNALS = dict(
    own_sem=0, raw_sem=0, d_send=0, d_recv=0, w_send=0, w_recv=0, b_send=0, b_recv=0,
    o_sem=0, q_sem=0, r_send=0, r_recv=0, d_free=0, r_free=0, s1_send=0, s1_recv=0, s2_send=0, s2_recv=0,
    s3_send=0, s3_recv=0, s4_send=0, s4_recv=0, s0_send=0, s0_recv=0, s5_send=0, s5_recv=0,
    t_sem=0,
)
scale = 32 ** (-0.5)


def moves(crops, rows, length, share, peers_w):
    half = length // 2
    crew = half // share
    piece = share // peers_w
    part = 2 * TOK
    parts = rows // part
    return dict(
        bucket=((length, 128), bf),
        landed_zero=((half, 128), bf),
        half_sum=((half, 128), bf),
        landed=((crew - 1, share, 128), bf),
        partial_sum=((share, 128), bf),
        landed_two=((peers_w - 1, piece, 128), bf),
        total=((length, 128), bf),
        own=((SLOTS, 2, 2, rows, WIDTH), bf),
        raw=((2, 2, 2, rows, WIDTH), bf),
        send_d=((SLOTS, parts, 2, part, 2 * WIDTH), bf),
        halo_d=((DEPTH_SLOTS, parts, 2, part, 2 * WIDTH), bf),
        halo_w=((crops, parts, part, 2 * WIDTH), bf),
        send_w=((SLOTS, parts, part, 2 * WIDTH), bf),
        back_send=((SLOTS, parts, part, 2 * WIDTH), bf),
        back_recv=((crops + 1, parts, part, 2 * WIDTH), bf),
        keep_res=((SLOTS, 2, rows, WIDTH), bf),
        keep_tok=((SLOTS, 2, rows, WIDTH), bf),
        grid_ret=((SLOTS, parts, 2, part, 2 * WIDTH), bf),
        ret_recv=((RETURN_SLOTS + 1, parts, 2, part, 2 * WIDTH), bf),
        stage=((2, 2, 2, rows, WIDTH), bf),
    )


MOVES = moves(1, 2 * TOK, 32, 16, 1)


def forward_tasks(r, first_half, tokens_of, edge):
    tasks = []
    slots = [(k, hp) for k in range(PAIRS) for hp in range(3)]
    held = {}

    def vec(at, lanes=SPAN):
        return wide(r.vec[at : at + WIDTH, :], lanes)

    def fetch():
        rows = []
        for s in range(SUBS):
            rows = rows + tokens_of(s)
        moved = dot(jnp.concatenate(rows, axis=0), r.take[...])
        for s in range(SUBS):
            lanes = slice(LANES * s, LANES * s + LANES)
            at = 2 * WIDTH * s
            up = moved[at + WIDTH : at + 2 * WIDTH]
            r.x[:, lanes] = moved[at : at + WIDTH]
            r.up[:, lanes] = up
            r.up_low[:, lanes] = up.astype(bf)

    def norm_one():
        unit_vals, inverse = unit_norm(r.x[...])
        r.unit_one[...] = unit_vals
        r.inverse_one[...] = jnp.broadcast_to(inverse, (8, SPAN))
        r.entry_one[:WIDTH] = (unit_vals * vec(GAIN_ONE) + vec(SHIFT_ONE)).astype(bf)

    def project():
        triple = dot(r.w_in_t[...], r.entry_one[...]).astype(bf)
        r.query[...] = triple[:WIDTH]
        r.keys[...] = triple[WIDTH : 2 * WIDTH]
        r.values[...] = triple[2 * WIDTH :]

    def turn():
        r.keys_t[...] = r.keys[...].T
        r.values_t[...] = r.values[...].T

    def scores(t):
        k, hp = slots[t]
        held["s", t] = cross(r.keys_t, r.query, 128 * k, hp, first_half)

    def soft(t):
        k, hp = slots[t]
        pieces = held.pop(("s", t))
        wides = []
        for head in (2 * hp, 2 * hp + 1):
            which = edge if k == PAIRS - 1 else 0
            s = (
                pieces[head - 2 * hp] * (scale * LOG2E)
                + r.table[which, :, 128 * head : 128 * head + 128]
            )
            e = jnp.exp2(s - jnp.max(s, 0, keepdims=True))
            p = e * (1.0 / jnp.sum(e, 0, keepdims=True))
            r.probs[k, head] = p
            p_low = p.astype(bf)
            r.probs_low[k, head] = p_low
            wides.append(two_windows(p_low, first_half))
        held["p", t] = wides

    def mix(t):
        k, hp = slots[t]
        lanes = slice(128 * k, 128 * k + 128)
        r.mixed[64 * hp : 64 * hp + 64, lanes] = dot(
            two_heads(r.values, hp, lanes), jnp.concatenate(held.pop(("p", t)), axis=0)
        ).astype(bf)

    def join():
        r.x[...] = r.x[...] + dot(r.w_out_t[...], r.mixed[...])

    def norm_two():
        unit_vals, inverse = unit_norm(r.x[...])
        r.unit_two[...] = unit_vals
        r.inverse_two[...] = jnp.broadcast_to(inverse, (8, SPAN))
        r.entry_two[:WIDTH] = (unit_vals * vec(GAIN_TWO) + vec(SHIFT_TWO)).astype(bf)

    def gelu(s, part):
        def run():
            lanes = slice(LANES * s, LANES * s + LANES)
            rows = slice(HID // 2 * part, HID // 2 * part + HID // 2)
            hidden = dot(r.w_exp_t[rows], r.entry_two[:, lanes])
            twice = 1.0 + lax.erf(hidden * INV_SQRT2)
            r.active[rows, lanes] = (hidden * twice).astype(bf)
            r.slope[rows, lanes] = twice + hidden * (
                (2.0 * INV_SQRT2PI) * jnp.exp2(hidden * hidden * (-0.5 * LOG2E))
            )

        return run

    def contracted(s):
        def run():
            lanes = slice(LANES * s, LANES * s + LANES)
            r.result[:, lanes] = (
                r.x[:, lanes]
                + dot(r.w_con_t[...], r.active[:, lanes])
                + vec(CON_BIAS, LANES)
            ).astype(bf)

        return run

    tasks = tasks + [(340, fetch), (120, norm_one), (180, project), (80, turn)]
    for t in range(len(slots) + 1):
        if t == 0:
            tasks.append((30, lambda: scores(0)))
        if t + 1 < len(slots):
            tasks.append((30, lambda t=t: scores(t + 1)))
        if t < len(slots):
            tasks.append((40, lambda t=t: soft(t)))
        if t >= 1:
            tasks.append((30, lambda t=t: mix(t - 1)))

    tasks = tasks + [(100, join), (150, norm_two)]
    tasks = tasks + [(270, gelu(s, part)) for s in range(SUBS) for part in range(2)]
    tasks = tasks + [(130, contracted(s)) for s in range(SUBS)]
    return tasks


def backward_tasks(r, first_half):
    slots = [(k, hp) for k in range(PAIRS) for hp in range(3)]
    held = {}

    def vec(at):
        return wide(r.vec[at : at + WIDTH, :], SPAN)

    def hidden_back(s, part):
        def run():
            lanes = slice(LANES * s, LANES * s + LANES)
            rows = slice(HID // 2 * part, HID // 2 * part + HID // 2)
            r.hidden_low[rows, lanes] = (
                dot(r.w_con[rows], r.up_low[:, lanes]) * r.slope[rows, lanes]
            ).astype(bf)

        return run

    def expand_back(s):
        def run():
            lanes = slice(LANES * s, LANES * s + LANES)
            r.grad_two[:, lanes] = dot(r.w_exp[...], r.hidden_low[:, lanes])

        return run

    def norm_two_back():
        grad = r.up[...] + unit_back(
            r.grad_two[...], r.unit_two[...], r.inverse_two[0:1, :], vec(GAIN_TWO)
        )
        r.middle_grad[...] = grad
        r.branch_low[...] = grad.astype(bf)

    def out_back():
        r.mixed_low[...] = dot(r.w_out[...], r.branch_low[...]).astype(bf)

    def expand_sum(part):
        def run():
            rows = slice(HID // 2 * part, HID // 2 * part + HID // 2)
            r.acc_exp[rows, :] += dot_nt(r.hidden_low[rows, :], r.entry_two[...])

        return run

    def contract_sum(part):
        def run():
            rows = slice(HID // 2 * part, HID // 2 * part + HID // 2)
            r.acc_con[rows, :] += dot_nt(r.active[rows, :], r.up_low[...])

        return run

    def prob_back(t):
        k, hp = slots[t]
        held["g", t] = cross(r.values_t, r.mixed_low, 128 * k, hp, first_half)

    def score_back(t):
        k, hp = slots[t]
        pieces = held.pop(("g", t))
        wides = []
        for head in (2 * hp, 2 * hp + 1):
            p, g = r.probs[k, head], pieces[head - 2 * hp]
            s = p * (g - jnp.sum(g * p, 0, keepdims=True))
            r.d_tab[:, 128 * head : 128 * head + 128] += s
            wides.append(two_windows(s.astype(bf), first_half))
        held["s", t] = wides

    def query_back(t):
        k, hp = slots[t]
        lanes = slice(128 * k, 128 * k + 128)
        at = 64 * hp
        r.triple_low[at : at + 64, lanes] = (
            dot(two_heads(r.keys, hp, lanes), jnp.concatenate(held["s", t], axis=0)) * scale
        ).astype(bf)

    def keys_back(t):
        k, hp = slots[t]
        lanes = slice(128 * k, 128 * k + 128)
        at = WIDTH + 64 * hp
        wides = held.pop(("s", t))
        r.triple_low[at : at + 64, lanes] = (
            dot_nt(two_heads(r.query, hp, lanes), jnp.concatenate(wides, axis=1)) * scale
        ).astype(bf)

    def values_back(t):
        k, hp = slots[t]
        lanes = slice(128 * k, 128 * k + 128)
        at = 2 * WIDTH + 64 * hp
        probs = jnp.concatenate(
            [two_windows(r.probs_low[k, head], first_half) for head in (2 * hp, 2 * hp + 1)], axis=1
        )
        r.triple_low[at : at + 64, lanes] = dot_nt(
            two_heads(r.mixed_low, hp, lanes), probs
        ).astype(bf)

    def entry_back(s):
        def run():
            lanes = slice(LANES * s, LANES * s + LANES)
            r.grad_one[:, lanes] = dot(r.w_in[...], r.triple_low[:, lanes])

        return run

    def in_sum():
        r.acc_in[: 3 * WIDTH, :] += dot_nt(r.triple_low[...], r.entry_one[...])

    def out_sum():
        r.acc_in[3 * WIDTH :, :] += dot_nt(r.branch_low[...], r.mixed[...])

    def norm_one_back():
        r.token_grad[...] = (
            r.middle_grad[...]
            + unit_back(
                r.grad_one[...], r.unit_one[...], r.inverse_one[0:1, :], vec(GAIN_ONE)
            )
        ).astype(bf)

    def vector_sum():
        one, two = r.grad_one[...], r.grad_two[...]
        for place, term in enumerate(
            (one * r.unit_one[...], one, two * r.unit_two[...], two, r.up[...])
        ):
            r.d_vec[WIDTH * place : WIDTH * place + WIDTH, :] += fold(term)

    tasks = [(80, hidden_back(s, part)) for s in range(SUBS) for part in range(2)]
    tasks = tasks + [(130, expand_back(s)) for s in range(SUBS)]
    tasks = tasks + [(200, norm_two_back), (100, out_back)]
    sums = [(130, expand_sum(part)) for part in range(2)]
    sums = sums + [(130, contract_sum(part)) for part in range(2)]
    fine = []
    for t in range(len(slots) + 1):
        if t == 0:
            fine.append((30, lambda: prob_back(0)))
        if t + 1 < len(slots):
            fine.append((30, lambda t=t: prob_back(t + 1)))
        if t < len(slots):
            fine.append((20, lambda t=t: values_back(t)))
            fine.append((40, lambda t=t: score_back(t)))
        if t >= 1:
            fine.append((20, lambda t=t: query_back(t - 1)))
            fine.append((20, lambda t=t: keys_back(t - 1)))
    tasks = tasks + weave(fine, sums)
    tasks = tasks + [(110, entry_back(s)) for s in range(SUBS)]
    tasks = tasks + [(200, in_sum), (200, norm_one_back), (70, out_sum), (200, vector_sum)]
    return tasks


def block_kernel(*refs):
    r = SimpleNamespace()
    place = 0
    for group in (ENDS, WEIGHTS, ONCE, MOVES, SIGNALS):
        for name in group:
            setattr(r, name, refs[place])
            place += 1
    states = []
    for _ in range(2):
        state = SimpleNamespace(**vars(r))
        for name in BOTH:
            setattr(state, name, refs[place])
            place += 1
        states.append(state)
    crops, _, rows, width = r.vox.shape
    per_crop = rows // (2 * TOK)
    subs = rows // TOK
    steps = crops * per_crop
    depth, peers_d = lax.axis_index("depth"), lax.axis_size("depth")
    column, peers_w = lax.axis_index("wide"), lax.axis_size("wide")
    d_prev = {"depth": lax.rem(depth + peers_d - 1, peers_d)}
    d_next = {"depth": lax.rem(depth + 1, peers_d)}
    w_prev = {"wide": lax.rem(column + peers_w - 1, peers_w)}
    w_next = {"wide": lax.rem(column + 1, peers_w)}
    mesh_id = pl.DeviceIdType.MESH
    sources = (r.vox, r.cot)
    results = (r.out_res, r.out_tok)
    keeps = (r.keep_res, r.keep_tok)
    own, halo_d, halo_w = r.own, r.halo_d, r.halo_w

    def own_copy(c, a):
        slot = lax.rem(c, SLOTS)
        return pltpu.make_async_copy(
            sources[a].at[c, pl.ds(SHIFT, 2)], own.at[slot, a], r.own_sem.at[slot, a]
        )

    def raw_copy(c, a):
        slot = lax.rem(c, 2)
        return pltpu.make_async_copy(
            sources[a].at[c, pl.ds(0, SHIFT)], r.raw.at[slot, a], r.raw_sem.at[slot, a]
        )

    def depth_copy(c, u):
        slot = lax.rem(c, SLOTS)
        return pltpu.make_async_remote_copy(
            src_ref=r.send_d.at[slot, u],
            dst_ref=halo_d.at[lax.rem(c, DEPTH_SLOTS), u],
            send_sem=r.d_send.at[slot, u],
            recv_sem=r.d_recv.at[c, u],
            device_id=d_prev,
            device_id_type=mesh_id,
        )

    def pack_depth(c, u):
        slot = lax.rem(c, 2)
        for start, size, at in parts_of(u):
            for d in range(SHIFT):
                r.send_d[lax.rem(c, SLOTS), u, d, at : at + size, :] = jnp.concatenate(
                    [r.raw[slot, a, d, pl.ds(start, size), :] for a in range(2)], axis=1
                )

    def parts_of(u):
        first = pl.multiple_of(u * 2 * TOK + 16, 16)
        second = pl.multiple_of(lax.rem(u * 2 * TOK + 2 * TOK, rows), 16)
        return (first, 2 * TOK - 16, 0), (second, 16, 2 * TOK - 16)

    def pack_depth_whole(c):
        def one(u, carry):
            pack_depth(c, u)
            depth_copy(c, u).start()
            return carry

        for a in range(2):
            raw_copy(c, a).wait()
        lax.fori_loop(0, per_crop, one, 0)

    def wide_copy(c, u):
        slot = lax.rem(c, SLOTS)
        return pltpu.make_async_remote_copy(
            src_ref=r.send_w.at[slot, u],
            dst_ref=halo_w.at[c, u],
            send_sem=r.w_send.at[slot, u],
            recv_sem=r.w_recv.at[c, u],
            device_id=w_prev,
            device_id_type=mesh_id,
        )

    def back_copy(c, u):
        slot = lax.rem(c, SLOTS)
        return pltpu.make_async_remote_copy(
            src_ref=r.back_send.at[slot, u],
            dst_ref=r.back_recv.at[c, u],
            send_sem=r.b_send.at[slot, u],
            recv_sem=r.b_recv.at[c, u],
            device_id=w_next,
            device_id_type=mesh_id,
        )

    def return_copy(c, u):
        slot = lax.rem(c, SLOTS)
        return pltpu.make_async_remote_copy(
            src_ref=r.grid_ret.at[slot, u],
            dst_ref=r.ret_recv.at[lax.rem(c, RETURN_SLOTS), u],
            send_sem=r.r_send.at[slot, u],
            recv_sem=r.r_recv.at[c, u],
            device_id=d_next,
            device_id_type=mesh_id,
        )

    def keep_copy(c, a):
        slot = lax.rem(c, SLOTS)
        return pltpu.make_async_copy(
            keeps[a].at[slot], results[a].at[c, pl.ds(SHIFT, 2)], r.o_sem.at[slot, a]
        )

    def out_copy(c, a):
        slot = lax.rem(c, 2)
        return pltpu.make_async_copy(
            r.stage.at[slot, a], results[a].at[c, pl.ds(0, SHIFT)], r.q_sem.at[slot, a]
        )

    chips_d = peers_d // 2
    crew = lax.axis_size("dp") * chips_d
    core = lax.rem(depth, 2)
    place = lax.axis_index("dp") * chips_d + depth // 2
    twin = {"depth": depth + 1 - 2 * core}

    def mate(step):
        other = lax.rem(place + step, crew)
        return other, {"dp": other // chips_d, "depth": lax.rem(other, chips_d) * 2 + core}

    def across(step):
        other = lax.rem(column + step, peers_w)
        return other, {"wide": other}

    barrier = pltpu.get_barrier_semaphore()
    peers = [mate(step)[1] for step in range(1, crew)]
    peers = peers + [across(step)[1] for step in range(1, peers_w)]
    for peer in peers + [d_prev, d_next]:
        pl.semaphore_signal(barrier, inc=1, device_id=peer, device_id_type=mesh_id)
    pl.semaphore_wait(barrier, crew + peers_w)

    for c in range(2):
        for a in range(2):
            raw_copy(c, a).start()
    for c in range(SLOTS):
        for a in range(2):
            own_copy(c, a).start()
    pack_depth_whole(jnp.int32(0))
    for a in range(2):
        raw_copy(2, a).start()
    pack_depth_whole(jnp.int32(1))
    for a in range(2):
        raw_copy(3, a).start()

    for ref in (r.acc_in, r.acc_exp, r.acc_con, r.d_vec, r.d_tab, r.bias_pad):
        ref[...] = jnp.zeros_like(ref)
    for state in states:
        for ref in (state.entry_one, state.entry_two, state.mixed):
            ref[WIDTH:, :] = jnp.ones((16, SPAN), bf)
    r.back_recv[crops] = jnp.zeros(r.back_recv.shape[1:], bf)
    for ref in (r.w_in_t, r.w_out_t, r.w_exp_t):
        ref[:, WIDTH:] = jnp.zeros((ref.shape[0], 16), bf)
    r.w_in[...] = r.f_in[...].astype(bf)
    r.w_in_t[:, :WIDTH] = r.f_in[...].T.astype(bf)
    r.w_out[...] = r.f_out[...].astype(bf)
    r.w_out_t[:, :WIDTH] = r.f_out[...].T.astype(bf)
    r.w_exp[...] = (r.f_exp[...].astype(bf).astype(fl) * 0.5).astype(bf)
    r.w_exp_t[:, :WIDTH] = r.f_exp[...].T.astype(bf)
    r.w_con_t[...] = (r.f_con[...].astype(bf).astype(fl) * 0.5).astype(bf)
    r.w_con[...] = r.f_con[...].T.astype(bf)
    lane16 = lax.broadcasted_iota(jnp.int32, (64, 16), 1)
    for tile in range(r.vectors.shape[0]):
        spread = jnp.broadcast_to(r.vectors[tile : tile + 1, :], (128, 128)).T
        for part in range(2):
            chunk = spread[64 * part : 64 * part + 64]
            member, at = divmod(128 * tile + 64 * part, WIDTH)
            narrow = chunk[:, :16]
            high = narrow.astype(bf).astype(fl)
            middle = (narrow - high).astype(bf).astype(fl)
            column_parts = jnp.where(
                lane16 == 0,
                high,
                jnp.where(
                    lane16 == 1, middle, jnp.where(lane16 == 2, narrow - high - middle, 0.0)
                ),
            ).astype(bf)
            if member in (0, 1, 5, 6, 7):
                base = {0: GAIN_ONE, 1: SHIFT_ONE, 5: GAIN_TWO, 6: SHIFT_TWO, 7: CON_BIAS}[member]
                r.vec[base + at : base + at + 64, :] = chunk
            elif member == 2:
                r.w_in_t[at : at + 64, WIDTH:] = column_parts
            elif member == 3:
                r.w_in_t[2 * WIDTH + at : 2 * WIDTH + at + 64, WIDTH:] = column_parts
            elif member == 4:
                r.w_out_t[at : at + 64, WIDTH:] = column_parts
            else:
                base = WIDTH * (member - 8)
                r.w_exp_t[base + at : base + at + 64, WIDTH:] = column_parts

    related = r.related

    def chooser(places):
        return (
            lax.broadcasted_iota(jnp.int32, (384, 128), 0)
            == jnp.broadcast_to(places, (384, 128))
        ).astype(bf)

    def eight(block):
        return pl.ds(pl.multiple_of(8 * block, 8), 8)

    def thirds(v):
        high = v.astype(bf)
        rest = v - high.astype(fl)
        middle = rest.astype(bf)
        return jnp.concatenate([high, middle, (rest - middle.astype(fl)).astype(bf)], axis=0)

    def ends(v):
        return v[:8] + v[8:16] + v[16:24]

    def code(at, window, edge):
        last_d = (depth == peers_d - 1).astype(jnp.int32)
        last_w = (column == peers_w - 1).astype(jnp.int32)
        d, h, w = at // 16, lax.rem(at // 4, 4), lax.rem(at, 4)
        return (
            last_d * (d >= SHIFT).astype(jnp.int32) * 4
            + edge * (h >= SHIFT).astype(jnp.int32) * 2
            + last_w * window * (w >= SHIFT).astype(jnp.int32)
        )

    r.bias_pad[: r.bias.shape[0], : r.bias.shape[1]] = r.bias[...]
    bias_parts = thirds(r.bias_pad[...])

    def table_rows(block, carry):
        near = related[eight(block), :]
        found = [ends(dot(bias_parts, chooser(near[k : k + 1]))) for k in range(8)]
        lane = lax.broadcasted_iota(jnp.int32, (8, 128), 1)
        j = lax.broadcasted_iota(jnp.int32, (8, 128), 0) + 8 * block
        window, i = lane // TOK, lax.rem(lane, TOK)
        for edge in range(2):
            differ = code(i, window, edge) != code(j, window, edge)
            mask = jnp.where(differ, mask_fill, 0.0)
            for head in range(HEADS):
                values = jnp.concatenate([row[head : head + 1, :] for row in found], axis=0)
                r.table[edge, eight(block), 128 * head : 128 * head + 128] = (
                    values + mask
                ) * LOG2E
        return carry

    lax.fori_loop(0, TOK // 8, table_rows, 0)
    first_half = lax.broadcasted_iota(jnp.int32, (TOK, 128), 1) < TOK

    def starts(b):
        first = pl.multiple_of(b * TOK + 16, 16)
        second = pl.multiple_of(lax.rem(b * TOK + TOK, rows), 16)
        return first, second

    def kept(c, a, b):
        first, second = starts(b)
        slot = lax.rem(c, SLOTS)
        parts = []
        for d in range(2):
            parts.append(own[slot, a, d, pl.ds(first, 48), :])
            parts.append(own[slot, a, d, pl.ds(second, 16), :])
        return jnp.concatenate(parts, axis=0)

    def brought(c, b):
        u, there = edge_rows(b)
        slot = lax.rem(c, DEPTH_SLOTS)
        return jnp.concatenate([halo_d[slot, u, d, there, :] for d in range(2)], axis=0)

    def edge_rows(b):
        return b // 2, pl.ds(pl.multiple_of(lax.rem(b, 2) * TOK, TOK), TOK)

    def pack(c, b):
        u, there = edge_rows(b)
        source = jnp.minimum(c, crops - 1)
        near = jnp.concatenate(
            [dot(r.pick[...], kept(source, a, b)) for a in range(2)], axis=1
        )
        far = dot(r.pick[...], brought(source, b))
        r.send_w[lax.rem(c, SLOTS), u, there, :] = jnp.concatenate([near, far], axis=0).astype(
            bf
        )

    ahead_units = SLOTS * 2 * per_crop

    def place_of(g):
        g = g + ahead_units
        return g // per_crop - 2 * SLOTS, lax.rem(g, per_crop)

    def merge(g, s):
        c, u = place_of(g)
        b = SUBS * u + s
        first, second = starts(b)
        _, there = edge_rows(b)
        slot = lax.rem(c + 2 * SLOTS, SLOTS)
        arrived = r.back_recv[jnp.where(c >= 0, c, crops), u, there, :]
        for a in range(2):
            extra = dot(r.fill[...], arrived[:TOK // 2, WIDTH * a : WIDTH * a + WIDTH]).astype(bf)
            for d in range(2):
                for start, size, at in ((first, 48, 64 * d), (second, 16, 64 * d + 48)):
                    keeps[a][slot, d, pl.ds(start, size), :] = (
                        keeps[a][slot, d, pl.ds(start, size), :] + extra[at : at + size]
                    )
        extra = dot(r.fill[...], arrived[TOK // 2 :, :]).astype(bf)
        for d in range(2):
            r.grid_ret[slot, u, d, there, :] = (
                r.grid_ret[slot, u, d, there, :] + extra[TOK * d : TOK * d + TOK]
            )

    def unpack(g):
        c, u = place_of(g)
        slot = jnp.where(c >= 0, lax.rem(c + 2 * RETURN_SLOTS, RETURN_SLOTS), RETURN_SLOTS)
        to = lax.rem(c + 2 * SLOTS, 2)
        for start, size, at in parts_of(u):
            for d in range(SHIFT):
                both = r.ret_recv[slot, u, d, at : at + size, :]
                for a in range(2):
                    r.stage[to, a, d, pl.ds(start, size), :] = both[
                        :, WIDTH * a : WIDTH * a + WIDTH
                    ]

    def put_keep(a, c, b, low):
        first, second = starts(b)
        slot = lax.rem(c, SLOTS)
        placed = low.T
        for d in range(2):
            keeps[a][slot, d, pl.ds(first, 48), :] = placed[64 * d : 64 * d + 48]
            keeps[a][slot, d, pl.ds(second, 16), :] = placed[64 * d + 48 : 64 * d + 64]

    def moved_out(ref, give):
        rows_of = jnp.concatenate(
            [ref[:, LANES * s : LANES * s + LANES] for s in range(SUBS)], axis=0
        )
        return dot(rows_of, give[...]).astype(bf)

    def put_result(g, state):
        c, u = g // per_crop, lax.rem(g, per_crop)

        def run():
            moved = moved_out(state.result, state.give)
            for s in range(SUBS):
                mine = moved[WIDTH * s : WIDTH * s + WIDTH]
                state.edge_res[s] = mine[:, 2 * TOK :]
                put_keep(0, c, 2 * u + s, mine[:, : 2 * TOK])

        return run

    def put_gradient(g, state):
        g = g + SLOTS * per_crop
        c, u = g // per_crop, lax.rem(g, per_crop)

        def run():
            moved = moved_out(state.token_grad, state.give)
            slot = lax.rem(c, SLOTS)
            for s in range(SUBS):
                b = 2 * u + s
                mine = moved[WIDTH * s : WIDTH * s + WIDTH]
                put_keep(1, c, b, mine[:, : 2 * TOK])
                both = jnp.concatenate([state.edge_res[s], mine[:, 2 * TOK :]], axis=0).T
                there = slice(TOK * s, TOK * s + TOK)
                for d in range(2):
                    r.grid_ret[slot, u, d, there, :] = both[TOK * d : TOK * d + TOK]
                r.back_send[slot, u, there, :] = both[2 * TOK :]

        return run

    def forward_of(g, state):
        c, u = g // per_crop, lax.rem(g, per_crop)

        def tokens_of(s):
            b = 2 * u + s
            part, there = edge_rows(b)
            edges = halo_w[c, part, there, :].T
            others = brought(c, b).T
            return [
                jnp.concatenate(
                    [
                        kept(c, a, b).T,
                        others[WIDTH * a : WIDTH * a + WIDTH],
                        edges[WIDTH * a : WIDTH * a + WIDTH],
                    ],
                    axis=1,
                )
                for a in range(2)
            ]

        def ready(s):
            return lambda: pack(c + 1, 2 * u + s)

        def depth_ready():
            pack_depth(c + SLOTS, u)

        edge = (u == per_crop - 1).astype(jnp.int32)
        tasks = forward_tasks(state, first_half, tokens_of, edge)
        return tasks, [(80, ready(0)), (40, depth_ready), (80, ready(1))]

    def backward_of(g, state):
        def mended(s):
            return lambda: merge(g - MERGE_LAG, s)

        def returned():
            unpack(g - UNPACK_LAG)

        tasks = backward_tasks(state, first_half)
        return tasks, [(120, mended(0)), (60, returned), (120, mended(1))]

    def before(f, b):
        if f is not None:
            c, u = f // per_crop, lax.rem(f, per_crop)

            @pl.when(u == 0)
            def _():
                @pl.when(c + 1 < crops)
                def _():
                    for a in range(2):
                        own_copy(c + 1, a).wait()

                @pl.when(c + SLOTS < crops)
                def _():
                    for a in range(2):
                        raw_copy(c + SLOTS, a).wait()

            wide_copy(c, u).wait_recv()
            depth_copy(c, u).wait_send()

            @pl.when(c + 1 < crops)
            def _():
                depth_copy(c + 1, u).wait_recv()

            @pl.when(c >= SLOTS - 1)
            def _():
                wide_copy(c + 1 - SLOTS, u).wait_send()

        if b is not None:
            c_b, u_b = place_of(b)

            @pl.when((u_b == 0) & (c_b >= SLOTS))
            def _():
                for a in range(2):
                    keep_copy(c_b - SLOTS, a).wait()

            ready_to_merge(b - MERGE_LAG)
            ready_to_unpack(b - UNPACK_LAG)
            c_p, u_p = place_of(b - 1)

            @pl.when(c_p >= SLOTS)
            def _():
                back_copy(c_p - SLOTS, u_p).wait_send()
                return_copy(c_p - SLOTS, u_p).wait_send()

    def ready_to_merge(g):
        @pl.when(g >= 0)
        def _():
            back_copy(*place_of(g)).wait_recv()

    def ready_to_unpack(g):
        c, u = place_of(g)

        @pl.when(g >= 0)
        def _():
            return_copy(c, u).wait_recv()

        @pl.when((u == 0) & (c >= 2))
        def _():
            for a in range(2):
                out_copy(c - 2, a).wait()

    def after_merge(g):
        c, u = place_of(g)

        @pl.when(g >= 0)
        def _():
            send_return(c, u)

            @pl.when(u == per_crop - 1)
            def _():
                for a in range(2):
                    keep_copy(c, a).start()

    def after_unpack(g):
        c, u = place_of(g)

        @pl.when((g >= 0) & (u == per_crop - 1))
        def _():
            for a in range(2):
                out_copy(c, a).start()

            @pl.when(c + RETURN_SLOTS < crops)
            def _():
                pl.semaphore_signal(r.r_free, inc=1, device_id=d_prev, device_id_type=mesh_id)

    def send_return(c, u):
        @pl.when((u == 0) & (c >= RETURN_SLOTS))
        def _():
            pl.semaphore_wait(r.r_free, 1)

        return_copy(c, u).start()

    def after(f, b):
        if f is not None:
            c, u = f // per_crop, lax.rem(f, per_crop)

            @pl.when(c + 1 < crops)
            def _():
                wide_copy(c + 1, u).start()

            @pl.when(c + SLOTS < crops)
            def _():
                @pl.when((u == 0) & (c + SLOTS >= DEPTH_SLOTS))
                def _():
                    pl.semaphore_wait(r.d_free, 1)

                depth_copy(c + SLOTS, u).start()

            @pl.when((u == per_crop - 1) & (c + SLOTS < crops))
            def _():
                for a in range(2):
                    own_copy(c + SLOTS, a).start()

            @pl.when((u == per_crop - 1) & (c + SLOTS + 2 < crops))
            def _():
                for a in range(2):
                    raw_copy(c + SLOTS + 2, a).start()

            @pl.when((u == per_crop - 1) & (c + DEPTH_SLOTS < crops))
            def _():
                pl.semaphore_signal(r.d_free, inc=1, device_id=d_next, device_id_type=mesh_id)

        if b is not None:
            @pl.when(b >= 1)
            def _():
                back_copy((b - 1) // per_crop, lax.rem(b - 1, per_crop)).start()

            after_merge(b - MERGE_LAG)
            after_unpack(b - UNPACK_LAG)

    def tasks_of(f, b, forward_state, backward_state):
        ahead, behind, extras = [], [], []
        if f is not None:
            ahead, more = forward_of(f, forward_state)
            extras = extras + more
        if b is not None:
            behind, more = backward_of(b, backward_state)
            extras = weave(extras, more)
            puts = [
                (140, put_result(b, backward_state)),
                (200, put_gradient(b - 1, forward_state)),
            ]
            extras = weave(extras, puts)
        return weave(weave(behind, ahead), extras)

    def half_step(f, b, forward_state, backward_state):
        before(f, b)
        for _, task in tasks_of(f, b, forward_state, backward_state):
            task()
        after(f, b)

    for a in range(2):
        own_copy(0, a).wait()

    def first_pack(u, carry):
        depth_copy(0, u).wait_recv()
        for s in range(SUBS):
            pack(0, SUBS * u + s)
        wide_copy(0, u).start()
        return carry

    lax.fori_loop(0, per_crop, first_pack, 0)
    pack_depth_whole(jnp.int32(2))
    for a in range(2):
        raw_copy(4, a).start()
    half_step(jnp.int32(0), None, states[0], None)

    def two_steps(i, carry):
        pair = ((2 * i + 1, 2 * i), (2 * i + 2, 2 * i + 1))
        for f, b in pair:
            before(f, b)
        tasks = tasks_of(*pair[0], states[1], states[0])
        tasks = tasks + tasks_of(*pair[1], states[0], states[1])
        for _, task in tasks:
            task()
        for f, b in pair:
            after(f, b)
        return carry

    lax.fori_loop(0, steps // 2 - 1, two_steps, 0)
    half_step(jnp.int32(steps - 1), jnp.int32(steps - 2), states[1], states[0])
    half_step(None, jnp.int32(steps - 1), states[0], states[1])
    back_copy(crops - 1 - SLOTS, per_crop - 1).wait_send()
    return_copy(crops - 1 - SLOTS, per_crop - 1).wait_send()
    put_gradient(jnp.int32(steps - 1), states[1])()
    back_copy(crops - 1, per_crop - 1).start()

    bucket, landed, total, d_row = r.bucket, r.landed, r.total, r.d_row
    partial_sum, landed_two = r.partial_sum, r.landed_two
    extra = 18 * width
    for tile in range(12):
        acc, at = ((r.acc_in, 128 * tile), (r.acc_exp, 128 * (tile - 6)))[tile // 6]
        turned = acc[at : at + 128, :].T * (1.0, 0.5)[tile // 6]
        bucket[width * tile : width * tile + width, :] = turned[:width].astype(bf)
        d_row[tile : tile + 1, :] = turned[width : width + 1]
    for tile in range(6):
        bucket[width * (12 + tile) : width * (13 + tile), :] = (
            r.acc_con[128 * tile : 128 * tile + 128, :].T * 0.5
        ).astype(bf)
    for tile in range(8):
        size = min(128, 5 * width - 128 * tile)
        d_row[12 + tile : 13 + tile, :size] = jnp.sum(
            r.d_vec[128 * tile : 128 * tile + size, :].T, 0, keepdims=True
        )
    d_row[19:20, 64:] = jnp.zeros((1, 64), fl)

    def table_sums(block, carry):
        near = related[eight(block), :]
        held = r.d_tab[eight(block), :]
        for k in range(8):
            rows_k = jnp.concatenate(
                [held[k : k + 1, 128 * head : 128 * head + 128] for head in range(HEADS)]
                + [jnp.zeros((2, 128), fl)],
                axis=0,
            )
            carry = carry + dot_nt(thirds(rows_k), chooser(near[k : k + 1]))
        return carry

    sums = ends(lax.fori_loop(0, TOK // 8, table_sums, jnp.zeros((24, 384), fl)))
    for tile in range(3):
        d_row[24 + 8 * tile : 32 + 8 * tile, :] = sums[:, 128 * tile : 128 * tile + 128]
    d_row[20:24, :] = jnp.zeros((4, 128), fl)
    bucket[extra : extra + 48, :] = d_row[...].astype(bf)
    length = bucket.shape[0]
    if length > extra + 48:
        bucket[extra + 48 :, :] = jnp.zeros((length - extra - 48, 128), bf)

    half = length // 2
    share = half // crew
    piece = share // peers_w

    def span(start, size):
        return pl.ds(pl.multiple_of(start, 16), size)

    base = core * half

    def zero_copy():
        return pltpu.make_async_remote_copy(
            src_ref=bucket.at[span((1 - core) * half, half)],
            dst_ref=r.landed_zero,
            send_sem=r.s0_send,
            recv_sem=r.s0_recv,
            device_id=twin,
            device_id_type=mesh_id,
        )

    def first_copy(step):
        other, peer = mate(step)
        return pltpu.make_async_remote_copy(
            src_ref=r.half_sum.at[span(other * share, share)],
            dst_ref=landed.at[step - 1],
            send_sem=r.s1_send.at[step - 1],
            recv_sem=r.s1_recv.at[step - 1],
            device_id=peer,
            device_id_type=mesh_id,
        )

    def second_copy(step):
        other, peer = across(step)
        return pltpu.make_async_remote_copy(
            src_ref=partial_sum.at[span(other * piece, piece)],
            dst_ref=landed_two.at[step - 1],
            send_sem=r.s2_send.at[step - 1],
            recv_sem=r.s2_recv.at[step - 1],
            device_id=peer,
            device_id_type=mesh_id,
        )

    def spread(start, size, send, recv, peer):
        there = total.at[span(start, size)]
        return pltpu.make_async_remote_copy(
            src_ref=there,
            dst_ref=there,
            send_sem=send,
            recv_sem=recv,
            device_id=peer,
            device_id_type=mesh_id,
        )

    def third_copy(step, owner=None):
        owner = column if owner is None else owner
        return spread(
            base + place * share + owner * piece,
            piece,
            r.s3_send.at[step - 1],
            r.s3_recv.at[step - 1],
            across(step)[1],
        )

    def fourth_copy(step, owner=None):
        owner = place if owner is None else owner
        return spread(
            base + owner * share,
            share,
            r.s4_send.at[step - 1],
            r.s4_recv.at[step - 1],
            mate(step)[1],
        )

    def fifth_copy(owner):
        return spread(owner * half, half, r.s5_send, r.s5_recv, twin)

    def third_arrival(step):
        return third_copy(step, lax.rem(column + peers_w - step, peers_w))

    def fourth_arrival(step):
        return fourth_copy(step, lax.rem(place + crew - step, crew))

    zero_copy().start()
    last = crops - 1

    def last_merge(g, carry):
        ready_to_merge(g)
        for s in range(SUBS):
            merge(g, s)
        after_merge(g)
        return carry

    def last_unpack(g, carry):
        ready_to_unpack(g)
        unpack(g)
        after_unpack(g)
        return carry

    zero_copy().wait_recv()
    r.half_sum[...] = (
        bucket[span(base, half), :].astype(fl) + r.landed_zero[...].astype(fl)
    ).astype(bf)
    for step in range(1, crew):
        first_copy(step).start()
    lax.fori_loop(steps - MERGE_LAG, steps, last_merge, 0)
    lax.fori_loop(steps - UNPACK_LAG, steps - per_crop, last_unpack, 0)
    for step in range(1, crew):
        first_copy(step).wait_recv()
    summed = r.half_sum[span(place * share, share), :].astype(fl)
    for step in range(1, crew):
        summed = summed + landed[step - 1].astype(fl)
    partial_sum[...] = summed.astype(bf)
    for step in range(1, peers_w):
        second_copy(step).start()
    for step in range(1, peers_w):
        second_copy(step).wait_recv()
    summed = partial_sum[span(column * piece, piece), :].astype(fl)
    for step in range(1, peers_w):
        summed = summed + landed_two[step - 1].astype(fl)
    total[span(base + place * share + column * piece, piece), :] = summed.astype(bf)
    for step in range(1, peers_w):
        third_copy(step).start()
    lax.fori_loop(steps - per_crop, steps, last_unpack, 0)
    for step in range(1, peers_w):
        third_arrival(step).wait_recv()
    for step in range(1, crew):
        fourth_copy(step).start()
    for step in range(1, crew):
        fourth_arrival(step).wait_recv()
    fifth_copy(core).start()
    fifth_copy(1 - core).wait_recv()
    leave = pltpu.make_async_copy(total, r.out_total, r.t_sem)
    leave.start()
    leave.wait()
    zero_copy().wait_send()
    fifth_copy(core).wait_send()
    for step in range(1, crew):
        first_copy(step).wait_send()
        fourth_copy(step).wait_send()
    for step in range(1, peers_w):
        second_copy(step).wait_send()
        third_copy(step).wait_send()

    def close(c, carry):
        for a in range(2):
            keep_copy(c, a).wait()
        for u in range(per_crop):
            back_copy(c, u).wait_send()
            return_copy(c, u).wait_send()
        return carry

    lax.fori_loop(crops - SLOTS, crops, close, 0)

    def close_wide(c, carry):
        for u in range(per_crop):
            wide_copy(c, u).wait_send()
        return carry

    lax.fori_loop(crops + 1 - SLOTS, crops, close_wide, 0)
    for c in (last - 1, last):
        for a in range(2):
            out_copy(c, a).wait()


def block_call(voxels, cotangent, matrices, bias_table, vectors):
    crops, planes, rows, width = voxels.shape
    whole = pl.BlockSpec(memory_space=pltpu.VMEM)
    far = pl.BlockSpec(memory_space=pl.ANY)
    related = relative_index().T
    related = jnp.asarray(np.concatenate([related, related], axis=1), jnp.int32)
    consts = list(matrices) + [bias_table, vectors, related] + placement()
    sem = pltpu.SemaphoreType.DMA
    parts = rows // (2 * TOK)
    crew = lax.axis_size("dp") * lax.axis_size("depth") // 2
    peers_w = lax.axis_size("wide")
    unit_rows = 32 * crew * peers_w
    length = -(-(18 * width + 48) // unit_rows) * unit_rows
    share = length // (2 * crew)
    return pl.pallas_call(
        block_kernel,
        in_specs=[far, far] + [whole] * len(consts),
        out_specs=[far, far, far],
        out_shape=[
            jax.ShapeDtypeStruct(voxels.shape, bf),
            jax.ShapeDtypeStruct(voxels.shape, bf),
            jax.ShapeDtypeStruct((length, 128), bf),
        ],
        scratch_shapes=[
            pltpu.VMEM(*spec)
            for spec in list(WEIGHTS.values())
            + list(ONCE.values())
            + list(moves(crops, rows, length, share, peers_w).values())
        ]
        + [
            sem((SLOTS, 2)),
            sem((2, 2)),
            sem((SLOTS, parts)),
            sem((crops, parts)),
            sem((SLOTS, parts)),
            sem((crops, parts)),
            sem((SLOTS, parts)),
            sem((crops, parts)),
            sem((SLOTS, 2)),
            sem((2, 2)),
            sem((SLOTS, parts)),
            sem((crops, parts)),
            pltpu.SemaphoreType.REGULAR,
            pltpu.SemaphoreType.REGULAR,
            sem((crew - 1,)),
            sem((crew - 1,)),
            sem((peers_w - 1,)),
            sem((peers_w - 1,)),
            sem((peers_w - 1,)),
            sem((peers_w - 1,)),
            sem((crew - 1,)),
            sem((crew - 1,)),
            sem(()),
            sem(()),
            sem(()),
            sem(()),
            sem(()),
        ]
        + [pltpu.VMEM(*spec) for spec in list(BOTH.values()) * 2],
        compiler_params=pltpu.CompilerParams(
            vmem_limit_bytes=63 * 2**20, collective_id=0, has_side_effects=True
        ),
        name="block",
    )(voxels, cotangent, *consts)


def update_kernel(*refs):
    far_in, total_in, far_params, far_out, far_new = (
        refs[0:2], refs[2], refs[3:21], refs[21:23], refs[23:51],
    )
    norm_ref, held, total = refs[51], refs[52], refs[53]
    params, grads_kept, copies = refs[54:72], refs[72:78], refs[78:82]
    in_sem, out_sem, load_sem, total_sem, save_sem = refs[82:87]
    crops = far_in[0].shape[0]

    def fetch(a, c):
        return pltpu.make_async_copy(far_in[a].at[c], held.at[a, c], in_sem.at[a, c])

    def store(a, c):
        return pltpu.make_async_copy(held.at[a, c], far_out[a].at[c], out_sem.at[a, c])

    def load(k):
        return pltpu.make_async_copy(far_params[k], params[k], load_sem.at[k])

    def save(k, ref):
        return pltpu.make_async_copy(ref, far_new[k], save_sem.at[k])

    whole = pltpu.make_async_copy(total_in, total, total_sem)
    whole.start()
    for k in range(18):
        load(k).start()
    for c in range(crops):
        for a in range(2):
            fetch(a, c).start()
    width = WIDTH
    whole.wait()

    def slab(tile):
        return total[width * tile : width * tile + width, :].astype(fl)

    small = total[18 * width : 18 * width + 48, :].astype(fl)
    low_half = slab(4)
    grads = [
        jnp.concatenate([slab(k) for k in range(4)] + [low_half[:, :64]], axis=1),
        jnp.concatenate([low_half[:, 64:], slab(5)], axis=1),
        jnp.concatenate([slab(k) for k in range(6, 12)], axis=1),
        jnp.concatenate([slab(k) for k in range(12, 18)], axis=1),
    ]
    flat_bias = jnp.concatenate([small[k : k + 1] for k in range(12)], axis=1)
    flat_sum = jnp.concatenate([small[k : k + 1] for k in range(12, 20)], axis=1)

    def cut(flat, index):
        return flat[:, width * index : width * index + width]

    table = jnp.concatenate([small[24:32], small[32:40], small[40:48]], axis=1)
    grads.append(table[:HEADS, : params[4].shape[1]])
    flat = jnp.concatenate(
        [
            cut(flat_sum, 0), cut(flat_sum, 1), cut(flat_bias, 0), cut(flat_bias, 2),
            cut(flat_bias, 3), cut(flat_sum, 2), cut(flat_sum, 3), cut(flat_sum, 4),
            flat_bias[:, 4 * width : 8 * width],
        ],
        axis=1,
    )
    grads.append(
        jnp.concatenate([flat[:, 128 * k : 128 * k + 128] for k in range(18)], axis=0)
    )
    squares = jnp.zeros((1, 1), fl)
    for grad in grads:
        squares = squares + jnp.sum(
            jnp.sum(grad * grad, 0, keepdims=True), 1, keepdims=True
        )
    norm_value = jnp.sqrt(squares)
    norm_ref[...] = norm_value
    factor = jnp.minimum(1.0, clip_bound / (norm_value + 1e-06))
    for member in (2, 3, 0, 1, 4, 5):
        matrix = member < 4
        for k in range(3):
            load(6 * k + member).wait()
        clipped = grads[member] * factor
        first, second, fresh = adam_update(
            params[member][...],
            params[6 + member][...],
            params[12 + member][...],
            clipped,
            rate_matrix if matrix else rate_vector,
            weight_decay if matrix else 0.0,
        )
        grads_kept[member][...] = clipped
        params[6 + member][...] = first
        params[12 + member][...] = second
        params[member][...] = fresh
        if matrix:
            copies[member][...] = fresh.astype(bf)
            save(24 + member, copies[member]).start()
        for place, ref in enumerate(
            (grads_kept[member], params[6 + member], params[12 + member], params[member])
        ):
            save(4 * member + place, ref).start()
        for c in range(member * crops // 6, (member + 1) * crops // 6):
            for a in range(2):
                fetch(a, c).wait()
                store(a, c).start()
    for member in range(6):
        for place, ref in enumerate(
            (grads_kept[member], params[6 + member], params[12 + member], params[member])
        ):
            save(4 * member + place, ref).wait()
        if member < 4:
            save(24 + member, copies[member]).wait()
    for a in range(2):
        for c in range(crops):
            store(a, c).wait()


def update_call(result, token_grad, total, params):
    whole = pl.BlockSpec(memory_space=pltpu.VMEM)
    far = pl.BlockSpec(memory_space=pl.ANY)
    shapes = []
    for member in range(6):
        shapes = shapes + [jax.ShapeDtypeStruct(params[member].shape, fl)] * 4
    for member in range(4):
        shapes.append(jax.ShapeDtypeStruct(params[member].shape, bf))
    shapes.append(jax.ShapeDtypeStruct((1, 1), fl))
    big = jax.ShapeDtypeStruct(result.shape, bf)
    sem = pltpu.SemaphoreType.DMA
    return pl.pallas_call(
        update_kernel,
        in_specs=[far] * 21,
        out_specs=[far] * 30 + [whole],
        out_shape=[big, big] + shapes,
        scratch_shapes=[pltpu.VMEM((2,) + result.shape, bf), pltpu.VMEM(total.shape, bf)]
        + [pltpu.VMEM(p.shape, fl) for p in params]
        + [pltpu.VMEM(p.shape, fl) for p in params[:6]]
        + [pltpu.VMEM(p.shape, bf) for p in params[:4]]
        + [sem((2, result.shape[0]))] * 2
        + [sem((18,)), sem(()), sem((28,))],
        compiler_params=pltpu.CompilerParams(vmem_limit_bytes=56 * 2**20),
        name="update",
    )(result, token_grad, total, *params)


def local(
    voxels,
    cotangent,
    project_in,
    project_out,
    expand,
    contract,
    bias_table,
    vectors,
    project_in_first,
    project_out_first,
    expand_first,
    contract_first,
    bias_table_first,
    vectors_first,
    project_in_second,
    project_out_second,
    expand_second,
    contract_second,
    bias_table_second,
    vectors_second,
):
    batches, planes, height, breadth, width = voxels.shape
    flat = (batches, planes, height * breadth, width)
    result, token_grad, total = block_call(
        voxels.reshape(flat),
        cotangent.reshape(flat),
        (project_in, project_out, expand, contract.T),
        bias_table,
        vectors.reshape(-1, 128),
    )
    params = [
        project_in,
        project_out,
        expand,
        contract.T,
        bias_table,
        vectors.reshape(-1, 128),
        project_in_first,
        project_out_first,
        expand_first,
        contract_first.T,
        bias_table_first,
        vectors_first.reshape(-1, 128),
        project_in_second,
        project_out_second,
        expand_second,
        contract_second.T,
        bias_table_second,
        vectors_second.reshape(-1, 128),
    ]
    done = update_call(result, token_grad, total, params)
    outs = list(done[2:30])
    for place in range(20, 24):
        outs[place] = outs[place].reshape(-1)
    for place in (12, 13, 14, 15, 27):
        outs[place] = outs[place].T
    return (
        (done[0].reshape(voxels.shape), done[1].reshape(voxels.shape))
        + tuple(outs)
        + (done[30].reshape(()),)
    )


def solution(mesh):
    split = P("dp", "depth", None, "wide", None)
    return jax.shard_map(
        local,
        mesh=mesh,
        in_specs=(split,) * 2 + (P(),) * 18,
        out_specs=(split,) * 2 + (P(),) * 29,
        check_vma=False,
    )
```

```python
from types import SimpleNamespace

import jax
import jax.numpy as jnp
import numpy as np
from jax import lax
from jax.experimental import pallas as pl
from jax.experimental.pallas import tpu as pltpu
from jax.sharding import PartitionSpec as P

HEADS = 6
WIN = 4
SHIFT = 2
STEP = 10
TOK = WIN**3
GROUP = 4
LANES = GROUP * TOK

norm_eps = 1e-05
mask_fill = -100.0
clip_bound = 1000.0
rate_matrix = 0.1
rate_vector = 0.6
weight_decay = 0.01
beta_first = 0.9
beta_second = 0.999
adam_eps = 1e-08
LOG2E = 1.4426950408889634
INV_SQRT2 = 0.7071067811865476
INV_SQRT2PI = 0.3989422804014327


def relative_index():
    extent = 2 * WIN - 1
    corner = np.arange(WIN)
    places = np.stack(np.meshgrid(corner, corner, corner, indexing="ij"), -1).reshape(-1, 3)
    offsets = places[:, None, :] - places[None, :, :] + WIN - 1
    return (offsets[..., 0] * extent + offsets[..., 1]) * extent + offsets[..., 2]


def adam_update(weight, first, second, gradient, rate, decay):
    first_new = beta_first * first + (1.0 - beta_first) * gradient
    second_new = beta_second * second + (1.0 - beta_second) * gradient * gradient
    first_hat = first_new / (1.0 - beta_first**STEP)
    second_hat = second_new / (1.0 - beta_second**STEP)
    weight_new = weight - rate * (first_hat / (jnp.sqrt(second_hat) + adam_eps) + decay * weight)
    return (first_new, second_new, weight_new)


fl = jnp.float32
bf = jnp.bfloat16


def dot(a, b):
    return jnp.dot(a, b, preferred_element_type=fl)


def dot_nt(a, b):
    return lax.dot_general(a, b, (((1,), (1,)), ((), ())), preferred_element_type=fl)


def wide(v, lanes):
    return jnp.concatenate([v] * (lanes // v.shape[1]), axis=1)


def unit_norm(v):
    width = v.shape[0]
    mean = jnp.sum(v, 0, keepdims=True) * (1.0 / width)
    centred = v - mean
    inverse = lax.rsqrt(jnp.sum(centred * centred, 0, keepdims=True) * (1.0 / width) + norm_eps)
    return centred * inverse, inverse


def unit_back(grad, unit, inverse, gain):
    width = grad.shape[0]
    scaled = grad * gain
    inner = jnp.sum(scaled, 0, keepdims=True) * (1.0 / width)
    along = jnp.sum(scaled * unit, 0, keepdims=True) * (1.0 / width)
    return inverse * (scaled - inner - unit * along)


def fold(v):
    total = v[:, :128]
    for lane in range(128, v.shape[1], 128):
        total = total + v[:, lane : lane + 128]
    return total


def two_windows(compact, first_half):
    zero = jnp.zeros_like(compact)
    return jnp.concatenate(
        [jnp.where(first_half, compact, zero), jnp.where(first_half, zero, compact)], axis=0
    )


def two_heads(ref, head_pair, lanes):
    at = 64 * head_pair
    zero = jnp.zeros((32, 128), bf)
    return jnp.concatenate(
        [
            jnp.concatenate([ref[at : at + 32, lanes], zero], axis=1),
            jnp.concatenate([zero, ref[at + 32 : at + 64, lanes]], axis=1),
        ],
        axis=0,
    )


def cross(token_major, low, first, head_pair, first_half):
    right = two_heads(low, head_pair, slice(first, first + 128))
    if head_pair == 1:
        right = jnp.concatenate([jnp.zeros((64, 256), bf), right], axis=0)
        left = token_major[first : first + 128, 0:128]
    else:
        at = 64 * head_pair
        left = token_major[first : first + 128, at : at + 64]
    full = dot(left, right)
    out = []
    for head in range(2):
        block = full[:, 128 * head : 128 * head + 128]
        out.append(jnp.where(first_half, block[:TOK], block[TOK:]))
    return out


def weave(one, other):
    whole_one = sum(weight for weight, _ in one) + 1e-9
    whole_other = sum(weight for weight, _ in other) + 1e-9
    merged, done_one, done_other = [], 0.0, 0.0
    one, other = list(one), list(other)
    while one or other:
        if not other or (
            one
            and (done_one + one[0][0] / 2) / whole_one
            <= (done_other + other[0][0] / 2) / whole_other
        ):
            merged.append(one.pop(0))
            done_one += merged[-1][0]
        else:
            merged.append(other.pop(0))
            done_other += merged[-1][0]
    return merged


def placement():
    take = np.zeros((LANES + TOK, LANES), np.float32)
    pick = np.zeros((TOK, LANES), np.float32)
    for hw in range(2):
        for ww in range(2):
            for d in range(WIN):
                for hh in range(WIN):
                    for wl in range(WIN):
                        t = ((hw * 2 + ww) * WIN + d) * 16 + hh * 4 + wl
                        h, w = 4 * hw + hh, 4 * ww + wl
                        if w < 2 * WIN - SHIFT:
                            row = d * 64 + h * 8 + w + SHIFT
                        else:
                            row = LANES + d * 16 + h * 2 + w - (2 * WIN - SHIFT)
                        take[row, t] = 1.0
    for d in range(WIN):
        for h in range(2 * WIN):
            for w in range(SHIFT):
                pick[d * 16 + h * 2 + w, d * 64 + h * 8 + w] = 1.0
    pick = pick[:32, :128]
    return [jnp.asarray(m, bf) for m in (take, take.T, pick, pick.T)]


WIDTH = 192
HID = 4 * WIDTH
SPAN = 2 * LANES
PAIRS = SPAN // 128
SUBS = SPAN // LANES
SLOTS = 3
DEPTH_SLOTS = 5
RETURN_SLOTS = 3
MERGE_LAG = 4
UNPACK_LAG = 8
BOTH = dict(
    up=((WIDTH, SPAN), fl),
    up_low=((WIDTH, SPAN), bf),
    unit_one=((WIDTH, SPAN), fl),
    inverse_one=((8, SPAN), fl),
    entry_one=((WIDTH + 16, SPAN), bf),
    query=((WIDTH, SPAN), bf),
    keys=((WIDTH, SPAN), bf),
    values=((WIDTH, SPAN), bf),
    values_t=((SPAN, WIDTH), bf),
    probs=((PAIRS, HEADS, TOK, 128), fl),
    probs_low=((PAIRS, HEADS, TOK, 128), bf),
    mixed=((WIDTH + 16, SPAN), bf),
    unit_two=((WIDTH, SPAN), fl),
    inverse_two=((8, SPAN), fl),
    entry_two=((WIDTH + 16, SPAN), bf),
    slope=((HID, SPAN), fl),
    active=((HID, SPAN), bf),
    edge_res=((SUBS, WIDTH, 3 * TOK), bf),
)
ONCE = dict(
    x=((WIDTH, SPAN), fl),
    keys_t=((SPAN, WIDTH), bf),
    result=((WIDTH, SPAN), bf),
    hidden_low=((HID, SPAN), bf),
    grad_two=((WIDTH, SPAN), fl),
    middle_grad=((WIDTH, SPAN), fl),
    branch_low=((WIDTH, SPAN), bf),
    mixed_low=((WIDTH, SPAN), bf),
    triple_low=((3 * WIDTH, SPAN), bf),
    grad_one=((WIDTH, SPAN), fl),
    token_grad=((WIDTH, SPAN), bf),
)
WEIGHTS = dict(
    table=((2, TOK, HEADS * 128), fl),
    vec=((5 * WIDTH, 128), fl),
    w_in_t=((3 * WIDTH, WIDTH + 16), bf),
    w_in=((WIDTH, 3 * WIDTH), bf),
    w_out_t=((WIDTH, WIDTH + 16), bf),
    w_out=((WIDTH, WIDTH), bf),
    w_exp_t=((HID, WIDTH + 16), bf),
    w_exp=((WIDTH, HID), bf),
    w_con=((HID, WIDTH), bf),
    w_con_t=((WIDTH, HID), bf),
    acc_in=((4 * WIDTH, WIDTH + 16), fl),
    acc_exp=((HID, WIDTH + 16), fl),
    acc_con=((HID, WIDTH), fl),
    d_vec=((5 * WIDTH, 128), fl),
    d_tab=((TOK, HEADS * 128), fl),
    d_row=((48, 128), fl),
    bias_pad=((8, 384), fl),
)
GAIN_ONE, SHIFT_ONE, GAIN_TWO, SHIFT_TWO, CON_BIAS = (WIDTH * k for k in range(5))
ENDS = dict(
    vox=0, cot=0, f_in=0, f_out=0, f_exp=0, f_con=0, bias=0, vectors=0, related=0,
    take=0, give=0, pick=0, fill=0, out_res=0, out_tok=0, out_total=0,
)
SIGNALS = dict(
    own_sem=0, raw_sem=0, d_send=0, d_recv=0, w_send=0, w_recv=0, b_send=0, b_recv=0,
    o_sem=0, q_sem=0, r_send=0, r_recv=0, d_free=0, r_free=0, s1_send=0, s1_recv=0, s2_send=0, s2_recv=0,
    s3_send=0, s3_recv=0, s4_send=0, s4_recv=0, s0_send=0, s0_recv=0, s5_send=0, s5_recv=0,
    t_sem=0,
)
scale = 32 ** (-0.5)


def moves(crops, rows, length, share, peers_w):
    half = length // 2
    crew = half // share
    piece = share // peers_w
    part = 2 * TOK
    parts = rows // part
    return dict(
        bucket=((length, 128), bf),
        landed_zero=((half, 128), bf),
        half_sum=((half, 128), bf),
        landed=((crew - 1, share, 128), bf),
        partial_sum=((share, 128), bf),
        landed_two=((peers_w - 1, piece, 128), bf),
        total=((length, 128), bf),
        own=((SLOTS, 2, 2, rows, WIDTH), bf),
        raw=((2, 2, 2, rows, WIDTH), bf),
        send_d=((SLOTS, parts, 2, part, 2 * WIDTH), bf),
        halo_d=((DEPTH_SLOTS, parts, 2, part, 2 * WIDTH), bf),
        halo_w=((crops, parts, part, 2 * WIDTH), bf),
        send_w=((SLOTS, parts, part, 2 * WIDTH), bf),
        back_send=((SLOTS, parts, part, 2 * WIDTH), bf),
        back_recv=((crops + 1, parts, part, 2 * WIDTH), bf),
        keep_res=((SLOTS, 2, rows, WIDTH), bf),
        keep_tok=((SLOTS, 2, rows, WIDTH), bf),
        grid_ret=((SLOTS, parts, 2, part, 2 * WIDTH), bf),
        ret_recv=((RETURN_SLOTS + 1, parts, 2, part, 2 * WIDTH), bf),
        stage=((2, 2, 2, rows, WIDTH), bf),
    )


MOVES = moves(1, 2 * TOK, 32, 16, 1)


def forward_tasks(r, first_half, tokens_of, edge):
    tasks = []
    slots = [(k, hp) for k in range(PAIRS) for hp in range(3)]
    held = {}

    def vec(at, lanes=SPAN):
        return wide(r.vec[at : at + WIDTH, :], lanes)

    def fetch():
        rows = []
        for s in range(SUBS):
            rows = rows + tokens_of(s)
        moved = dot(jnp.concatenate(rows, axis=0), r.take[...])
        for s in range(SUBS):
            lanes = slice(LANES * s, LANES * s + LANES)
            at = 2 * WIDTH * s
            up = moved[at + WIDTH : at + 2 * WIDTH]
            r.x[:, lanes] = moved[at : at + WIDTH]
            r.up[:, lanes] = up
            r.up_low[:, lanes] = up.astype(bf)

    def norm_one():
        unit_vals, inverse = unit_norm(r.x[...])
        r.unit_one[...] = unit_vals
        r.inverse_one[...] = jnp.broadcast_to(inverse, (8, SPAN))
        r.entry_one[:WIDTH] = (unit_vals * vec(GAIN_ONE) + vec(SHIFT_ONE)).astype(bf)

    def project():
        triple = dot(r.w_in_t[...], r.entry_one[...]).astype(bf)
        r.query[...] = triple[:WIDTH]
        r.keys[...] = triple[WIDTH : 2 * WIDTH]
        r.values[...] = triple[2 * WIDTH :]

    def turn():
        r.keys_t[...] = r.keys[...].T
        r.values_t[...] = r.values[...].T

    def scores(t):
        k, hp = slots[t]
        held["s", t] = cross(r.keys_t, r.query, 128 * k, hp, first_half)

    def soft(t):
        k, hp = slots[t]
        pieces = held.pop(("s", t))
        wides = []
        for head in (2 * hp, 2 * hp + 1):
            which = edge if k == PAIRS - 1 else 0
            s = (
                pieces[head - 2 * hp] * (scale * LOG2E)
                + r.table[which, :, 128 * head : 128 * head + 128]
            )
            e = jnp.exp2(s - jnp.max(s, 0, keepdims=True))
            p = e * (1.0 / jnp.sum(e, 0, keepdims=True))
            r.probs[k, head] = p
            p_low = p.astype(bf)
            r.probs_low[k, head] = p_low
            wides.append(two_windows(p_low, first_half))
        held["p", t] = wides

    def mix(t):
        k, hp = slots[t]
        lanes = slice(128 * k, 128 * k + 128)
        r.mixed[64 * hp : 64 * hp + 64, lanes] = dot(
            two_heads(r.values, hp, lanes), jnp.concatenate(held.pop(("p", t)), axis=0)
        ).astype(bf)

    def join():
        r.x[...] = r.x[...] + dot(r.w_out_t[...], r.mixed[...])

    def norm_two():
        unit_vals, inverse = unit_norm(r.x[...])
        r.unit_two[...] = unit_vals
        r.inverse_two[...] = jnp.broadcast_to(inverse, (8, SPAN))
        r.entry_two[:WIDTH] = (unit_vals * vec(GAIN_TWO) + vec(SHIFT_TWO)).astype(bf)

    def gelu(s, part):
        def run():
            lanes = slice(LANES * s, LANES * s + LANES)
            rows = slice(HID // 2 * part, HID // 2 * part + HID // 2)
            hidden = dot(r.w_exp_t[rows], r.entry_two[:, lanes])
            twice = 1.0 + lax.erf(hidden * INV_SQRT2)
            r.active[rows, lanes] = (hidden * twice).astype(bf)
            r.slope[rows, lanes] = twice + hidden * (
                (2.0 * INV_SQRT2PI) * jnp.exp2(hidden * hidden * (-0.5 * LOG2E))
            )

        return run

    def contracted(s):
        def run():
            lanes = slice(LANES * s, LANES * s + LANES)
            r.result[:, lanes] = (
                r.x[:, lanes]
                + dot(r.w_con_t[...], r.active[:, lanes])
                + vec(CON_BIAS, LANES)
            ).astype(bf)

        return run

    tasks = tasks + [(360, fetch), (97, norm_one), (443, project), (106, turn)]
    for t in range(len(slots) + 1):
        if t == 0:
            tasks.append((31, lambda: scores(0)))
        if t + 1 < len(slots):
            tasks.append((131, lambda t=t: scores(t + 1)))
        if t < len(slots):
            tasks.append((61, lambda t=t: soft(t)))
        if t >= 1:
            tasks.append((47, lambda t=t: mix(t - 1)))

    tasks = tasks + [(264, join), (93, norm_two)]
    tasks = tasks + [(206, gelu(s, part)) for s in range(SUBS) for part in range(2)]
    tasks = tasks + [(207, contracted(s)) for s in range(SUBS)]
    return tasks


def backward_tasks(r, first_half):
    slots = [(k, hp) for k in range(PAIRS) for hp in range(3)]
    held = {}

    def vec(at):
        return wide(r.vec[at : at + WIDTH, :], SPAN)

    def hidden_back(s, part):
        def run():
            lanes = slice(LANES * s, LANES * s + LANES)
            rows = slice(HID // 2 * part, HID // 2 * part + HID // 2)
            r.hidden_low[rows, lanes] = (
                dot(r.w_con[rows], r.up_low[:, lanes]) * r.slope[rows, lanes]
            ).astype(bf)

        return run

    def expand_back(s):
        def run():
            lanes = slice(LANES * s, LANES * s + LANES)
            r.grad_two[:, lanes] = dot(r.w_exp[...], r.hidden_low[:, lanes])

        return run

    def norm_two_back():
        grad = r.up[...] + unit_back(
            r.grad_two[...], r.unit_two[...], r.inverse_two[0:1, :], vec(GAIN_TWO)
        )
        r.middle_grad[...] = grad
        r.branch_low[...] = grad.astype(bf)

    def out_back():
        r.mixed_low[...] = dot(r.w_out[...], r.branch_low[...]).astype(bf)

    def expand_sum(part):
        def run():
            rows = slice(HID // 2 * part, HID // 2 * part + HID // 2)
            r.acc_exp[rows, :] += dot_nt(r.hidden_low[rows, :], r.entry_two[...])

        return run

    def contract_sum(part):
        def run():
            rows = slice(HID // 2 * part, HID // 2 * part + HID // 2)
            r.acc_con[rows, :] += dot_nt(r.active[rows, :], r.up_low[...])

        return run

    def prob_back(t):
        k, hp = slots[t]
        held["g", t] = cross(r.values_t, r.mixed_low, 128 * k, hp, first_half)

    def score_back(t):
        k, hp = slots[t]
        pieces = held.pop(("g", t))
        wides = []
        for head in (2 * hp, 2 * hp + 1):
            p, g = r.probs[k, head], pieces[head - 2 * hp]
            s = p * (g - jnp.sum(g * p, 0, keepdims=True))
            r.d_tab[:, 128 * head : 128 * head + 128] += s
            wides.append(two_windows(s.astype(bf), first_half))
        held["s", t] = wides

    def query_back(t):
        k, hp = slots[t]
        lanes = slice(128 * k, 128 * k + 128)
        at = 64 * hp
        r.triple_low[at : at + 64, lanes] = (
            dot(two_heads(r.keys, hp, lanes), jnp.concatenate(held["s", t], axis=0)) * scale
        ).astype(bf)

    def keys_back(t):
        k, hp = slots[t]
        lanes = slice(128 * k, 128 * k + 128)
        at = WIDTH + 64 * hp
        wides = held.pop(("s", t))
        r.triple_low[at : at + 64, lanes] = (
            dot_nt(two_heads(r.query, hp, lanes), jnp.concatenate(wides, axis=1)) * scale
        ).astype(bf)

    def values_back(t):
        k, hp = slots[t]
        lanes = slice(128 * k, 128 * k + 128)
        at = 2 * WIDTH + 64 * hp
        probs = jnp.concatenate(
            [two_windows(r.probs_low[k, head], first_half) for head in (2 * hp, 2 * hp + 1)], axis=1
        )
        r.triple_low[at : at + 64, lanes] = dot_nt(
            two_heads(r.mixed_low, hp, lanes), probs
        ).astype(bf)

    def entry_back(s):
        def run():
            lanes = slice(LANES * s, LANES * s + LANES)
            r.grad_one[:, lanes] = dot(r.w_in[...], r.triple_low[:, lanes])

        return run

    def in_sum():
        r.acc_in[: 3 * WIDTH, :] += dot_nt(r.triple_low[...], r.entry_one[...])

    def out_sum():
        r.acc_in[3 * WIDTH :, :] += dot_nt(r.branch_low[...], r.mixed[...])

    def norm_one_back():
        r.token_grad[...] = (
            r.middle_grad[...]
            + unit_back(
                r.grad_one[...], r.unit_one[...], r.inverse_one[0:1, :], vec(GAIN_ONE)
            )
        ).astype(bf)

    def vector_sum():
        one, two = r.grad_one[...], r.grad_two[...]
        for place, term in enumerate(
            (one * r.unit_one[...], one, two * r.unit_two[...], two, r.up[...])
        ):
            r.d_vec[WIDTH * place : WIDTH * place + WIDTH, :] += fold(term)

    tasks = [(96, hidden_back(s, part)) for s in range(SUBS) for part in range(2)]
    tasks = tasks + [(117, expand_back(s)) for s in range(SUBS)]
    tasks = tasks + [(738, norm_two_back), (76, out_back)]
    sums = [(132, expand_sum(part)) for part in range(2)]
    sums = sums + [(134, contract_sum(part)) for part in range(2)]
    fine = []
    for t in range(len(slots) + 1):
        if t == 0:
            fine.append((27, lambda: prob_back(0)))
        if t + 1 < len(slots):
            fine.append((89, lambda t=t: prob_back(t + 1)))
        if t < len(slots):
            fine.append((17, lambda t=t: values_back(t)))
            fine.append((52, lambda t=t: score_back(t)))
        if t >= 1:
            fine.append((12, lambda t=t: query_back(t - 1)))
            fine.append((21, lambda t=t: keys_back(t - 1)))
    tasks = tasks + weave(fine, sums)
    tasks = tasks + [(99, entry_back(s)) for s in range(SUBS)]
    tasks = tasks + [(136, in_sum), (170, norm_one_back), (44, out_sum), (502, vector_sum)]
    return tasks


def block_kernel(*refs):
    r = SimpleNamespace()
    place = 0
    for group in (ENDS, WEIGHTS, ONCE, MOVES, SIGNALS):
        for name in group:
            setattr(r, name, refs[place])
            place += 1
    states = []
    for _ in range(2):
        state = SimpleNamespace(**vars(r))
        for name in BOTH:
            setattr(state, name, refs[place])
            place += 1
        states.append(state)
    crops, _, rows, width = r.vox.shape
    per_crop = rows // (2 * TOK)
    subs = rows // TOK
    steps = crops * per_crop
    depth, peers_d = lax.axis_index("depth"), lax.axis_size("depth")
    column, peers_w = lax.axis_index("wide"), lax.axis_size("wide")
    d_prev = {"depth": lax.rem(depth + peers_d - 1, peers_d)}
    d_next = {"depth": lax.rem(depth + 1, peers_d)}
    w_prev = {"wide": lax.rem(column + peers_w - 1, peers_w)}
    w_next = {"wide": lax.rem(column + 1, peers_w)}
    mesh_id = pl.DeviceIdType.MESH
    sources = (r.vox, r.cot)
    results = (r.out_res, r.out_tok)
    keeps = (r.keep_res, r.keep_tok)
    own, halo_d, halo_w = r.own, r.halo_d, r.halo_w

    def own_copy(c, a):
        slot = lax.rem(c, SLOTS)
        return pltpu.make_async_copy(
            sources[a].at[c, pl.ds(SHIFT, 2)], own.at[slot, a], r.own_sem.at[slot, a]
        )

    def raw_copy(c, a):
        slot = lax.rem(c, 2)
        return pltpu.make_async_copy(
            sources[a].at[c, pl.ds(0, SHIFT)], r.raw.at[slot, a], r.raw_sem.at[slot, a]
        )

    def depth_copy(c, u):
        slot = lax.rem(c, SLOTS)
        return pltpu.make_async_remote_copy(
            src_ref=r.send_d.at[slot, u],
            dst_ref=halo_d.at[lax.rem(c, DEPTH_SLOTS), u],
            send_sem=r.d_send.at[slot, u],
            recv_sem=r.d_recv.at[c, u],
            device_id=d_prev,
            device_id_type=mesh_id,
        )

    def pack_depth(c, u):
        slot = lax.rem(c, 2)
        for start, size, at in parts_of(u):
            for d in range(SHIFT):
                r.send_d[lax.rem(c, SLOTS), u, d, at : at + size, :] = jnp.concatenate(
                    [r.raw[slot, a, d, pl.ds(start, size), :] for a in range(2)], axis=1
                )

    def parts_of(u):
        first = pl.multiple_of(u * 2 * TOK + 16, 16)
        second = pl.multiple_of(lax.rem(u * 2 * TOK + 2 * TOK, rows), 16)
        return (first, 2 * TOK - 16, 0), (second, 16, 2 * TOK - 16)

    def pack_depth_whole(c):
        def one(u, carry):
            pack_depth(c, u)
            depth_copy(c, u).start()
            return carry

        for a in range(2):
            raw_copy(c, a).wait()
        lax.fori_loop(0, per_crop, one, 0)

    def wide_copy(c, u):
        slot = lax.rem(c, SLOTS)
        return pltpu.make_async_remote_copy(
            src_ref=r.send_w.at[slot, u],
            dst_ref=halo_w.at[c, u],
            send_sem=r.w_send.at[slot, u],
            recv_sem=r.w_recv.at[c, u],
            device_id=w_prev,
            device_id_type=mesh_id,
        )

    def back_copy(c, u):
        slot = lax.rem(c, SLOTS)
        return pltpu.make_async_remote_copy(
            src_ref=r.back_send.at[slot, u],
            dst_ref=r.back_recv.at[c, u],
            send_sem=r.b_send.at[slot, u],
            recv_sem=r.b_recv.at[c, u],
            device_id=w_next,
            device_id_type=mesh_id,
        )

    def return_copy(c, u):
        slot = lax.rem(c, SLOTS)
        return pltpu.make_async_remote_copy(
            src_ref=r.grid_ret.at[slot, u],
            dst_ref=r.ret_recv.at[lax.rem(c, RETURN_SLOTS), u],
            send_sem=r.r_send.at[slot, u],
            recv_sem=r.r_recv.at[c, u],
            device_id=d_next,
            device_id_type=mesh_id,
        )

    def keep_copy(c, a):
        slot = lax.rem(c, SLOTS)
        return pltpu.make_async_copy(
            keeps[a].at[slot], results[a].at[c, pl.ds(SHIFT, 2)], r.o_sem.at[slot, a]
        )

    def out_copy(c, a):
        slot = lax.rem(c, 2)
        return pltpu.make_async_copy(
            r.stage.at[slot, a], results[a].at[c, pl.ds(0, SHIFT)], r.q_sem.at[slot, a]
        )

    chips_d = peers_d // 2
    crew = lax.axis_size("dp") * chips_d
    core = lax.rem(depth, 2)
    place = lax.axis_index("dp") * chips_d + depth // 2
    twin = {"depth": depth + 1 - 2 * core}

    def mate(step):
        other = lax.rem(place + step, crew)
        return other, {"dp": other // chips_d, "depth": lax.rem(other, chips_d) * 2 + core}

    def across(step):
        other = lax.rem(column + step, peers_w)
        return other, {"wide": other}

    barrier = pltpu.get_barrier_semaphore()
    peers = [mate(step)[1] for step in range(1, crew)]
    peers = peers + [across(step)[1] for step in range(1, peers_w)]
    for peer in peers + [d_prev, d_next]:
        pl.semaphore_signal(barrier, inc=1, device_id=peer, device_id_type=mesh_id)
    pl.semaphore_wait(barrier, crew + peers_w)

    for c in range(2):
        for a in range(2):
            raw_copy(c, a).start()
    for c in range(SLOTS):
        for a in range(2):
            own_copy(c, a).start()
    pack_depth_whole(jnp.int32(0))
    for a in range(2):
        raw_copy(2, a).start()

    for ref in (r.acc_in, r.acc_exp, r.acc_con, r.d_vec, r.d_tab, r.bias_pad):
        ref[...] = jnp.zeros_like(ref)
    for state in states:
        for ref in (state.entry_one, state.entry_two, state.mixed):
            ref[WIDTH:, :] = jnp.ones((16, SPAN), bf)
    r.back_recv[crops] = jnp.zeros(r.back_recv.shape[1:], bf)
    for ref in (r.w_in_t, r.w_out_t, r.w_exp_t):
        ref[:, WIDTH:] = jnp.zeros((ref.shape[0], 16), bf)
    r.w_in[...] = r.f_in[...].astype(bf)
    r.w_in_t[:, :WIDTH] = r.f_in[...].T.astype(bf)
    r.w_out[...] = r.f_out[...].astype(bf)
    r.w_out_t[:, :WIDTH] = r.f_out[...].T.astype(bf)
    r.w_exp[...] = (r.f_exp[...].astype(bf).astype(fl) * 0.5).astype(bf)
    r.w_exp_t[:, :WIDTH] = r.f_exp[...].T.astype(bf)
    r.w_con_t[...] = (r.f_con[...].astype(bf).astype(fl) * 0.5).astype(bf)
    r.w_con[...] = r.f_con[...].T.astype(bf)
    lane16 = lax.broadcasted_iota(jnp.int32, (64, 16), 1)
    for tile in range(r.vectors.shape[0]):
        spread = jnp.broadcast_to(r.vectors[tile : tile + 1, :], (128, 128)).T
        for part in range(2):
            chunk = spread[64 * part : 64 * part + 64]
            member, at = divmod(128 * tile + 64 * part, WIDTH)
            narrow = chunk[:, :16]
            high = narrow.astype(bf).astype(fl)
            middle = (narrow - high).astype(bf).astype(fl)
            column_parts = jnp.where(
                lane16 == 0,
                high,
                jnp.where(
                    lane16 == 1, middle, jnp.where(lane16 == 2, narrow - high - middle, 0.0)
                ),
            ).astype(bf)
            if member in (0, 1, 5, 6, 7):
                base = {0: GAIN_ONE, 1: SHIFT_ONE, 5: GAIN_TWO, 6: SHIFT_TWO, 7: CON_BIAS}[member]
                r.vec[base + at : base + at + 64, :] = chunk
            elif member == 2:
                r.w_in_t[at : at + 64, WIDTH:] = column_parts
            elif member == 3:
                r.w_in_t[2 * WIDTH + at : 2 * WIDTH + at + 64, WIDTH:] = column_parts
            elif member == 4:
                r.w_out_t[at : at + 64, WIDTH:] = column_parts
            else:
                base = WIDTH * (member - 8)
                r.w_exp_t[base + at : base + at + 64, WIDTH:] = column_parts

    related = r.related

    def chooser(places):
        return (
            lax.broadcasted_iota(jnp.int32, (384, 128), 0)
            == jnp.broadcast_to(places, (384, 128))
        ).astype(bf)

    def eight(block):
        return pl.ds(pl.multiple_of(8 * block, 8), 8)

    def thirds(v):
        high = v.astype(bf)
        rest = v - high.astype(fl)
        middle = rest.astype(bf)
        return jnp.concatenate([high, middle, (rest - middle.astype(fl)).astype(bf)], axis=0)

    def ends(v):
        return v[:8] + v[8:16] + v[16:24]

    def code(at, window, edge):
        last_d = (depth == peers_d - 1).astype(jnp.int32)
        last_w = (column == peers_w - 1).astype(jnp.int32)
        d, h, w = at // 16, lax.rem(at // 4, 4), lax.rem(at, 4)
        return (
            last_d * (d >= SHIFT).astype(jnp.int32) * 4
            + edge * (h >= SHIFT).astype(jnp.int32) * 2
            + last_w * window * (w >= SHIFT).astype(jnp.int32)
        )

    r.bias_pad[: r.bias.shape[0], : r.bias.shape[1]] = r.bias[...]
    bias_parts = thirds(r.bias_pad[...])

    def table_rows(block, carry):
        near = related[eight(block), :]
        found = [ends(dot(bias_parts, chooser(near[k : k + 1]))) for k in range(8)]
        lane = lax.broadcasted_iota(jnp.int32, (8, 128), 1)
        j = lax.broadcasted_iota(jnp.int32, (8, 128), 0) + 8 * block
        window, i = lane // TOK, lax.rem(lane, TOK)
        for edge in range(2):
            differ = code(i, window, edge) != code(j, window, edge)
            mask = jnp.where(differ, mask_fill, 0.0)
            for head in range(HEADS):
                values = jnp.concatenate([row[head : head + 1, :] for row in found], axis=0)
                r.table[edge, eight(block), 128 * head : 128 * head + 128] = (
                    values + mask
                ) * LOG2E
        return carry

    first_half = lax.broadcasted_iota(jnp.int32, (TOK, 128), 1) < TOK

    def starts(b):
        first = pl.multiple_of(b * TOK + 16, 16)
        second = pl.multiple_of(lax.rem(b * TOK + TOK, rows), 16)
        return first, second

    def kept(c, a, b):
        first, second = starts(b)
        slot = lax.rem(c, SLOTS)
        parts = []
        for d in range(2):
            parts.append(own[slot, a, d, pl.ds(first, 48), :])
            parts.append(own[slot, a, d, pl.ds(second, 16), :])
        return jnp.concatenate(parts, axis=0)

    def brought(c, b):
        u, there = edge_rows(b)
        slot = lax.rem(c, DEPTH_SLOTS)
        return jnp.concatenate([halo_d[slot, u, d, there, :] for d in range(2)], axis=0)

    def edge_rows(b):
        return b // 2, pl.ds(pl.multiple_of(lax.rem(b, 2) * TOK, TOK), TOK)

    def pack(c, b):
        u, there = edge_rows(b)
        source = jnp.minimum(c, crops - 1)
        near = jnp.concatenate(
            [dot(r.pick[...], kept(source, a, b)) for a in range(2)], axis=1
        )
        far = dot(r.pick[...], brought(source, b))
        r.send_w[lax.rem(c, SLOTS), u, there, :] = jnp.concatenate([near, far], axis=0).astype(
            bf
        )

    ahead_units = SLOTS * 2 * per_crop

    def place_of(g):
        g = g + ahead_units
        return g // per_crop - 2 * SLOTS, lax.rem(g, per_crop)

    def merge(g, s):
        c, u = place_of(g)
        b = SUBS * u + s
        first, second = starts(b)
        _, there = edge_rows(b)
        slot = lax.rem(c + 2 * SLOTS, SLOTS)
        arrived = r.back_recv[jnp.where(c >= 0, c, crops), u, there, :]
        for a in range(2):
            extra = dot(r.fill[...], arrived[:TOK // 2, WIDTH * a : WIDTH * a + WIDTH]).astype(bf)
            for d in range(2):
                for start, size, at in ((first, 48, 64 * d), (second, 16, 64 * d + 48)):
                    keeps[a][slot, d, pl.ds(start, size), :] = (
                        keeps[a][slot, d, pl.ds(start, size), :] + extra[at : at + size]
                    )
        extra = dot(r.fill[...], arrived[TOK // 2 :, :]).astype(bf)
        for d in range(2):
            r.grid_ret[slot, u, d, there, :] = (
                r.grid_ret[slot, u, d, there, :] + extra[TOK * d : TOK * d + TOK]
            )

    def unpack(g):
        c, u = place_of(g)
        slot = jnp.where(c >= 0, lax.rem(c + 2 * RETURN_SLOTS, RETURN_SLOTS), RETURN_SLOTS)
        to = lax.rem(c + 2 * SLOTS, 2)
        for start, size, at in parts_of(u):
            for d in range(SHIFT):
                both = r.ret_recv[slot, u, d, at : at + size, :]
                for a in range(2):
                    r.stage[to, a, d, pl.ds(start, size), :] = both[
                        :, WIDTH * a : WIDTH * a + WIDTH
                    ]

    def put_keep(a, c, b, low):
        first, second = starts(b)
        slot = lax.rem(c, SLOTS)
        placed = low.T
        for d in range(2):
            keeps[a][slot, d, pl.ds(first, 48), :] = placed[64 * d : 64 * d + 48]
            keeps[a][slot, d, pl.ds(second, 16), :] = placed[64 * d + 48 : 64 * d + 64]

    def moved_out(ref, give):
        rows_of = jnp.concatenate(
            [ref[:, LANES * s : LANES * s + LANES] for s in range(SUBS)], axis=0
        )
        return dot(rows_of, give[...]).astype(bf)

    def put_result(g, state):
        c, u = g // per_crop, lax.rem(g, per_crop)

        def run():
            moved = moved_out(state.result, state.give)
            for s in range(SUBS):
                mine = moved[WIDTH * s : WIDTH * s + WIDTH]
                state.edge_res[s] = mine[:, 2 * TOK :]
                put_keep(0, c, 2 * u + s, mine[:, : 2 * TOK])

        return run

    def put_gradient(g, state):
        g = g + SLOTS * per_crop
        c, u = g // per_crop, lax.rem(g, per_crop)

        def run():
            moved = moved_out(state.token_grad, state.give)
            slot = lax.rem(c, SLOTS)
            for s in range(SUBS):
                b = 2 * u + s
                mine = moved[WIDTH * s : WIDTH * s + WIDTH]
                put_keep(1, c, b, mine[:, : 2 * TOK])
                both = jnp.concatenate([state.edge_res[s], mine[:, 2 * TOK :]], axis=0).T
                there = slice(TOK * s, TOK * s + TOK)
                for d in range(2):
                    r.grid_ret[slot, u, d, there, :] = both[TOK * d : TOK * d + TOK]
                r.back_send[slot, u, there, :] = both[2 * TOK :]

        return run

    def forward_of(g, state):
        c, u = g // per_crop, lax.rem(g, per_crop)

        def tokens_of(s):
            b = 2 * u + s
            part, there = edge_rows(b)
            edges = halo_w[c, part, there, :].T
            others = brought(c, b).T
            return [
                jnp.concatenate(
                    [
                        kept(c, a, b).T,
                        others[WIDTH * a : WIDTH * a + WIDTH],
                        edges[WIDTH * a : WIDTH * a + WIDTH],
                    ],
                    axis=1,
                )
                for a in range(2)
            ]

        def ready(s):
            return lambda: pack(c + 1, 2 * u + s)

        def depth_ready():
            pack_depth(c + SLOTS, u)

        edge = (u == per_crop - 1).astype(jnp.int32)
        tasks = forward_tasks(state, first_half, tokens_of, edge)
        return tasks, [(88, ready(0)), (17, depth_ready), (61, ready(1))]

    def backward_of(g, state):
        def mended(s):
            return lambda: merge(g - MERGE_LAG, s)

        def returned():
            unpack(g - UNPACK_LAG)

        tasks = backward_tasks(state, first_half)
        return tasks, [(363, mended(0)), (21, returned), (153, mended(1))]

    def before(f, b):
        if f is not None:
            c, u = f // per_crop, lax.rem(f, per_crop)

            @pl.when(u == 0)
            def _():
                @pl.when(c + 1 < crops)
                def _():
                    for a in range(2):
                        own_copy(c + 1, a).wait()

                @pl.when(c + SLOTS < crops)
                def _():
                    for a in range(2):
                        raw_copy(c + SLOTS, a).wait()

            wide_copy(c, u).wait_recv()
            depth_copy(c, u).wait_send()

            @pl.when(c + 1 < crops)
            def _():
                depth_copy(c + 1, u).wait_recv()

            @pl.when(c >= SLOTS - 1)
            def _():
                wide_copy(c + 1 - SLOTS, u).wait_send()

        if b is not None:
            c_b, u_b = place_of(b)

            @pl.when((u_b == 0) & (c_b >= SLOTS))
            def _():
                for a in range(2):
                    keep_copy(c_b - SLOTS, a).wait()

            ready_to_merge(b - MERGE_LAG)
            ready_to_unpack(b - UNPACK_LAG)
            c_p, u_p = place_of(b - 1)

            @pl.when(c_p >= SLOTS)
            def _():
                back_copy(c_p - SLOTS, u_p).wait_send()
                return_copy(c_p - SLOTS, u_p).wait_send()

    def ready_to_merge(g):
        @pl.when(g >= 0)
        def _():
            back_copy(*place_of(g)).wait_recv()

    def ready_to_unpack(g):
        c, u = place_of(g)

        @pl.when(g >= 0)
        def _():
            return_copy(c, u).wait_recv()

        @pl.when((u == 0) & (c >= 2))
        def _():
            for a in range(2):
                out_copy(c - 2, a).wait()

    def after_merge(g):
        c, u = place_of(g)

        @pl.when(g >= 0)
        def _():
            send_return(c, u)

            @pl.when(u == per_crop - 1)
            def _():
                for a in range(2):
                    keep_copy(c, a).start()

    def after_unpack(g):
        c, u = place_of(g)

        @pl.when((g >= 0) & (u == per_crop - 1))
        def _():
            for a in range(2):
                out_copy(c, a).start()

            @pl.when(c + RETURN_SLOTS < crops)
            def _():
                pl.semaphore_signal(r.r_free, inc=1, device_id=d_prev, device_id_type=mesh_id)

    def send_return(c, u):
        @pl.when((u == 0) & (c >= RETURN_SLOTS))
        def _():
            pl.semaphore_wait(r.r_free, 1)

        return_copy(c, u).start()

    def after(f, b):
        if f is not None:
            c, u = f // per_crop, lax.rem(f, per_crop)

            @pl.when(c + 1 < crops)
            def _():
                wide_copy(c + 1, u).start()

            @pl.when(c + SLOTS < crops)
            def _():
                @pl.when((u == 0) & (c + SLOTS >= DEPTH_SLOTS))
                def _():
                    pl.semaphore_wait(r.d_free, 1)

                depth_copy(c + SLOTS, u).start()

            @pl.when((u == per_crop - 1) & (c + SLOTS < crops))
            def _():
                for a in range(2):
                    own_copy(c + SLOTS, a).start()

            @pl.when((u == per_crop - 1) & (c + SLOTS + 2 < crops))
            def _():
                for a in range(2):
                    raw_copy(c + SLOTS + 2, a).start()

            @pl.when((u == per_crop - 1) & (c + DEPTH_SLOTS < crops))
            def _():
                pl.semaphore_signal(r.d_free, inc=1, device_id=d_next, device_id_type=mesh_id)

        if b is not None:
            @pl.when(b >= 1)
            def _():
                back_copy((b - 1) // per_crop, lax.rem(b - 1, per_crop)).start()

            after_merge(b - MERGE_LAG)
            after_unpack(b - UNPACK_LAG)

    def tasks_of(f, b, forward_state, backward_state):
        ahead, behind, extras = [], [], []
        if f is not None:
            ahead, more = forward_of(f, forward_state)
            extras = extras + more
        if b is not None:
            behind, more = backward_of(b, backward_state)
            extras = weave(extras, more)
            puts = [
                (128, put_result(b, backward_state)),
                (105, put_gradient(b - 1, forward_state)),
            ]
            extras = weave(extras, puts)
        return weave(weave(behind, ahead), extras)

    def half_step(f, b, forward_state, backward_state):
        before(f, b)
        for _, task in tasks_of(f, b, forward_state, backward_state):
            task()
        after(f, b)

    for a in range(2):
        own_copy(0, a).wait()

    def first_pack(u, carry):
        depth_copy(0, u).wait_recv()
        for s in range(SUBS):
            pack(0, SUBS * u + s)
        wide_copy(0, u).start()
        return carry

    lax.fori_loop(0, per_crop, first_pack, 0)
    pack_depth_whole(jnp.int32(1))
    for a in range(2):
        raw_copy(3, a).start()
    lax.fori_loop(0, TOK // 8, table_rows, 0)
    pack_depth_whole(jnp.int32(2))
    for a in range(2):
        raw_copy(4, a).start()
    half_step(jnp.int32(0), None, states[0], None)

    def two_steps(i, carry):
        half_step(2 * i + 1, 2 * i, states[1], states[0])
        half_step(2 * i + 2, 2 * i + 1, states[0], states[1])
        return carry

    lax.fori_loop(0, steps // 2 - 1, two_steps, 0)
    half_step(jnp.int32(steps - 1), jnp.int32(steps - 2), states[1], states[0])
    bucket, d_row = r.bucket, r.d_row

    def expand_rows(tile):
        def run():
            turned = r.acc_exp[128 * tile : 128 * tile + 128, :].T * 0.5
            bucket[width * (6 + tile) : width * (7 + tile), :] = turned[:width].astype(bf)
            d_row[6 + tile : 7 + tile, :] = turned[width : width + 1]

        return run

    def contract_rows(tile):
        def run():
            bucket[width * (12 + tile) : width * (13 + tile), :] = (
                r.acc_con[128 * tile : 128 * tile + 128, :].T * 0.5
            ).astype(bf)

        return run

    table_total = [jnp.zeros((24, 384), fl)]

    def table_sums(block):
        def run():
            near = related[8 * block : 8 * block + 8, :]
            held = r.d_tab[8 * block : 8 * block + 8, :]
            for k in range(8):
                rows_k = jnp.concatenate(
                    [held[k : k + 1, 128 * head : 128 * head + 128] for head in range(HEADS)]
                    + [jnp.zeros((2, 128), fl)],
                    axis=0,
                )
                table_total[0] = table_total[0] + dot_nt(
                    thirds(rows_k), chooser(near[k : k + 1])
                )

        return run

    closing = [(300, table_sums(block)) for block in range(TOK // 8)]
    closing = weave(
        closing,
        [(40, expand_rows(tile)) for tile in range(6)]
        + [(40, contract_rows(tile)) for tile in range(6)],
    )
    last_unit = jnp.int32(steps - 1)
    before(None, last_unit)
    behind, more = backward_of(last_unit, states[1])
    more = weave(
        more, [(140, put_result(last_unit, states[1])), (200, put_gradient(last_unit - 1, states[0]))]
    )
    tail = 6
    for _, task in weave(behind[:-tail], more) + weave(behind[-tail:], closing):
        task()
    after(None, last_unit)
    back_copy(crops - 1 - SLOTS, per_crop - 1).wait_send()
    return_copy(crops - 1 - SLOTS, per_crop - 1).wait_send()
    put_gradient(jnp.int32(steps - 1), states[1])()
    back_copy(crops - 1, per_crop - 1).start()

    landed, total = r.landed, r.total
    partial_sum, landed_two = r.partial_sum, r.landed_two
    extra = 18 * width
    for tile in range(6):
        turned = r.acc_in[128 * tile : 128 * tile + 128, :].T
        bucket[width * tile : width * tile + width, :] = turned[:width].astype(bf)
        d_row[tile : tile + 1, :] = turned[width : width + 1]
    for tile in range(8):
        size = min(128, 5 * width - 128 * tile)
        d_row[12 + tile : 13 + tile, :size] = jnp.sum(
            r.d_vec[128 * tile : 128 * tile + size, :].T, 0, keepdims=True
        )
    d_row[19:20, 64:] = jnp.zeros((1, 64), fl)

    sums = ends(table_total[0])
    for tile in range(3):
        d_row[24 + 8 * tile : 32 + 8 * tile, :] = sums[:, 128 * tile : 128 * tile + 128]
    d_row[20:24, :] = jnp.zeros((4, 128), fl)
    bucket[extra : extra + 48, :] = d_row[...].astype(bf)
    length = bucket.shape[0]
    if length > extra + 48:
        bucket[extra + 48 :, :] = jnp.zeros((length - extra - 48, 128), bf)

    half = length // 2
    share = half // crew
    piece = share // peers_w

    def span(start, size):
        return pl.ds(pl.multiple_of(start, 16), size)

    base = core * half

    def zero_copy():
        return pltpu.make_async_remote_copy(
            src_ref=bucket.at[span((1 - core) * half, half)],
            dst_ref=r.landed_zero,
            send_sem=r.s0_send,
            recv_sem=r.s0_recv,
            device_id=twin,
            device_id_type=mesh_id,
        )

    def first_copy(step):
        other, peer = mate(step)
        return pltpu.make_async_remote_copy(
            src_ref=r.half_sum.at[span(other * share, share)],
            dst_ref=landed.at[step - 1],
            send_sem=r.s1_send.at[step - 1],
            recv_sem=r.s1_recv.at[step - 1],
            device_id=peer,
            device_id_type=mesh_id,
        )

    def second_copy(step):
        other, peer = across(step)
        return pltpu.make_async_remote_copy(
            src_ref=partial_sum.at[span(other * piece, piece)],
            dst_ref=landed_two.at[step - 1],
            send_sem=r.s2_send.at[step - 1],
            recv_sem=r.s2_recv.at[step - 1],
            device_id=peer,
            device_id_type=mesh_id,
        )

    def spread(start, size, send, recv, peer):
        there = total.at[span(start, size)]
        return pltpu.make_async_remote_copy(
            src_ref=there,
            dst_ref=there,
            send_sem=send,
            recv_sem=recv,
            device_id=peer,
            device_id_type=mesh_id,
        )

    def third_copy(step, owner=None):
        owner = column if owner is None else owner
        return spread(
            base + place * share + owner * piece,
            piece,
            r.s3_send.at[step - 1],
            r.s3_recv.at[step - 1],
            across(step)[1],
        )

    def fourth_copy(step, owner=None):
        owner = place if owner is None else owner
        return spread(
            base + owner * share,
            share,
            r.s4_send.at[step - 1],
            r.s4_recv.at[step - 1],
            mate(step)[1],
        )

    def fifth_copy(owner):
        return spread(owner * half, half, r.s5_send, r.s5_recv, twin)

    def third_arrival(step):
        return third_copy(step, lax.rem(column + peers_w - step, peers_w))

    def fourth_arrival(step):
        return fourth_copy(step, lax.rem(place + crew - step, crew))

    zero_copy().start()
    last = crops - 1

    def last_merge(g, carry):
        ready_to_merge(g)
        for s in range(SUBS):
            merge(g, s)
        after_merge(g)
        return carry

    def last_unpack(g, carry):
        ready_to_unpack(g)
        unpack(g)
        after_unpack(g)
        return carry

    zero_copy().wait_recv()
    r.half_sum[...] = (
        bucket[span(base, half), :].astype(fl) + r.landed_zero[...].astype(fl)
    ).astype(bf)
    for step in range(1, crew):
        first_copy(step).start()
    lax.fori_loop(steps - MERGE_LAG, steps, last_merge, 0)
    lax.fori_loop(steps - UNPACK_LAG, steps - per_crop, last_unpack, 0)
    for step in range(1, crew):
        first_copy(step).wait_recv()
    summed = r.half_sum[span(place * share, share), :].astype(fl)
    for step in range(1, crew):
        summed = summed + landed[step - 1].astype(fl)
    partial_sum[...] = summed.astype(bf)
    for step in range(1, peers_w):
        second_copy(step).start()
    for step in range(1, peers_w):
        second_copy(step).wait_recv()
    summed = partial_sum[span(column * piece, piece), :].astype(fl)
    for step in range(1, peers_w):
        summed = summed + landed_two[step - 1].astype(fl)
    total[span(base + place * share + column * piece, piece), :] = summed.astype(bf)
    for step in range(1, peers_w):
        third_copy(step).start()
    lax.fori_loop(steps - per_crop, steps, last_unpack, 0)
    for step in range(1, peers_w):
        third_arrival(step).wait_recv()
    for step in range(1, crew):
        fourth_copy(step).start()
    for step in range(1, crew):
        fourth_arrival(step).wait_recv()
    fifth_copy(core).start()
    fifth_copy(1 - core).wait_recv()
    leave = pltpu.make_async_copy(total, r.out_total, r.t_sem)
    leave.start()
    leave.wait()
    zero_copy().wait_send()
    fifth_copy(core).wait_send()
    for step in range(1, crew):
        first_copy(step).wait_send()
        fourth_copy(step).wait_send()
    for step in range(1, peers_w):
        second_copy(step).wait_send()
        third_copy(step).wait_send()

    def close(c, carry):
        for a in range(2):
            keep_copy(c, a).wait()
        for u in range(per_crop):
            back_copy(c, u).wait_send()
            return_copy(c, u).wait_send()
        return carry

    lax.fori_loop(crops - SLOTS, crops, close, 0)

    def close_wide(c, carry):
        for u in range(per_crop):
            wide_copy(c, u).wait_send()
        return carry

    lax.fori_loop(crops + 1 - SLOTS, crops, close_wide, 0)
    for c in (last - 1, last):
        for a in range(2):
            out_copy(c, a).wait()


def block_call(voxels, cotangent, matrices, bias_table, vectors):
    crops, planes, rows, width = voxels.shape
    whole = pl.BlockSpec(memory_space=pltpu.VMEM)
    far = pl.BlockSpec(memory_space=pl.ANY)
    related = relative_index().T
    related = jnp.asarray(np.concatenate([related, related], axis=1), jnp.int32)
    consts = list(matrices) + [bias_table, vectors, related] + placement()
    sem = pltpu.SemaphoreType.DMA
    parts = rows // (2 * TOK)
    crew = lax.axis_size("dp") * lax.axis_size("depth") // 2
    peers_w = lax.axis_size("wide")
    unit_rows = 32 * crew * peers_w
    length = -(-(18 * width + 48) // unit_rows) * unit_rows
    share = length // (2 * crew)
    return pl.pallas_call(
        block_kernel,
        in_specs=[far, far] + [whole] * len(consts),
        out_specs=[far, far, far],
        out_shape=[
            jax.ShapeDtypeStruct(voxels.shape, bf),
            jax.ShapeDtypeStruct(voxels.shape, bf),
            jax.ShapeDtypeStruct((length, 128), bf),
        ],
        scratch_shapes=[
            pltpu.VMEM(*spec)
            for spec in list(WEIGHTS.values())
            + list(ONCE.values())
            + list(moves(crops, rows, length, share, peers_w).values())
        ]
        + [
            sem((SLOTS, 2)),
            sem((2, 2)),
            sem((SLOTS, parts)),
            sem((crops, parts)),
            sem((SLOTS, parts)),
            sem((crops, parts)),
            sem((SLOTS, parts)),
            sem((crops, parts)),
            sem((SLOTS, 2)),
            sem((2, 2)),
            sem((SLOTS, parts)),
            sem((crops, parts)),
            pltpu.SemaphoreType.REGULAR,
            pltpu.SemaphoreType.REGULAR,
            sem((crew - 1,)),
            sem((crew - 1,)),
            sem((peers_w - 1,)),
            sem((peers_w - 1,)),
            sem((peers_w - 1,)),
            sem((peers_w - 1,)),
            sem((crew - 1,)),
            sem((crew - 1,)),
            sem(()),
            sem(()),
            sem(()),
            sem(()),
            sem(()),
        ]
        + [pltpu.VMEM(*spec) for spec in list(BOTH.values()) * 2],
        compiler_params=pltpu.CompilerParams(
            vmem_limit_bytes=63 * 2**20, collective_id=0, has_side_effects=True
        ),
        name="block",
    )(voxels, cotangent, *consts)


def update_kernel(*refs):
    far_in, total_in, far_params, far_out, far_new = (
        refs[0:2], refs[2], refs[3:21], refs[21:23], refs[23:51],
    )
    norm_ref, held, total = refs[51], refs[52], refs[53]
    params, grads_kept, copies = refs[54:72], refs[72:78], refs[78:82]
    in_sem, out_sem, load_sem, total_sem, save_sem = refs[82:87]
    crops = far_in[0].shape[0]

    def fetch(a, c):
        return pltpu.make_async_copy(far_in[a].at[c], held.at[a, c], in_sem.at[a, c])

    def store(a, c):
        return pltpu.make_async_copy(held.at[a, c], far_out[a].at[c], out_sem.at[a, c])

    def load(k):
        return pltpu.make_async_copy(far_params[k], params[k], load_sem.at[k])

    def save(k, ref):
        return pltpu.make_async_copy(ref, far_new[k], save_sem.at[k])

    whole = pltpu.make_async_copy(total_in, total, total_sem)
    whole.start()
    for k in range(18):
        load(k).start()
    for c in range(crops):
        for a in range(2):
            fetch(a, c).start()
    width = WIDTH
    whole.wait()

    def slab(tile):
        return total[width * tile : width * tile + width, :].astype(fl)

    small = total[18 * width : 18 * width + 48, :].astype(fl)
    low_half = slab(4)
    grads = [
        jnp.concatenate([slab(k) for k in range(4)] + [low_half[:, :64]], axis=1),
        jnp.concatenate([low_half[:, 64:], slab(5)], axis=1),
        jnp.concatenate([slab(k) for k in range(6, 12)], axis=1),
        jnp.concatenate([slab(k) for k in range(12, 18)], axis=1),
    ]
    flat_bias = jnp.concatenate([small[k : k + 1] for k in range(12)], axis=1)
    flat_sum = jnp.concatenate([small[k : k + 1] for k in range(12, 20)], axis=1)

    def cut(flat, index):
        return flat[:, width * index : width * index + width]

    table = jnp.concatenate([small[24:32], small[32:40], small[40:48]], axis=1)
    grads.append(table[:HEADS, : params[4].shape[1]])
    flat = jnp.concatenate(
        [
            cut(flat_sum, 0), cut(flat_sum, 1), cut(flat_bias, 0), cut(flat_bias, 2),
            cut(flat_bias, 3), cut(flat_sum, 2), cut(flat_sum, 3), cut(flat_sum, 4),
            flat_bias[:, 4 * width : 8 * width],
        ],
        axis=1,
    )
    grads.append(
        jnp.concatenate([flat[:, 128 * k : 128 * k + 128] for k in range(18)], axis=0)
    )
    squares = jnp.zeros((1, 1), fl)
    for grad in grads:
        squares = squares + jnp.sum(
            jnp.sum(grad * grad, 0, keepdims=True), 1, keepdims=True
        )
    norm_value = jnp.sqrt(squares)
    norm_ref[...] = norm_value
    factor = jnp.minimum(1.0, clip_bound / (norm_value + 1e-06))
    for member in (2, 3, 0, 1, 4, 5):
        matrix = member < 4
        for k in range(3):
            load(6 * k + member).wait()
        clipped = grads[member] * factor
        first, second, fresh = adam_update(
            params[member][...],
            params[6 + member][...],
            params[12 + member][...],
            clipped,
            rate_matrix if matrix else rate_vector,
            weight_decay if matrix else 0.0,
        )
        grads_kept[member][...] = clipped
        params[6 + member][...] = first
        params[12 + member][...] = second
        params[member][...] = fresh
        if matrix:
            copies[member][...] = fresh.astype(bf)
            save(24 + member, copies[member]).start()
        for place, ref in enumerate(
            (grads_kept[member], params[6 + member], params[12 + member], params[member])
        ):
            save(4 * member + place, ref).start()
        for c in range(member * crops // 6, (member + 1) * crops // 6):
            for a in range(2):
                fetch(a, c).wait()
                store(a, c).start()
    for member in range(6):
        for place, ref in enumerate(
            (grads_kept[member], params[6 + member], params[12 + member], params[member])
        ):
            save(4 * member + place, ref).wait()
        if member < 4:
            save(24 + member, copies[member]).wait()
    for a in range(2):
        for c in range(crops):
            store(a, c).wait()


def update_call(result, token_grad, total, params):
    whole = pl.BlockSpec(memory_space=pltpu.VMEM)
    far = pl.BlockSpec(memory_space=pl.ANY)
    shapes = []
    for member in range(6):
        shapes = shapes + [jax.ShapeDtypeStruct(params[member].shape, fl)] * 4
    for member in range(4):
        shapes.append(jax.ShapeDtypeStruct(params[member].shape, bf))
    shapes.append(jax.ShapeDtypeStruct((1, 1), fl))
    big = jax.ShapeDtypeStruct(result.shape, bf)
    sem = pltpu.SemaphoreType.DMA
    return pl.pallas_call(
        update_kernel,
        in_specs=[far] * 21,
        out_specs=[far] * 30 + [whole],
        out_shape=[big, big] + shapes,
        scratch_shapes=[pltpu.VMEM((2,) + result.shape, bf), pltpu.VMEM(total.shape, bf)]
        + [pltpu.VMEM(p.shape, fl) for p in params]
        + [pltpu.VMEM(p.shape, fl) for p in params[:6]]
        + [pltpu.VMEM(p.shape, bf) for p in params[:4]]
        + [sem((2, result.shape[0]))] * 2
        + [sem((18,)), sem(()), sem((28,))],
        compiler_params=pltpu.CompilerParams(vmem_limit_bytes=56 * 2**20),
        name="update",
    )(result, token_grad, total, *params)


def local(
    voxels,
    cotangent,
    project_in,
    project_out,
    expand,
    contract,
    bias_table,
    vectors,
    project_in_first,
    project_out_first,
    expand_first,
    contract_first,
    bias_table_first,
    vectors_first,
    project_in_second,
    project_out_second,
    expand_second,
    contract_second,
    bias_table_second,
    vectors_second,
):
    batches, planes, height, breadth, width = voxels.shape
    flat = (batches, planes, height * breadth, width)
    result, token_grad, total = block_call(
        voxels.reshape(flat),
        cotangent.reshape(flat),
        (project_in, project_out, expand, contract.T),
        bias_table,
        vectors.reshape(-1, 128),
    )
    params = [
        project_in,
        project_out,
        expand,
        contract.T,
        bias_table,
        vectors.reshape(-1, 128),
        project_in_first,
        project_out_first,
        expand_first,
        contract_first.T,
        bias_table_first,
        vectors_first.reshape(-1, 128),
        project_in_second,
        project_out_second,
        expand_second,
        contract_second.T,
        bias_table_second,
        vectors_second.reshape(-1, 128),
    ]
    done = update_call(result, token_grad, total, params)
    outs = list(done[2:30])
    for place in range(20, 24):
        outs[place] = outs[place].reshape(-1)
    for place in (12, 13, 14, 15, 27):
        outs[place] = outs[place].T
    return (
        (done[0].reshape(voxels.shape), done[1].reshape(voxels.shape))
        + tuple(outs)
        + (done[30].reshape(()),)
    )


def solution(mesh):
    split = P("dp", "depth", None, "wide", None)
    return jax.shard_map(
        local,
        mesh=mesh,
        in_specs=(split,) * 2 + (P(),) * 18,
        out_specs=(split,) * 2 + (P(),) * 29,
        check_vma=False,
    )
```
